32 devices in a mesh: prow: 4 (over y, x), pcol: 8 (over z, core).
Axes of the slice: x: 2, y: 2, z: 4, core: 2. Of those that a mesh axis runs over, the one named last changes fastest.
Arguments:
- matrix: float32 [16, 4, 256, 8, 8, 256], P(None, 'prow', None, None, 'pcol'), may hold values from -6 to 6
- pivots: int32 [2, 256], replicated, may hold values from 256 to 16383, as said below
- inverse_blocks: float32 [2, 256, 256], replicated, may hold values from -1 to 1
Outputs:
- factored: float32 [16, 4, 256, 8, 8, 256], P(None, 'prow', None, None, 'pcol')
The draws below stay inside these ranges and needn't reach their ends.
Inputs may be any that keep to these rules, and one draw needn't show every extreme that they name: Entries of pivots[0] lie in 256 to 16383, entries of pivots[1] in 512 to 16383; the entries of one panel are distinct.
All inputs are finite; a program needn't handle non-finite values.
Results may differ from the reference program's by a relative error of at most 0.00013.
Values sent between devices are 32-bit elements; how exact they have to be, the bound alone decides.
No kernel may reach another device: no remote copies, remote signals or barrier semaphores. Data moves between devices by JAX's collectives and lax.ppermute only.
A program may use at most 192 MiB of HBM per device.

```python
import jax
import jax.numpy as jnp
from jax import lax

N = 16384
NB = 256
RBD = 16
CBD = 8
N_PROW = 4
N_PCOL = 8


def draw_pivots(key, part):
    key = jax.random.fold_in(key, 5)
    panels = []
    for section in range(2):
        lowest = (section + 1) * NB
        sub_key = jax.random.fold_in(key, section)
        shuffled = jax.random.permutation(sub_key, N - lowest - 2).astype(jnp.int32) + lowest + 1
        listed = jnp.concatenate([jnp.array([lowest], jnp.int32), shuffled[:NB - 2], jnp.array([N - 1], jnp.int32)])
        order_key = jax.random.fold_in(sub_key, 7)
        panels.append(jax.random.permutation(order_key, listed))
    return jnp.stack(panels).astype(jnp.int32)


def draw_inverse_blocks(key, part):
    key = jax.random.fold_in(key, 9)
    noise_key, diag_key = jax.random.split(key)
    noise = jax.random.normal(noise_key, (2, NB, NB), jnp.float32)
    offdiag = jnp.clip(noise / jnp.sqrt(jnp.float32(NB)), -1.0, 1.0)
    diag_vals = jax.random.uniform(diag_key, (2, NB), jnp.float32, 0.7, 1.3)
    scale = 1.0 / jnp.sqrt(jnp.float32(NB))
    rows = jnp.arange(NB)[:, None]
    cols = jnp.arange(NB)[None, :]
    upper_part = jnp.where(cols > rows, offdiag * scale, 0.0)
    diag_part = jnp.where(cols == rows, diag_vals[:, :, None] * scale, 0.0)
    lower_part = jnp.where(cols < rows, offdiag, 0.0)
    return (upper_part + diag_part + lower_part).astype(jnp.float32)


def block_scale(stream_key, extent, shards, low, high):
    gain = 1.0
    for dim, parts in shards:
        heights = jax.random.uniform(jax.random.fold_in(jax.random.fold_in(stream_key, 6), dim), (parts,), jnp.float32, low / len(shards), high / len(shards))
        gain = gain * jnp.repeat(jnp.exp(heights), extent[dim] // parts).reshape((-1,) + (1,) * (len(extent) - 1 - dim))
    return gain


def centred(key, dims, scale, reach, cuts=(), held_as=jnp.bfloat16):
    entries = jax.random.normal(key, dims, jnp.float32) * scale
    if len(cuts) > 0:
        entries = block_scale(key, dims, cuts, -0.22, 0.18) * entries
    return jnp.clip(entries, min=-reach, max=reach).astype(held_as)


def setup_inputs(seed: int = 0) -> dict:
    arg_keys = jax.random.split(jax.random.key(seed), 4)
    return {
        "matrix": centred(arg_keys[0], (RBD, N_PROW, NB, CBD, N_PCOL, NB), 1.0, 6.0, ((1, 4), (4, 8)), jnp.float32),
        "pivots": draw_pivots(jax.random.fold_in(arg_keys[3], 71), 0),
        "inverse_blocks": draw_inverse_blocks(jax.random.fold_in(arg_keys[3], 71), 0),
    }


def reference(matrix, pivots, inverse_blocks):
    matrix_now = matrix.reshape(N, N)
    identity = jnp.eye(NB, dtype=jnp.float32)
    for section in range(2):
        row_top = section * NB
        row_mid = row_top + NB
        pivot_list = pivots[section]
        block_rows = matrix_now[row_top:row_mid]
        chosen = matrix_now[pivot_list]
        matrix_now = matrix_now.at[row_top:row_mid].set(chosen).at[pivot_list].set(block_rows)
        packed = inverse_blocks[section]
        upper_inv = jnp.triu(packed)
        lower_inv = jnp.tril(packed, -1) + identity
        lower_panel = jnp.dot(matrix_now[row_mid:, row_top:row_mid], upper_inv, precision=lax.Precision.HIGHEST, preferred_element_type=jnp.float32)
        upper_rows = jnp.dot(lower_inv, matrix_now[row_top:row_mid, row_mid:], precision=lax.Precision.HIGHEST, preferred_element_type=jnp.float32)
        matrix_now = matrix_now.at[row_mid:, row_top:row_mid].set(lower_panel)
        matrix_now = matrix_now.at[row_top:row_mid, row_mid:].set(upper_rows)
        update = jnp.dot(lower_panel, upper_rows, precision=lax.Precision.HIGHEST, preferred_element_type=jnp.float32)
        matrix_now = matrix_now.at[row_mid:, row_mid:].add(-update)
    return matrix_now.reshape(matrix.shape)
```

```python
import functools

import jax
import jax.numpy as jnp
from jax import lax
from jax.experimental import pallas as pl
from jax.experimental.pallas import tpu as pltpu
from jax.sharding import PartitionSpec as P

LANES = 128
CHUNKS = 8
TILE = 256
F32 = jnp.float32
BF16 = jnp.bfloat16
ANY = pl.BlockSpec(memory_space=pl.ANY)
VMEM = pl.BlockSpec(memory_space=pltpu.VMEM)
SMEM = pl.BlockSpec(memory_space=pltpu.SMEM)
PARAMS = pltpu.CompilerParams(vmem_limit_bytes=56 << 20)


def cost(flops, nbytes):
    return pl.CostEstimate(flops=int(flops), bytes_accessed=int(nbytes), transcendentals=0)


def split(x):
    high = x.astype(BF16)
    return high, (x - high.astype(F32)).astype(BF16)


def dot3(left, right):
    out = jnp.dot(left[0], right[0], preferred_element_type=F32)
    out += jnp.dot(left[0], right[1], preferred_element_type=F32)
    return out + jnp.dot(left[1], right[0], preferred_element_type=F32)


def upper(packed):
    row = lax.broadcasted_iota(jnp.int32, packed.shape, 0)
    col = lax.broadcasted_iota(jnp.int32, packed.shape, 1)
    return jnp.where(col >= row, packed, 0.0)


def unit_lower(packed):
    row = lax.broadcasted_iota(jnp.int32, packed.shape, 0)
    col = lax.broadcasted_iota(jnp.int32, packed.shape, 1)
    return jnp.where(col < row, packed, jnp.where(col == row, 1.0, 0.0))


def get_block(ref, start, count, groups, block, per):
    parts = [
        ref[pl.ds(start * groups + block * per + h, count, stride=groups), :] for h in range(per)
    ]
    return jnp.concatenate(parts, axis=1)


def put_block(ref, start, count, groups, block, per, value):
    for h in range(per):
        ref[pl.ds(start * groups + block * per + h, count, stride=groups), :] = value[
            :, h * LANES : (h + 1) * LANES
        ]


def update_rows(count, groups, per, mc, c0, c1, inv_ref, u01_ref, uhl_ref, m_ref, o_ref):
    width = per * LANES
    l0 = dot3(split(c0), split(upper(inv_ref[0])))
    l0s = split(l0)
    rest = c1 - dot3(l0s, split(u01_ref[...]))
    l1 = dot3(split(rest), split(upper(inv_ref[1])))
    l1s = split(l1)
    high = jnp.concatenate([l0s[0], l1s[0]], axis=1)
    low = jnp.concatenate([l0s[1], l1s[1]], axis=1)
    for block in range(groups // per):
        cols = slice(block * width, (block + 1) * width)
        acc = dot3((high, low), (uhl_ref[0, :, cols], uhl_ref[1, :, cols]))
        new = get_block(m_ref, 0, count, groups, block, per) - acc
        if block == 0:
            new = jnp.where(mc == 0, l0, jnp.where(mc == 1, l1, new))
        put_block(o_ref, 0, count, groups, block, per, new)


def rows_kernel(list_ref, m_ref, o_ref, sem):
    count = o_ref.shape[0]

    def step(k, carry):
        pltpu.make_async_copy(m_ref.at[list_ref[k]], o_ref.at[k], sem).start()
        return carry

    lax.fori_loop(0, count, step, 0)
    pltpu.make_async_copy(o_ref, o_ref, sem).wait()


def take_rows(indices, m4):
    count = indices.shape[0]
    shape = (count,) + m4.shape[1:]
    return pl.pallas_call(
        rows_kernel,
        in_specs=[SMEM, ANY],
        out_specs=ANY,
        out_shape=jax.ShapeDtypeStruct(shape, F32),
        scratch_shapes=[pltpu.SemaphoreType.DMA],
        cost_estimate=cost(0, 4 * shape[0] * shape[1] * shape[2] * shape[3]),
        name="take_rows",
    )(indices, m4)


def send_rows_kernel(info_ref, list_ref, m_ref, *rest):
    outs, sem = rest[:-1], rest[-1]
    count = outs[0].shape[0]

    @pl.when(info_ref[0] < 2)
    def _():
        for x, out in enumerate(outs):

            def step(k, carry):
                pltpu.make_async_copy(m_ref.at[list_ref[x, k]], out.at[k], sem).start()
                return carry

            lax.fori_loop(0, count, step, 0)
        for out in outs:
            pltpu.make_async_copy(out, out, sem).wait()


def send_rows(info, lists, m4):
    kinds, count = lists.shape
    shape = (count,) + m4.shape[1:]
    return pl.pallas_call(
        send_rows_kernel,
        in_specs=[SMEM, SMEM, ANY],
        out_specs=[ANY] * kinds,
        out_shape=[jax.ShapeDtypeStruct(shape, F32)] * kinds,
        scratch_shapes=[pltpu.SemaphoreType.DMA],
        cost_estimate=cost(0, 8 * kinds * shape[0] * shape[1] * shape[2] * shape[3]),
        name="send_rows",
    )(info, lists, m4)


def pick_kernel(first, rows, info_ref, m_ref, recv_ref, o_ref, sem):
    @pl.when(info_ref[2] == 0)
    def _():
        copy = pltpu.make_async_copy(m_ref.at[pl.ds(first, rows), 0], o_ref, sem)
        copy.start()
        copy.wait()

    @pl.when(info_ref[2] != 0)
    def _():
        copy = pltpu.make_async_copy(recv_ref, o_ref, sem)
        copy.start()
        copy.wait()


def pick(info, m4, recv, first):
    return pl.pallas_call(
        functools.partial(pick_kernel, first, recv.shape[0]),
        in_specs=[SMEM, ANY, ANY],
        out_specs=ANY,
        out_shape=jax.ShapeDtypeStruct(recv.shape, F32),
        scratch_shapes=[pltpu.SemaphoreType.DMA],
        cost_estimate=cost(0, 8 * recv.size),
        name="pick",
    )(info, m4, recv)


def panel_kernel(first, rows, m_ref, o_ref, sem):
    copy = pltpu.make_async_copy(m_ref.at[pl.ds(first, rows), 0], o_ref, sem)
    copy.start()
    copy.wait()


def panel(m4, first, rows):
    shape = (rows,) + m4.shape[2:]
    return pl.pallas_call(
        functools.partial(panel_kernel, first, rows),
        in_specs=[ANY],
        out_specs=ANY,
        out_shape=jax.ShapeDtypeStruct(shape, F32),
        scratch_shapes=[pltpu.SemaphoreType.DMA],
        cost_estimate=cost(0, 8 * rows * shape[1] * shape[2]),
        name="panel",
    )(m4)


def assemble_kernel(width, info_ref, index_ref, g_ref, o_ref, tab_ref):
    per = tab_ref.shape[1]
    base = jnp.where(info_ref[3] == 0, width, 0)

    def step(k, carry):
        o_ref[k] = g_ref[index_ref[k]]
        return carry

    def tab_step(k, carry):
        tab_ref[k] = g_ref[index_ref[base + k], 0:per, :]
        return carry

    lax.fori_loop(0, 2 * width, step, 0, unroll=4)
    lax.fori_loop(0, width, tab_step, 0, unroll=4)


def assemble(info, index, gathered, width, per):
    groups = gathered.shape[1]
    return pl.pallas_call(
        functools.partial(assemble_kernel, width),
        in_specs=[SMEM, SMEM, VMEM],
        out_specs=[VMEM, VMEM],
        out_shape=[
            jax.ShapeDtypeStruct((2 * width, groups, LANES), F32),
            jax.ShapeDtypeStruct((width, per, LANES), F32),
        ],
        compiler_params=PARAMS,
        cost_estimate=cost(0, 8 * gathered.size),
        name="assemble",
    )(info, index, gathered)


def fetch_kernel(info_ref, *rest):
    *ins, f_ref, tab_ref, sem = rest
    me = info_ref[0]
    rows = ins[0].shape[0]
    for source in range(2):
        spot = pl.ds(source * rows, rows)
        for x, buf in enumerate(ins):

            @pl.when((me ^ source) == x)
            def _():
                whole = pltpu.make_async_copy(buf, f_ref.at[spot], sem.at[0])
                head = pltpu.make_async_copy(buf.at[:, 0], tab_ref.at[spot], sem.at[1])
                whole.start()
                head.start()
                whole.wait()
                head.wait()


def fetch(info, bufs):
    rows, blocks, per, _ = bufs[0].shape
    return pl.pallas_call(
        fetch_kernel,
        in_specs=[SMEM] + [ANY] * len(bufs),
        out_specs=[ANY, ANY],
        out_shape=[
            jax.ShapeDtypeStruct((2 * rows, blocks, per, LANES), F32),
            jax.ShapeDtypeStruct((2 * rows, per, LANES), F32),
        ],
        scratch_shapes=[pltpu.SemaphoreType.DMA((2,))],
        cost_estimate=cost(0, 16 * bufs[0].size),
        name="fetch",
    )(info, *bufs)


def solve_kernel(groups, per, info_ref, a_ref, own_ref, sib_ref, inv_ref, uhl_ref, brow_ref, u01_ref):
    width = per * LANES
    mc = info_ref[1]
    even = info_ref[3] == 0
    own = get_block(own_ref, 0, width, per, 0, per)
    sib = get_block(sib_ref, 0, width, per, 0, per)
    z1c0 = jnp.where(even, own, sib)
    g0c1 = jnp.where(even, sib, own)
    low0 = split(unit_lower(inv_ref[0]))
    low1 = split(unit_lower(inv_ref[1]))
    l01 = dot3(split(z1c0), split(upper(inv_ref[0])))
    l01s = split(l01)
    u01_ref[...] = dot3(low0, split(g0c1))
    for block in range(groups // per):
        cols = slice(block * width, (block + 1) * width)
        g0 = get_block(a_ref, 0, width, groups, block, per)
        z1 = get_block(a_ref, width, width, groups, block, per)
        u0 = dot3(low0, split(g0))
        u0s = split(u0)
        a1 = z1 - dot3(l01s, u0s)
        u1 = dot3(low1, split(a1))
        u1s = split(u1)
        for part in range(2):
            uhl_ref[part, :width, cols] = u0s[part]
            uhl_ref[part, width:, cols] = u1s[part]
        if block == 0:
            top = jnp.where(mc == 0, g0, u0)
            mid = jnp.where(mc == 0, l01, jnp.where(mc == 1, a1, u1))
        else:
            top, mid = u0, u1
        put_block(brow_ref, 0, width, groups, block, per, top)
        put_block(brow_ref, width, width, groups, block, per, mid)


def solve(info, asm, own, sib, inv, groups, per):
    width = per * LANES
    cols = groups * LANES
    return pl.pallas_call(
        functools.partial(solve_kernel, groups, per),
        in_specs=[SMEM, VMEM, VMEM, VMEM, VMEM],
        out_specs=[VMEM, VMEM, VMEM],
        out_shape=[
            jax.ShapeDtypeStruct((2, 2 * width, cols), BF16),
            jax.ShapeDtypeStruct((2 * width * groups, LANES), F32),
            jax.ShapeDtypeStruct((width, width), F32),
        ],
        compiler_params=PARAMS,
        cost_estimate=cost(18 * width * width * cols, 24 * width * cols),
        name="solve",
    )(info, asm, own, sib, inv)


def bulk_kernel(chips, groups, per, tile, fresh, info_ref, *rest):
    owns, sibs = rest[:chips], rest[chips : 2 * chips]
    m_ref, inv_ref, u01_ref, uhl_ref = rest[2 * chips : 2 * chips + 4]
    o_ref, c0_ref, c1_ref, sem = rest[-4:]
    step = pl.program_id(0)

    @pl.when(step == 0)
    def _():
        for h in range(chips):
            for core in range(2):

                @pl.when((info_ref[2] == h) & (info_ref[3] == core))
                def _():
                    first, second = (owns[h], sibs[h]) if core == 0 else (sibs[h], owns[h])
                    one = pltpu.make_async_copy(first, c0_ref, sem.at[0])
                    two = pltpu.make_async_copy(second, c1_ref, sem.at[1])
                    one.start()
                    two.start()
                    one.wait()
                    two.wait()

    c0 = get_block(c0_ref, step * tile, tile, per, 0, per)
    c1 = get_block(c1_ref, step * tile, tile, per, 0, per)
    update_rows(
        tile, groups, per, info_ref[1], c0, c1, inv_ref, u01_ref, uhl_ref, m_ref, o_ref
    )


def bulk(info, owns, sibs, m2, inv, u01, uhl, out, first, rows, groups, per):
    chips = len(owns)
    tile = min(TILE, rows)
    base = first // tile
    width = per * LANES
    cols = groups * LANES
    block = pl.BlockSpec((tile * groups, LANES), lambda i: (base + i, 0))
    fresh = out is None
    in_specs = [SMEM] + [ANY] * (2 * chips) + [block, VMEM, VMEM, VMEM]
    args = [info, *owns, *sibs, m2, inv, u01, uhl]
    aliases = {}
    if not fresh:
        in_specs.append(ANY)
        aliases = {len(args): 0}
        args.append(out)
    return pl.pallas_call(
        functools.partial(bulk_kernel, chips, groups, per, tile, fresh),
        grid=(rows // tile,),
        in_specs=in_specs,
        out_specs=block,
        out_shape=jax.ShapeDtypeStruct(m2.shape, F32),
        scratch_shapes=[
            pltpu.VMEM((rows * per, LANES), F32),
            pltpu.VMEM((rows * per, LANES), F32),
            pltpu.SemaphoreType.DMA((2,)),
        ],
        input_output_aliases=aliases,
        compiler_params=PARAMS,
        cost_estimate=cost(12 * rows * width * cols, 8 * rows * cols),
        name="bulk",
    )(*args)


def moved_kernel(groups, per, info_ref, f_ref, own_ref, sib_ref, inv_ref, u01_ref, uhl_ref, o_ref):
    rows = f_ref.shape[0] // groups
    even = info_ref[3] == 0
    own = get_block(own_ref, 0, rows, per, 0, per)
    sib = get_block(sib_ref, 0, rows, per, 0, per)
    c0 = jnp.where(even, own, sib)
    c1 = jnp.where(even, sib, own)
    update_rows(rows, groups, per, info_ref[1], c0, c1, inv_ref, u01_ref, uhl_ref, f_ref, o_ref)


def moved(info, f2, own, sib, inv, u01, uhl, groups, per):
    rows = f2.shape[0] // groups
    return pl.pallas_call(
        functools.partial(moved_kernel, groups, per),
        in_specs=[SMEM] + [VMEM] * 6,
        out_specs=VMEM,
        out_shape=jax.ShapeDtypeStruct(f2.shape, F32),
        compiler_params=PARAMS,
        cost_estimate=cost(12 * rows * per * groups * LANES * LANES, 8 * f2.size),
        name="moved",
    )(info, f2, own, sib, inv, u01, uhl)


def place_kernel(info_ref, spot_ref, f_ref, brow_ref, _, o_ref, sem):
    width = brow_ref.shape[0] // 2
    count = f_ref.shape[0]

    def put(k):
        return pltpu.make_async_copy(f_ref.at[k], o_ref.at[spot_ref[k]], sem.at[0])

    def start(k, carry):
        @pl.when(spot_ref[k] >= 0)
        def _():
            put(k).start()

        return carry

    def finish(k, carry):
        @pl.when(spot_ref[k] >= 0)
        def _():
            put(k).wait()

        return carry

    for source in range(2):

        @pl.when(info_ref[0] == source)
        def _():
            pltpu.make_async_copy(
                brow_ref.at[pl.ds(source * width, width)], o_ref.at[pl.ds(0, width)], sem.at[1]
            ).start()

    lax.fori_loop(0, count, start, 0)
    lax.fori_loop(0, count, finish, 0)
    for source in range(2):

        @pl.when(info_ref[0] == source)
        def _():
            pltpu.make_async_copy(
                brow_ref.at[pl.ds(source * width, width)], o_ref.at[pl.ds(0, width)], sem.at[1]
            ).wait()


def place(info, spots, f3, brow, out):
    return pl.pallas_call(
        place_kernel,
        in_specs=[SMEM, SMEM, ANY, ANY, ANY],
        out_specs=ANY,
        out_shape=jax.ShapeDtypeStruct(out.shape, F32),
        scratch_shapes=[pltpu.SemaphoreType.DMA((2,))],
        input_output_aliases={4: 0},
        cost_estimate=cost(0, 8 * (f3.size + brow.size)),
        name="place",
    )(info, spots, f3, brow, out)


def plan(pivots, width, procs, me):
    p0, p1 = pivots[0], pivots[1]
    count = jnp.arange(width, dtype=jnp.int32)
    hit = p0[:, None] == p1[None, :]
    back = p0[:, None] == width + count[None, :]
    src1 = jnp.where(hit.any(0), jnp.sum(jnp.where(hit, count[:, None], 0), 0), p1)
    dest0 = jnp.where(
        back.any(1),
        jnp.sum(jnp.where(back, p1[None, :], 0), 1),
        jnp.where(hit.any(1), -1, p0),
    )
    dest1 = jnp.where(back.any(0), -1, p1)
    src = jnp.concatenate([p0, src1])
    dest = jnp.concatenate([dest0, dest1])
    src_owner = src // width % procs
    src_local = src // width // procs * width + src % width
    dest_owner = jnp.where(dest >= 0, dest // width % procs, -1)
    dest_local = dest // width // procs * width + dest % width
    order = jnp.arange(2 * width, dtype=jnp.int32)
    earlier = order[None, :] < order[:, None]
    same_half = (order[None, :] // width) == (order[:, None] // width)
    src_rank = jnp.sum(
        (earlier & (src_owner[None, :] == src_owner[:, None])).astype(jnp.int32), 1
    )
    dest_rank = jnp.sum(
        (earlier & same_half & (dest_owner[None, :] == dest_owner[:, None])).astype(jnp.int32), 1
    )
    src_most = jnp.max(src_rank) + 1
    dest_most = jnp.max(jnp.where(dest >= 0, dest_rank, -1)) + 1
    return src_owner, src_local, src_rank, dest_owner, dest_local, dest_rank, src_most, dest_most


def factor(cap, fcap, matrix, inv, info, src, dest):
    row_blocks, _, width, blocks, _, _ = matrix.shape
    procs = lax.axis_size("prow")
    chips = lax.axis_size("pcol") // 2
    per = width // LANES
    groups = blocks * per
    rows = row_blocks * width
    me, z = info[0], info[2]
    m2 = matrix.reshape(rows * groups, LANES)
    m4 = matrix.reshape(rows, blocks, per, LANES)
    src_owner, src_local, src_rank = src
    dest_owner, dest_local, dest_rank = dest
    hop = [(q, q + 2) for q in range(2 * chips - 2)]
    swap = [(q, q ^ 1) for q in range(2 * chips)]

    slots = jnp.arange(cap, dtype=jnp.int32)
    mine = (src_owner == me)[None, :] & (src_rank[None, :] == slots[:, None])
    row_list = jnp.sum(jnp.where(mine, src_local[None, :], 0), 1)
    index = src_owner * cap + src_rank

    fslots = jnp.arange(fcap, dtype=jnp.int32)
    owner2 = dest_owner.reshape(2, width)
    rank2 = dest_rank.reshape(2, width)
    local2 = dest_local.reshape(2, width)
    half = jnp.minimum(me, 1)
    to = me ^ jnp.arange(procs, dtype=jnp.int32)
    out_owner = jnp.where(half == 0, owner2[0], owner2[1])
    out_rank = jnp.where(half == 0, rank2[0], rank2[1])
    chosen = (out_owner[None, None, :] == to[:, None, None]) & (
        out_rank[None, None, :] == fslots[None, :, None]
    )
    out_list = jnp.sum(jnp.where(chosen, jnp.arange(width, dtype=jnp.int32), 0), 2)
    landing = (owner2[:, None, :] == me) & (rank2[:, None, :] == fslots[None, :, None])
    spots = (jnp.sum(jnp.where(landing, local2[:, None, :] + 1, 0), 2) - 1).reshape(2 * fcap)

    chunk = rows // CHUNKS
    own, sib = [], []
    for t in range(CHUNKS + chips - 1):
        if t == 0:
            cur = panel(m4, 0, chunk)
        else:
            cur = lax.ppermute(own[-1], "pcol", hop).reshape(chunk, per, LANES)
            if t < CHUNKS:
                cur = pick(info, m4, cur, t * chunk)
        cur = cur.reshape(chunk * per, LANES)
        own.append(cur)
        sib.append(lax.ppermute(cur, "pcol", swap))

    sent = take_rows(row_list, m4).reshape(cap * groups, LANES)
    gathered = lax.all_gather(sent, "prow", axis=0, tiled=True)
    asm, tab = assemble(info, index, gathered.reshape(procs * cap, groups, LANES), width, per)

    outgoing = send_rows(info, out_list, m4)
    bufs = [outgoing[0]]
    for x in range(1, procs):
        pairs = [(s, s ^ x) for s in range(2)]
        moved_buf = lax.ppermute(outgoing[x].reshape(fcap * groups, LANES), "prow", pairs)
        bufs.append(moved_buf.reshape(outgoing[x].shape))
    f4, ftab = fetch(info, bufs)

    def spread(table):
        for h in range(1, chips):
            pairs = [(2 * h - 2, 2 * h), (2 * h - 1, 2 * h + 1)]
            table = jnp.where(z == h, lax.ppermute(table, "pcol", pairs), table)
        return table, lax.ppermute(table, "pcol", swap)

    tab_own, tab_sib = spread(tab.reshape(width * per, LANES))
    uhl, brow, u01 = solve(
        info, asm.reshape(2 * width * groups, LANES), tab_own, tab_sib, inv, groups, per
    )
    ftab_own, ftab_sib = spread(ftab.reshape(2 * fcap * per, LANES))
    fixed = moved(
        info, f4.reshape(2 * fcap * groups, LANES), ftab_own, ftab_sib, inv, u01, uhl, groups, per
    )

    out = None
    for s in range(CHUNKS):
        out = bulk(
            info, own[s : s + chips], sib[s : s + chips], m2, inv, u01, uhl, out, s * chunk, chunk,
            groups, per,
        )
    out = place(
        info,
        spots,
        fixed.reshape(2 * fcap, groups, LANES),
        brow.reshape(2 * width, groups, LANES),
        out.reshape(rows, groups, LANES),
    )
    return out.reshape(matrix.shape)


def shards(matrix, pivots, inverse_blocks):
    width = matrix.shape[2]
    procs = lax.axis_size("prow")
    me = lax.axis_index("prow").astype(jnp.int32)
    mc = lax.axis_index("pcol").astype(jnp.int32)
    info = jnp.stack([me, mc, mc // 2, mc % 2])
    so, sl, sr, do, dl, dr, src_most, dest_most = plan(pivots, width, procs, me)
    mean = 2 * width // procs
    cap = min(2 * width, (mean + 3 * mean // 8 + 7) // 8 * 8)
    fmean = width // procs
    fcap = min(width, (fmean + fmean // 2 + 7) // 8 * 8)
    fits = (src_most <= cap) & (dest_most <= fcap)
    return lax.cond(
        fits,
        functools.partial(factor, cap, fcap),
        functools.partial(factor, 2 * width, width),
        matrix, inverse_blocks, info, (so, sl, sr), (do, dl, dr),
    )


def solution(mesh):
    return jax.shard_map(
        shards,
        mesh=mesh,
        in_specs=(P(None, "prow", None, None, "pcol", None), P(), P()),
        out_specs=P(None, "prow", None, None, "pcol", None),
        check_vma=False,
    )
```

```python
import functools

import jax
import jax.numpy as jnp
from jax import lax
from jax.experimental import pallas as pl
from jax.experimental.pallas import tpu as pltpu
from jax.sharding import PartitionSpec as P

LANES = 128
CHUNKS = 16
CHAINS = 2
TILE = 256
F32 = jnp.float32
BF16 = jnp.bfloat16
ANY = pl.BlockSpec(memory_space=pl.ANY)
VMEM = pl.BlockSpec(memory_space=pltpu.VMEM)
SMEM = pl.BlockSpec(memory_space=pltpu.SMEM)
PARAMS = pltpu.CompilerParams(vmem_limit_bytes=56 << 20)


def cost(flops, nbytes):
    return pl.CostEstimate(flops=int(flops), bytes_accessed=int(nbytes), transcendentals=0)


def split(x):
    high = x.astype(BF16)
    return high, (x - high.astype(F32)).astype(BF16)


def dot3(left, right):
    out = jnp.dot(left[0], right[0], preferred_element_type=F32)
    out += jnp.dot(left[0], right[1], preferred_element_type=F32)
    return out + jnp.dot(left[1], right[0], preferred_element_type=F32)


def upper(packed):
    row = lax.broadcasted_iota(jnp.int32, packed.shape, 0)
    col = lax.broadcasted_iota(jnp.int32, packed.shape, 1)
    return jnp.where(col >= row, packed, 0.0)


def unit_lower(packed):
    row = lax.broadcasted_iota(jnp.int32, packed.shape, 0)
    col = lax.broadcasted_iota(jnp.int32, packed.shape, 1)
    return jnp.where(col < row, packed, jnp.where(col == row, 1.0, 0.0))


def get_block(ref, start, count, pitch, block, per):
    parts = [ref[pl.ds(start * pitch + block * per + h, count, stride=pitch), :] for h in range(per)]
    return jnp.concatenate(parts, axis=1)


def put_block(ref, start, count, pitch, block, per, value):
    for h in range(per):
        ref[pl.ds(start * pitch + block * per + h, count, stride=pitch), :] = value[
            :, h * LANES : (h + 1) * LANES
        ]


def update_rows(count, groups, per, mc, c0, c1, inv_ref, u01_ref, uhl_ref, s_ref, get, put):
    width = per * LANES
    pitch = groups + 1
    l0 = dot3(split(c0), split(upper(inv_ref[0])))
    l0s = split(l0)
    rest = c1 - dot3(l0s, split(u01_ref[...]))
    l1 = dot3(split(rest), split(upper(inv_ref[1])))
    l1s = split(l1)
    high = jnp.concatenate([l0s[0], l1s[0]], axis=1)
    low = jnp.concatenate([l0s[1], l1s[1]], axis=1)
    for block in range(groups // per):
        cols = slice(block * width, (block + 1) * width)
        acc = dot3((high, low), (uhl_ref[0, :, cols], uhl_ref[1, :, cols]))
        if block == 0:
            acc = jnp.where(mc == 0, -l0, jnp.where(mc == 1, -l1, acc))
        put_block(s_ref, 0, count, pitch, block, per, acc)
    drop = (lax.broadcasted_iota(jnp.int32, (groups, LANES), 0) < per) & (mc < 2)

    def step(i, carry):
        put(i, jnp.where(drop, 0.0, get(i)) - s_ref[pl.ds(i * pitch, groups), :])
        return carry

    lax.fori_loop(0, count, step, 0, unroll=8)


def panel(m4, first, count, rows):
    shape = (rows,) + m4.shape[2:]

    def kernel(m_ref, *rest):
        outs, sem = rest[:count], rest[count]
        copies = [
            pltpu.make_async_copy(m_ref.at[pl.ds((first + k) * rows, rows), 0], outs[k], sem.at[k])
            for k in range(count)
        ]
        for copy in copies:
            copy.start()
        for copy in copies:
            copy.wait()

    return pl.pallas_call(
        kernel,
        in_specs=[ANY],
        out_specs=[VMEM] * count,
        out_shape=[jax.ShapeDtypeStruct(shape, F32)] * count,
        scratch_shapes=[pltpu.SemaphoreType.DMA((count,))],
        compiler_params=PARAMS,
        cost_estimate=cost(0, 8 * count * rows * shape[1] * shape[2]),
        name="panel",
    )(m4)


def collect_kernel(procs, per, info_ref, list_ref, out_list_ref, m_ref, *rest):
    a_ref, b_ref = rest[:2]
    out_refs, head_refs = rest[2 : 2 + procs], rest[2 + procs : 2 + 2 * procs]
    row_ref, top_ref, sem = rest[2 + 2 * procs :]
    cap, groups, _ = row_ref.shape
    width = top_ref.shape[0]
    fcap = out_refs[0].shape[0]
    top = pltpu.make_async_copy(m_ref.at[pl.ds(0, width)], top_ref, sem.at[0])
    top.start()

    def fetch(k, carry):
        pltpu.make_async_copy(m_ref.at[list_ref[k]], row_ref.at[k], sem.at[1]).start()
        return carry

    lax.fori_loop(0, cap, fetch, 0)
    top.wait()

    @pl.when(info_ref[0] < 2)
    def _():
        for x in range(procs):

            def give(k, carry):
                row = top_ref[out_list_ref[x, k]]
                out_refs[x][k] = row
                head_refs[x][cap + k] = row[0:per]
                return carry

            lax.fori_loop(0, fcap, give, 0, unroll=4)

    pltpu.make_async_copy(row_ref, row_ref, sem.at[1]).wait()

    def keep(k, carry):
        row = row_ref[k]
        a_ref[k] = row[: groups // 2]
        b_ref[k] = row[groups // 2 :]
        for x in range(procs):
            head_refs[x][k] = row[0:per]
        return carry

    lax.fori_loop(0, cap, keep, 0, unroll=2)


def collect(info, row_list, out_list, m3, per, width):
    cap = row_list.shape[0]
    procs, fcap = out_list.shape
    groups = m3.shape[1]
    half = jax.ShapeDtypeStruct((cap, groups // 2, LANES), F32)
    out = jax.ShapeDtypeStruct((fcap, groups, LANES), F32)
    head = jax.ShapeDtypeStruct((cap + fcap, per, LANES), F32)
    outs = pl.pallas_call(
        functools.partial(collect_kernel, procs, per),
        in_specs=[SMEM, SMEM, SMEM, ANY],
        out_specs=[VMEM] * (2 + 2 * procs),
        out_shape=[half, half] + [out] * procs + [head] * procs,
        scratch_shapes=[
            pltpu.VMEM((cap, groups, LANES), F32),
            pltpu.VMEM((width, groups, LANES), F32),
            pltpu.SemaphoreType.DMA((2,)),
        ],
        compiler_params=PARAMS,
        cost_estimate=cost(0, 16 * (cap + procs * fcap) * groups * LANES),
        name="collect",
    )(info, row_list, out_list, m3)
    return outs[:2], outs[2 : 2 + procs], outs[2 + procs :]


def tables_kernel(procs, cap, info_ref, owner_ref, rank_ref, *rest):
    ins = rest[:procs]
    g_ref, f_ref, buf_ref, sem = rest[procs:]
    width = g_ref.shape[0]
    fcap = f_ref.shape[0] // 2
    copies = [
        pltpu.make_async_copy(ins[x], buf_ref.at[info_ref[0] ^ x], sem.at[x]) for x in range(procs)
    ]
    for copy in copies:
        copy.start()
    for copy in copies:
        copy.wait()
    base = jnp.where(info_ref[3] == 0, width, 0)

    def pivot(k, carry):
        g_ref[k] = buf_ref[owner_ref[base + k], rank_ref[base + k]]
        return carry

    lax.fori_loop(0, width, pivot, 0, unroll=4)
    for source in range(2):

        def other(k, carry):
            f_ref[source * fcap + k] = buf_ref[source, cap + k]
            return carry

        lax.fori_loop(0, fcap, other, 0, unroll=4)


def tables(info, owner, rank, heads, cap, width):
    procs = len(heads)
    both, per, _ = heads[0].shape
    fcap = both - cap
    return pl.pallas_call(
        functools.partial(tables_kernel, procs, cap),
        in_specs=[SMEM, SMEM, SMEM] + [ANY] * procs,
        out_specs=[VMEM, VMEM],
        out_shape=[
            jax.ShapeDtypeStruct((width, per, LANES), F32),
            jax.ShapeDtypeStruct((2 * fcap, per, LANES), F32),
        ],
        scratch_shapes=[
            pltpu.VMEM((procs, both, per, LANES), F32),
            pltpu.SemaphoreType.DMA((procs,)),
        ],
        compiler_params=PARAMS,
        cost_estimate=cost(0, 8 * procs * heads[0].size),
        name="tables",
    )(info, owner, rank, *heads)


def solve_kernel(procs, order_a, order_b, groups, per, info_ref, owner_ref, rank_ref, *rest):
    a_ins, b_ins = rest[:procs], rest[procs : 2 * procs]
    own_ref, sib_ref, inv_ref, uhl_ref, brow_ref, u01_ref, a_ref, b_ref, s_ref, sem = rest[
        2 * procs :
    ]
    width = per * LANES
    pitch = groups + 1
    me, mc = info_ref[0], info_ref[1]
    even = info_ref[3] == 0
    copies = []
    for n in range(procs):
        copies.append(pltpu.make_async_copy(a_ins[n], a_ref.at[me ^ order_a[n]], sem.at[n]))
        copies.append(pltpu.make_async_copy(b_ins[n], b_ref.at[me ^ order_b[n]], sem.at[procs + n]))
    for copy in copies:
        copy.start()
    own = get_block(own_ref, 0, width, per, 0, per)
    sib = get_block(sib_ref, 0, width, per, 0, per)
    z1c0 = jnp.where(even, own, sib)
    g0c1 = jnp.where(even, sib, own)
    low0 = split(unit_lower(inv_ref[0]))
    low1 = split(unit_lower(inv_ref[1]))
    l01 = dot3(split(z1c0), split(upper(inv_ref[0])))
    l01s = split(l01)
    u01_ref[...] = dot3(low0, split(g0c1))
    for copy in copies:
        copy.wait()

    def line_up(k, carry):
        owner, rank = owner_ref[k], rank_ref[k]
        s_ref[pl.ds(k * pitch, groups // 2), :] = a_ref[owner, rank]
        s_ref[pl.ds(k * pitch + groups // 2, groups // 2), :] = b_ref[owner, rank]
        return carry

    lax.fori_loop(0, 2 * width, line_up, 0, unroll=4)
    for block in range(groups // per):
        cols = slice(block * width, (block + 1) * width)
        g0 = get_block(s_ref, 0, width, pitch, block, per)
        z1 = get_block(s_ref, width, width, pitch, block, per)
        u0 = dot3(low0, split(g0))
        u0s = split(u0)
        a1 = z1 - dot3(l01s, u0s)
        u1 = dot3(low1, split(a1))
        u1s = split(u1)
        for part in range(2):
            uhl_ref[part, :width, cols] = u0s[part]
            uhl_ref[part, width:, cols] = u1s[part]
        if block == 0:
            top = jnp.where(mc == 0, g0, u0)
            mid = jnp.where(mc == 0, l01, jnp.where(mc == 1, a1, u1))
        else:
            top, mid = u0, u1
        put_block(s_ref, 0, width, pitch, block, per, top)
        put_block(s_ref, width, width, pitch, block, per, mid)

    def lay_out(k, carry):
        brow_ref[k] = s_ref[pl.ds(k * pitch, groups), :]
        return carry

    lax.fori_loop(0, 2 * width, lay_out, 0, unroll=4)


def solve(info, owner, rank, a_bufs, b_bufs, order_a, order_b, own, sib, inv, groups, per):
    procs = len(a_bufs)
    width = per * LANES
    cols = groups * LANES
    half = pltpu.VMEM((procs,) + a_bufs[0].shape, F32)
    return pl.pallas_call(
        functools.partial(solve_kernel, procs, order_a, order_b, groups, per),
        in_specs=[SMEM, SMEM, SMEM] + [ANY] * (2 * procs) + [VMEM] * 3,
        out_specs=[VMEM, VMEM, VMEM],
        out_shape=[
            jax.ShapeDtypeStruct((2, 2 * width, cols), BF16),
            jax.ShapeDtypeStruct((2 * width, groups, LANES), F32),
            jax.ShapeDtypeStruct((width, width), F32),
        ],
        scratch_shapes=[
            half,
            half,
            pltpu.VMEM((2 * width * (groups + 1), LANES), F32),
            pltpu.SemaphoreType.DMA((2 * procs,)),
        ],
        compiler_params=PARAMS,
        cost_estimate=cost(18 * width * width * cols, 24 * width * cols),
        name="solve",
    )(info, owner, rank, *a_bufs, *b_bufs, own, sib, inv)


def make_bulk_kernel(chips, count, chunk, tile, groups, per):
    def kernel(info_ref, *rest):
        bufs = rest[: 2 * chips * count]
        m_ref, inv_ref, u01_ref, uhl_ref = rest[2 * chips * count : 2 * chips * count + 4]
        o_ref, c0_ref, c1_ref, s_ref, sem = rest[-5:]
        step = pl.program_id(0)

        @pl.when(step == 0)
        def _():
            for h in range(chips):
                for core in range(2):

                    @pl.when((info_ref[2] == h) & (info_ref[3] == core))
                    def _():
                        copies = []
                        for n in range(count):
                            own, sib = bufs[2 * n * chips + h], bufs[(2 * n + 1) * chips + h]
                            first, second = (own, sib) if core == 0 else (sib, own)
                            spot = pl.ds(n * chunk * per, chunk * per)
                            copies.append(
                                pltpu.make_async_copy(first, c0_ref.at[spot], sem.at[2 * n])
                            )
                            copies.append(
                                pltpu.make_async_copy(second, c1_ref.at[spot], sem.at[2 * n + 1])
                            )
                        for copy in copies:
                            copy.start()
                        for copy in copies:
                            copy.wait()

        def get(i):
            return m_ref[pl.ds(pl.multiple_of(i * groups, groups), groups), :]

        def put(i, value):
            o_ref[pl.ds(pl.multiple_of(i * groups, groups), groups), :] = value

        c0 = get_block(c0_ref, step * tile, tile, per, 0, per)
        c1 = get_block(c1_ref, step * tile, tile, per, 0, per)
        update_rows(
            tile, groups, per, info_ref[1], c0, c1, inv_ref, u01_ref, uhl_ref, s_ref, get, put
        )

    return kernel


def bulk(info, bufs, m2, inv, u01, uhl, out, first, count, chunk, groups, per):
    chips = len(bufs) // (2 * count)
    tile = min(TILE, chunk)
    rows = count * chunk
    base = first // tile
    width = per * LANES
    cols = groups * LANES
    block = pl.BlockSpec((tile * groups, LANES), lambda i: (base + i, 0))
    in_specs = [SMEM] + [ANY] * len(bufs) + [block, VMEM, VMEM, VMEM]
    args = [info, *bufs, m2, inv, u01, uhl]
    aliases = {}
    if out is not None:
        in_specs.append(ANY)
        aliases = {len(args): 0}
        args.append(out)
    return pl.pallas_call(
        make_bulk_kernel(chips, count, chunk, tile, groups, per),
        grid=(rows // tile,),
        in_specs=in_specs,
        out_specs=block,
        out_shape=jax.ShapeDtypeStruct(m2.shape, F32),
        scratch_shapes=[
            pltpu.VMEM((rows * per, LANES), F32),
            pltpu.VMEM((rows * per, LANES), F32),
            pltpu.VMEM((tile * (groups + 1), LANES), F32),
            pltpu.SemaphoreType.DMA((2 * count,)),
        ],
        input_output_aliases=aliases,
        compiler_params=PARAMS,
        cost_estimate=cost(12 * rows * width * cols, 8 * rows * cols),
        name="bulk",
    )(*args)


def moved_kernel(procs, groups, per, info_ref, *rest):
    ins = rest[:procs]
    own_ref, sib_ref, inv_ref, u01_ref, uhl_ref, o_ref, f_ref, s_ref, sem = rest[procs:]
    rows = f_ref.shape[0]
    for source in range(2):
        spot = pl.ds(source * (rows // 2), rows // 2)
        for x in range(procs):

            @pl.when((info_ref[0] ^ source) == x)
            def _():
                copy = pltpu.make_async_copy(ins[x], f_ref.at[spot], sem)
                copy.start()
                copy.wait()

    def get(i):
        return f_ref[i]

    def put(i, value):
        o_ref[i] = value

    even = info_ref[3] == 0
    own = get_block(own_ref, 0, rows, per, 0, per)
    sib = get_block(sib_ref, 0, rows, per, 0, per)
    c0 = jnp.where(even, own, sib)
    c1 = jnp.where(even, sib, own)
    update_rows(rows, groups, per, info_ref[1], c0, c1, inv_ref, u01_ref, uhl_ref, s_ref, get, put)


def moved(info, bufs, own, sib, inv, u01, uhl, per):
    fcap, groups, _ = bufs[0].shape
    rows = 2 * fcap
    return pl.pallas_call(
        functools.partial(moved_kernel, len(bufs), groups, per),
        in_specs=[SMEM] + [ANY] * len(bufs) + [VMEM] * 5,
        out_specs=VMEM,
        out_shape=jax.ShapeDtypeStruct((rows, groups, LANES), F32),
        scratch_shapes=[
            pltpu.VMEM((rows, groups, LANES), F32),
            pltpu.VMEM((rows * (groups + 1), LANES), F32),
            pltpu.SemaphoreType.DMA,
        ],
        compiler_params=PARAMS,
        cost_estimate=cost(12 * rows * per * groups * LANES * LANES, 8 * rows * groups * LANES),
        name="moved",
    )(info, *bufs, own, sib, inv, u01, uhl)


def place_kernel(info_ref, spot_ref, f_ref, brow_ref, _, o_ref, sem):
    width = brow_ref.shape[0] // 2
    count = f_ref.shape[0]

    def put(k):
        return pltpu.make_async_copy(f_ref.at[k], o_ref.at[spot_ref[k]], sem.at[0])

    def start(k, carry):
        @pl.when(spot_ref[k] >= 0)
        def _():
            put(k).start()

        return carry

    def finish(k, carry):
        @pl.when(spot_ref[k] >= 0)
        def _():
            put(k).wait()

        return carry

    source = jnp.minimum(info_ref[0], 1)
    top = pltpu.make_async_copy(
        brow_ref.at[pl.ds(source * width, width)], o_ref.at[pl.ds(0, width)], sem.at[1]
    )

    @pl.when(info_ref[0] < 2)
    def _():
        top.start()

    lax.fori_loop(0, count, start, 0)
    lax.fori_loop(0, count, finish, 0)

    @pl.when(info_ref[0] < 2)
    def _():
        top.wait()


def place(info, spots, f3, brow, out):
    return pl.pallas_call(
        place_kernel,
        in_specs=[SMEM, SMEM, VMEM, VMEM, ANY],
        out_specs=ANY,
        out_shape=jax.ShapeDtypeStruct(out.shape, F32),
        scratch_shapes=[pltpu.SemaphoreType.DMA((2,))],
        input_output_aliases={4: 0},
        compiler_params=PARAMS,
        cost_estimate=cost(0, 8 * (f3.size + brow.size)),
        name="place",
    )(info, spots, f3, brow, out)


def plan(pivots, width, procs, me):
    p0, p1 = pivots[0], pivots[1]
    count = jnp.arange(width, dtype=jnp.int32)
    hit = p0[:, None] == p1[None, :]
    back = p0[:, None] == width + count[None, :]
    src1 = jnp.where(hit.any(0), jnp.sum(jnp.where(hit, count[:, None], 0), 0), p1)
    dest0 = jnp.where(
        back.any(1),
        jnp.sum(jnp.where(back, p1[None, :], 0), 1),
        jnp.where(hit.any(1), -1, p0),
    )
    dest1 = jnp.where(back.any(0), -1, p1)
    src = jnp.concatenate([p0, src1])
    dest = jnp.concatenate([dest0, dest1])
    src_owner = src // width % procs
    src_local = src // width // procs * width + src % width
    dest_owner = jnp.where(dest >= 0, dest // width % procs, -1)
    dest_local = dest // width // procs * width + dest % width
    order = jnp.arange(2 * width, dtype=jnp.int32)
    earlier = order[None, :] < order[:, None]
    same_half = (order[None, :] // width) == (order[:, None] // width)
    src_rank = jnp.sum(
        (earlier & (src_owner[None, :] == src_owner[:, None])).astype(jnp.int32), 1
    )
    dest_rank = jnp.sum(
        (earlier & same_half & (dest_owner[None, :] == dest_owner[:, None])).astype(jnp.int32), 1
    )
    src_most = jnp.max(src_rank) + 1
    dest_most = jnp.max(jnp.where(dest >= 0, dest_rank, -1)) + 1
    return src_owner, src_local, src_rank, dest_owner, dest_local, dest_rank, src_most, dest_most


def flip(procs, x):
    return [(s, s ^ x) for s in range(procs)]


def send(value, axis, pairs):
    flat = value.reshape(-1, LANES)
    return lax.ppermute(flat, axis, pairs).reshape(value.shape)


def exchange(cap, fcap, m3, width, info, src, dest):
    per = width // LANES
    procs = lax.axis_size("prow")
    me = info[0]
    src_owner, src_local, src_rank = src
    dest_owner, dest_local, dest_rank = dest

    src_rank = jnp.minimum(src_rank, cap - 1)
    slots = jnp.arange(cap, dtype=jnp.int32)
    mine = (src_owner == me)[None, :] & (src_rank[None, :] == slots[:, None])
    row_list = jnp.max(jnp.where(mine, src_local[None, :], 0), 1)

    fslots = jnp.arange(fcap, dtype=jnp.int32)
    owner2 = dest_owner.reshape(2, width)
    rank2 = dest_rank.reshape(2, width)
    local2 = dest_local.reshape(2, width)
    to = me ^ jnp.arange(procs, dtype=jnp.int32)
    out_owner = jnp.where(me == 0, owner2[0], owner2[1])
    out_rank = jnp.where(me == 0, rank2[0], rank2[1])
    chosen = (out_owner[None, None, :] == to[:, None, None]) & (
        out_rank[None, None, :] == fslots[None, :, None]
    )
    out_list = jnp.sum(jnp.where(chosen, jnp.arange(width, dtype=jnp.int32), 0), 2)
    landing = (owner2[:, None, :] == me) & (rank2[:, None, :] == fslots[None, :, None])
    spots = (jnp.sum(jnp.where(landing, local2[:, None, :] + 1, 0), 2) - 1).reshape(2 * fcap)

    halves, outgoing, heads = collect(info, row_list, out_list, m3, per, width)
    heads = [heads[0]] + [send(heads[x], "prow", flip(procs, x)) for x in range(1, procs)]
    bits = [1 << b for b in range(procs.bit_length() - 1)]
    turned = bits[len(bits) // 2 :] + bits[: len(bits) // 2]
    gathered = []
    for half, order in zip(halves, (bits, turned)):
        bufs, kinds = [half], [0]
        for bit in order:
            bufs = bufs + [send(buf, "prow", flip(procs, bit)) for buf in bufs]
            kinds = kinds + [kind ^ bit for kind in kinds]
        gathered.append((bufs, tuple(kinds)))
    displaced = [outgoing[0]] + [
        send(outgoing[x], "prow", [(s, s ^ x) for s in range(2)]) for x in range(1, procs)
    ]
    return info, src_owner, src_rank, heads, gathered, displaced, spots


def exchange_any(m3, width, info, src, dest):
    per = width // LANES
    half = m3.shape[1] // 2
    me = info[0]
    src_owner, src_local, _ = src
    dest_owner, dest_local, _ = dest
    rows = jnp.where((src_owner == me)[:, None, None], m3[src_local], 0.0)
    rows = lax.psum(rows.reshape(-1, LANES), "prow").reshape(rows.shape)
    displaced = []
    for source in range(2):
        top = jnp.where(me == source, m3[:width], 0.0)
        displaced.append(lax.psum(top.reshape(-1, LANES), "prow").reshape(top.shape))
    heads = [jnp.concatenate([rows[:, :per], top[:, :per]]) for top in displaced]
    gathered = [([rows[:, :half]], (0,)), ([rows[:, half:]], (0,))]
    spots = jnp.where(dest_owner == me, dest_local, -1)
    order = jnp.arange(2 * width, dtype=jnp.int32)
    first = jnp.concatenate([jnp.zeros((1,), jnp.int32), info[1:]])
    return first, jnp.zeros_like(order), order, heads, gathered, displaced, spots


def factor(cap, fcap, m3, inv, info, src, dest, out=None):
    rows, groups, _ = m3.shape
    width = inv.shape[1]
    chips = lax.axis_size("pcol") // 2
    per = width // LANES
    z = info[2]
    m2 = m3.reshape(rows * groups, LANES)
    m4 = m3.reshape(rows, groups // per, per, LANES)
    hop = [(q, q + 2) for q in range(2 * chips - 2)]
    swap = [(q, q ^ 1) for q in range(2 * chips)]

    chunk = rows // CHUNKS
    length = CHUNKS // CHAINS
    pieces = panel(m4, 0, CHAINS, chunk) + panel(m4, CHAINS, CHUNKS - CHAINS, chunk)
    own = [[] for _ in range(CHAINS)]
    sib = [[] for _ in range(CHAINS)]
    for t in range(length + chips - 1):
        for k in range(CHAINS):
            piece = pieces[t * CHAINS + k].reshape(chunk * per, LANES) if t < length else None
            if t == 0:
                cur = piece
            else:
                cur = send(own[k][-1], "pcol", hop)
                if t < length:
                    cur = jnp.where(z == 0, piece, cur)
            own[k].append(cur)
            sib[k].append(send(cur, "pcol", swap))

    if cap is None:
        cap, moves = 2 * width, exchange_any(m3, width, info, src, dest)
    else:
        moves = exchange(cap, fcap, m3, width, info, src, dest)
    seen, owner, rank, heads, gathered, displaced, spots = moves
    tab, ftab = tables(seen, owner, rank, heads, cap, width)

    def spread(table):
        table = table.reshape(-1, LANES)
        for h in range(1, chips):
            pairs = [(2 * h - 2, 2 * h), (2 * h - 1, 2 * h + 1)]
            table = jnp.where(z == h, lax.ppermute(table, "pcol", pairs), table)
        return table, lax.ppermute(table, "pcol", swap)

    tab_own, tab_sib = spread(tab)
    ftab_own, ftab_sib = spread(ftab)
    (a_bufs, order_a), (b_bufs, order_b) = gathered
    uhl, brow, u01 = solve(
        seen, owner, rank, a_bufs, b_bufs, order_a, order_b, tab_own, tab_sib, inv, groups, per
    )
    fixed = moved(seen, displaced, ftab_own, ftab_sib, inv, u01, uhl, per)

    if out is not None:
        out = out.reshape(m2.shape)
    for t in range(length):
        bufs = []
        for k in range(CHAINS):
            bufs += own[k][t : t + chips] + sib[k][t : t + chips]
        out = bulk(
            info, bufs, m2, inv, u01, uhl, out, t * CHAINS * chunk, CHAINS, chunk, groups, per
        )
    return place(info, spots, fixed, brow, out.reshape(rows, groups, LANES))


def shards(matrix, pivots, inverse_blocks):
    row_blocks, _, width, blocks, _, _ = matrix.shape
    procs = lax.axis_size("prow")
    me = lax.axis_index("prow").astype(jnp.int32)
    mc = lax.axis_index("pcol").astype(jnp.int32)
    info = jnp.stack([me, mc, mc // 2, mc % 2])
    so, sl, sr, do, dl, dr, src_most, dest_most = plan(pivots, width, procs, me)
    mean = 2 * width // procs
    cap = min(2 * width, (mean + 3 * mean // 8 + 7) // 8 * 8)
    fmean = width // procs
    fcap = min(width, (fmean + fmean // 2 + 7) // 8 * 8)
    again = (src_most > cap) | (dest_most > fcap)
    m3 = matrix.reshape(row_blocks * width, -1, LANES)
    args = (m3, inverse_blocks, info, (so, sl, sr), (do, dl, dr))
    out = factor(cap, fcap, *args)

    out = lax.cond(
        again,
        lambda done, *rest: factor(None, None, *rest, done),
        lambda done, *rest: done,
        out,
        *args,
    )
    return out.reshape(matrix.shape)


def solution(mesh):
    return jax.shard_map(
        shards,
        mesh=mesh,
        in_specs=(P(None, "prow", None, None, "pcol", None), P(), P()),
        out_specs=P(None, "prow", None, None, "pcol", None),
        check_vma=False,
    )
```

```python
import functools

import jax
import jax.numpy as jnp
from jax import lax
from jax.experimental import pallas as pl
from jax.experimental.pallas import tpu as pltpu
from jax.sharding import PartitionSpec as P

LANES = 128
CHUNKS = 16
CHAINS = 2
TABLE_AT = 2
TILE = 256
F32 = jnp.float32
BF16 = jnp.bfloat16
ANY = pl.BlockSpec(memory_space=pl.ANY)
VMEM = pl.BlockSpec(memory_space=pltpu.VMEM)
SMEM = pl.BlockSpec(memory_space=pltpu.SMEM)
PARAMS = pltpu.CompilerParams(vmem_limit_bytes=56 << 20)


def cost(flops, nbytes):
    return pl.CostEstimate(flops=int(flops), bytes_accessed=int(nbytes), transcendentals=0)


def split(x):
    high = x.astype(BF16)
    return high, (x - high.astype(F32)).astype(BF16)


def dot3(left, right):
    out = jnp.dot(left[0], right[0], preferred_element_type=F32)
    out += jnp.dot(left[0], right[1], preferred_element_type=F32)
    return out + jnp.dot(left[1], right[0], preferred_element_type=F32)


def upper(packed):
    row = lax.broadcasted_iota(jnp.int32, packed.shape, 0)
    col = lax.broadcasted_iota(jnp.int32, packed.shape, 1)
    return jnp.where(col >= row, packed, 0.0)


def unit_lower(packed):
    row = lax.broadcasted_iota(jnp.int32, packed.shape, 0)
    col = lax.broadcasted_iota(jnp.int32, packed.shape, 1)
    return jnp.where(col < row, packed, jnp.where(col == row, 1.0, 0.0))


def get_block(ref, start, count, pitch, block, per):
    parts = [ref[pl.ds(start * pitch + block * per + h, count, stride=pitch), :] for h in range(per)]
    return jnp.concatenate(parts, axis=1)


def put_block(ref, start, count, pitch, block, per, value):
    for h in range(per):
        ref[pl.ds(start * pitch + block * per + h, count, stride=pitch), :] = value[
            :, h * LANES : (h + 1) * LANES
        ]


def multiply(count, width, mc, l0, l1, stack_ref, uhl_ref, s_ref, pitch, per):
    l0s, l1s = split(l0), split(l1)
    for part in range(2):
        stack_ref[part * count : (part + 1) * count, :width] = l0s[part]
        stack_ref[part * count : (part + 1) * count, width:] = l1s[part]

    def step(block, carry):
        cols = pl.ds(pl.multiple_of(block * width, width), width)
        both = jnp.dot(stack_ref[...], uhl_ref[0, :, cols], preferred_element_type=F32)
        acc = jnp.dot(stack_ref[:count], uhl_ref[1, :, cols], preferred_element_type=F32)
        put_block(s_ref, 0, count, pitch, block, per, acc + both[:count] + both[count:])
        return carry

    lax.fori_loop(0, uhl_ref.shape[2] // width, step, 0)

    @pl.when(mc == 0)
    def _():
        put_block(s_ref, 0, count, pitch, 0, per, -l0)

    @pl.when(mc == 1)
    def _():
        put_block(s_ref, 0, count, pitch, 0, per, -l1)


def lower_rows(c0, c1, inv_ref, u01_ref):
    l0 = dot3(split(c0), split(upper(inv_ref[0])))
    rest = c1 - dot3(split(l0), split(u01_ref[...]))
    return l0, dot3(split(rest), split(upper(inv_ref[1])))


def combine(first, count, groups, per, mc, s_ref, get, put):
    drop = (lax.broadcasted_iota(jnp.int32, (groups, LANES), 0) < per) & (mc < 2)

    def step(i, carry):
        put(i, jnp.where(drop, 0.0, get(i)) - s_ref[pl.ds(i * (groups + 1), groups), :])
        return carry

    lax.fori_loop(first, first + count, step, 0, unroll=8)


def panel_copies(info_ref, chips, bufs, c0_ref, c1_ref, sem, act):
    rows = bufs[0].shape[0]
    for h in range(chips):
        for core in range(2):

            @pl.when((info_ref[2] == h) & (info_ref[3] == core))
            def _():
                for n in range(len(bufs) // (2 * chips)):
                    own, sib = bufs[2 * n * chips + h], bufs[(2 * n + 1) * chips + h]
                    first, second = (own, sib) if core == 0 else (sib, own)
                    spot = pl.ds(n * rows, rows)
                    act(pltpu.make_async_copy(first, c0_ref.at[spot], sem.at[2 * n]))
                    act(pltpu.make_async_copy(second, c1_ref.at[spot], sem.at[2 * n + 1]))


def start(copy):
    copy.start()


def wait(copy):
    copy.wait()


def panel(m4, first, count, rows):
    shape = (rows,) + m4.shape[2:]

    def kernel(m_ref, *rest):
        outs, sem = rest[:count], rest[count]
        copies = [
            pltpu.make_async_copy(m_ref.at[pl.ds((first + k) * rows, rows), 0], outs[k], sem.at[k])
            for k in range(count)
        ]
        for copy in copies:
            copy.start()
        for copy in copies:
            copy.wait()

    return pl.pallas_call(
        kernel,
        in_specs=[ANY],
        out_specs=[VMEM] * count,
        out_shape=[jax.ShapeDtypeStruct(shape, F32)] * count,
        scratch_shapes=[pltpu.SemaphoreType.DMA((count,))],
        compiler_params=PARAMS,
        cost_estimate=cost(0, 8 * count * rows * shape[1] * shape[2]),
        name="panel",
    )(m4)


def collect_kernel(procs, per, info_ref, list_ref, out_list_ref, m_ref, *rest):
    row_ref = rest[0]
    out_refs, head_refs = rest[1 : 1 + procs], rest[1 + procs : 1 + 2 * procs]
    top_ref, sem = rest[1 + 2 * procs :]
    cap = row_ref.shape[0]
    width = top_ref.shape[0]
    fcap = out_refs[0].shape[0]
    top = pltpu.make_async_copy(m_ref.at[pl.ds(0, width)], top_ref, sem.at[0])
    top.start()

    def fetch(k, carry):
        pltpu.make_async_copy(m_ref.at[list_ref[k]], row_ref.at[k], sem.at[1]).start()
        return carry

    lax.fori_loop(0, cap, fetch, 0)
    top.wait()

    @pl.when(info_ref[0] < 2)
    def _():
        for x in range(procs):

            def give(k, carry):
                row = top_ref[out_list_ref[x, k]]
                out_refs[x][k] = row
                head_refs[x][cap + k] = row[0:per]
                return carry

            lax.fori_loop(0, fcap, give, 0, unroll=4)

    pltpu.make_async_copy(row_ref, row_ref, sem.at[1]).wait()

    def keep(k, carry):
        row = row_ref[k, 0:per, :]
        for x in range(procs):
            head_refs[x][k] = row
        return carry

    lax.fori_loop(0, cap, keep, 0, unroll=4)


def collect(info, row_list, out_list, m3, per, width):
    cap = row_list.shape[0]
    procs, fcap = out_list.shape
    groups = m3.shape[1]
    out = jax.ShapeDtypeStruct((fcap, groups, LANES), F32)
    head = jax.ShapeDtypeStruct((cap + fcap, per, LANES), F32)
    outs = pl.pallas_call(
        functools.partial(collect_kernel, procs, per),
        in_specs=[SMEM, SMEM, SMEM, ANY],
        out_specs=[VMEM] * (1 + 2 * procs),
        out_shape=[jax.ShapeDtypeStruct((cap, groups, LANES), F32)] + [out] * procs + [head] * procs,
        scratch_shapes=[
            pltpu.VMEM((width, groups, LANES), F32),
            pltpu.SemaphoreType.DMA((2,)),
        ],
        compiler_params=PARAMS,
        cost_estimate=cost(0, 16 * (cap + procs * fcap) * groups * LANES),
        name="collect",
    )(info, row_list, out_list, m3)
    return outs[0], outs[1 : 1 + procs], outs[1 + procs :]


def tables_kernel(procs, cap, width, info_ref, owner_ref, rank_ref, *rest):
    ins = rest[:procs]
    o_ref, buf_ref, sem = rest[procs:]
    fcap = buf_ref.shape[1] - cap
    copies = [
        pltpu.make_async_copy(ins[x], buf_ref.at[info_ref[0] ^ x], sem.at[x]) for x in range(procs)
    ]
    for copy in copies:
        copy.start()
    for copy in copies:
        copy.wait()
    base = jnp.where(info_ref[3] == 0, width, 0)

    def pivot(k, carry):
        o_ref[k] = buf_ref[owner_ref[base + k], rank_ref[base + k]]
        return carry

    lax.fori_loop(0, width, pivot, 0, unroll=4)
    for source in range(2):

        def other(k, carry):
            o_ref[width + source * fcap + k] = buf_ref[source, cap + k]
            return carry

        lax.fori_loop(0, fcap, other, 0, unroll=4)


def tables(info, owner, rank, heads, cap, width, rows):
    procs = len(heads)
    both, per, _ = heads[0].shape
    return pl.pallas_call(
        functools.partial(tables_kernel, procs, cap, width),
        in_specs=[SMEM, SMEM, SMEM] + [ANY] * procs,
        out_specs=VMEM,
        out_shape=jax.ShapeDtypeStruct((rows, per, LANES), F32),
        scratch_shapes=[
            pltpu.VMEM((procs, both, per, LANES), F32),
            pltpu.SemaphoreType.DMA((procs,)),
        ],
        compiler_params=PARAMS,
        cost_estimate=cost(0, 8 * procs * heads[0].size),
        name="tables",
    )(info, owner, rank, *heads)


def solve_kernel(chips, groups, per, info_ref, owner_ref, rank_ref, g_ref, *rest):
    (*bufs, inv_ref, uhl_ref, brow_ref, u01_ref, a_ref, c0_ref, c1_ref, s_ref, sem) = rest
    width = per * LANES
    pitch = groups + 1
    mc = info_ref[1]
    rows = pltpu.make_async_copy(g_ref, a_ref, sem.at[0])
    rows.start()
    panel_copies(info_ref, chips, bufs, c0_ref, c1_ref, sem.at[pl.ds(1, sem.shape[0] - 1)], start)
    panel_copies(info_ref, chips, bufs, c0_ref, c1_ref, sem.at[pl.ds(1, sem.shape[0] - 1)], wait)
    z1c0 = get_block(c0_ref, 0, width, per, 0, per)
    g0c1 = get_block(c1_ref, 0, width, per, 0, per)
    one0 = unit_lower(inv_ref[0])
    low0, low1 = split(one0), split(unit_lower(inv_ref[1]))
    l01 = dot3(split(z1c0), split(upper(inv_ref[0])))
    l01s = split(l01)
    u01_ref[...] = dot3(low0, split(g0c1))
    back = split(dot3(low1, split(dot3(l01s, low0))))
    highs = jnp.concatenate([low0[0], back[0]], axis=0)
    every = jnp.concatenate([highs, low0[1], back[1]], axis=0)
    low1s = jnp.concatenate([low1[0], low1[1]], axis=0)
    rows.wait()

    def line_up(k, carry):
        s_ref[pl.ds(k * pitch, groups), :] = a_ref[owner_ref[k], rank_ref[k]]
        return carry

    lax.fori_loop(0, 2 * width, line_up, 0, unroll=8)

    def solved(block):
        g0 = get_block(s_ref, 0, width, pitch, block, per)
        z1 = get_block(s_ref, width, width, pitch, block, per)
        g0s, z1s = split(g0), split(z1)
        first = jnp.dot(every, g0s[0], preferred_element_type=F32)
        second = jnp.dot(highs, g0s[1], preferred_element_type=F32)
        both = first[: 2 * width] + second + first[2 * width :]
        third = jnp.dot(low1s, z1s[0], preferred_element_type=F32)
        own = third[:width] + third[width:] + jnp.dot(low1[0], z1s[1], preferred_element_type=F32)
        u0 = both[:width]
        u1 = own - both[width:]
        cols = pl.ds(block * width, width)
        for ref_rows, value in ((pl.ds(0, width), u0), (pl.ds(width, width), u1)):
            high, low = split(value)
            uhl_ref[0, ref_rows, cols] = high
            uhl_ref[1, ref_rows, cols] = low
        return g0, z1, u0, u1

    g0, z1, u0, u1 = solved(0)
    a1 = z1 - dot3(l01s, split(u0))
    put_block(s_ref, 0, width, pitch, 0, per, jnp.where(mc == 0, g0, u0))
    put_block(s_ref, width, width, pitch, 0, per, jnp.where(mc == 0, l01, jnp.where(mc == 1, a1, u1)))

    def step(block, carry):
        _, _, u0, u1 = solved(pl.multiple_of(block, 1))
        put_block(s_ref, 0, width, pitch, block, per, u0)
        put_block(s_ref, width, width, pitch, block, per, u1)
        return carry

    lax.fori_loop(1, groups // per, step, 0)

    def lay_out(k, carry):
        brow_ref[k] = s_ref[pl.ds(k * pitch, groups), :]
        return carry

    lax.fori_loop(0, 2 * width, lay_out, 0, unroll=8)


def solve(info, owner, rank, gathered, chips, bufs, inv):
    groups = gathered.shape[2]
    width = inv.shape[1]
    per = width // LANES
    cols = groups * LANES
    count = len(bufs) // (2 * chips)
    tab = pltpu.VMEM((count * bufs[0].shape[0], LANES), F32)
    return pl.pallas_call(
        functools.partial(solve_kernel, chips, groups, per),
        in_specs=[SMEM, SMEM, SMEM] + [ANY] * (1 + len(bufs)) + [VMEM],
        out_specs=[VMEM, VMEM, VMEM],
        out_shape=[
            jax.ShapeDtypeStruct((2, 2 * width, cols), BF16),
            jax.ShapeDtypeStruct((2 * width, groups, LANES), F32),
            jax.ShapeDtypeStruct((width, width), F32),
        ],
        scratch_shapes=[
            pltpu.VMEM(gathered.shape, F32),
            tab,
            tab,
            pltpu.VMEM((2 * width * (groups + 1), LANES), F32),
            pltpu.SemaphoreType.DMA((1 + 2 * count,)),
        ],
        compiler_params=PARAMS,
        cost_estimate=cost(18 * width * width * cols, 24 * width * cols),
        name="solve",
    )(info, owner, rank, gathered, *bufs, inv)


def bulk_kernel(chips, number, first, parts, groups, per, info_ref, *rest):
    bufs = rest[:number]
    m_ref, uhl_ref, inv_ref, u01_ref = rest[number : number + 4]
    o_ref, c0_ref, c1_ref, u_ref, row_ref, stack_ref, s_ref, psem, sem = rest[-9:]
    count = stack_ref.shape[0] // 2
    width = per * LANES
    panel_copies(info_ref, chips, bufs, c0_ref, c1_ref, psem, start)
    u_copy = pltpu.make_async_copy(uhl_ref, u_ref, sem.at[0])
    u_copy.start()
    rows = pltpu.make_async_copy(m_ref.at[pl.ds(first * groups, count * groups)], row_ref, sem.at[1])
    rows.start()
    panel_copies(info_ref, chips, bufs, c0_ref, c1_ref, psem, wait)
    l0, l1 = lower_rows(
        get_block(c0_ref, 0, count, per, 0, per),
        get_block(c1_ref, 0, count, per, 0, per),
        inv_ref,
        u01_ref,
    )
    u_copy.wait()
    multiply(count, width, info_ref[1], l0, l1, stack_ref, u_ref, s_ref, groups + 1, per)
    rows.wait()

    def get(i):
        return row_ref[pl.ds(pl.multiple_of(i * groups, groups), groups), :]

    def put(i, value):
        row_ref[pl.ds(pl.multiple_of(i * groups, groups), groups), :] = value

    piece = count // parts
    outs = []
    for n in range(parts):
        combine(n * piece, piece, groups, per, info_ref[1], s_ref, get, put)
        copy = pltpu.make_async_copy(
            row_ref.at[pl.ds(n * piece * groups, piece * groups)],
            o_ref.at[pl.ds((first + n * piece) * groups, piece * groups)],
            sem.at[2 + n],
        )
        copy.start()
        outs.append(copy)
    for copy in outs:
        copy.wait()


def bulk(info, chips, bufs, m2, inv, u01, uhl, out, first, groups):
    width = inv.shape[1]
    per = width // LANES
    count = len(bufs) // (2 * chips) * bufs[0].shape[0] // per
    cols = groups * LANES
    parts = 4
    in_specs = [SMEM] + [ANY] * (len(bufs) + 2) + [VMEM] * 2
    args = [info, *bufs, m2, uhl, inv, u01]
    aliases = {}
    if out is not None:
        in_specs.append(ANY)
        aliases = {len(args): 0}
        args.append(out)
    return pl.pallas_call(
        functools.partial(bulk_kernel, chips, len(bufs), first, parts, groups, per),
        in_specs=in_specs,
        out_specs=ANY,
        out_shape=jax.ShapeDtypeStruct(m2.shape, F32),
        scratch_shapes=[
            pltpu.VMEM((count * per, LANES), F32),
            pltpu.VMEM((count * per, LANES), F32),
            pltpu.VMEM(uhl.shape, BF16),
            pltpu.VMEM((count * groups, LANES), F32),
            pltpu.VMEM((2 * count, 2 * width), BF16),
            pltpu.VMEM((count * (groups + 1), LANES), F32),
            pltpu.SemaphoreType.DMA((len(bufs) // chips,)),
            pltpu.SemaphoreType.DMA((2 + parts,)),
        ],
        input_output_aliases=aliases,
        compiler_params=PARAMS,
        cost_estimate=cost(12 * count * width * cols, 8 * count * cols),
        name="bulk",
    )(*args)


def moved_kernel(chips, procs, skip, groups, per, info_ref, *rest):
    ins = rest[:procs]
    (*bufs, inv_ref, u01_ref, uhl_ref, o_ref, c0_ref, c1_ref, f_ref, stack_ref, s_ref, psem, sem) = rest[
        procs:
    ]
    rows = f_ref.shape[0]
    panel_copies(info_ref, chips, bufs, c0_ref, c1_ref, psem, start)
    for act in (start, wait):
        for source in range(2):
            spot = pl.ds(source * (rows // 2), rows // 2)
            for x in range(procs):

                @pl.when((info_ref[0] ^ source) == x)
                def _():
                    act(pltpu.make_async_copy(ins[x], f_ref.at[spot], sem.at[source]))

    panel_copies(info_ref, chips, bufs, c0_ref, c1_ref, psem, wait)
    l0, l1 = lower_rows(
        get_block(c0_ref, skip, rows, per, 0, per),
        get_block(c1_ref, skip, rows, per, 0, per),
        inv_ref,
        u01_ref,
    )
    multiply(rows, per * LANES, info_ref[1], l0, l1, stack_ref, uhl_ref, s_ref, groups + 1, per)

    def get(i):
        return f_ref[i]

    def put(i, value):
        o_ref[i] = value

    combine(0, rows, groups, per, info_ref[1], s_ref, get, put)


def moved(info, displaced, chips, bufs, inv, u01, uhl):
    fcap, groups, _ = displaced[0].shape
    rows = 2 * fcap
    width = inv.shape[1]
    per = width // LANES
    tab = pltpu.VMEM((len(bufs) // (2 * chips) * bufs[0].shape[0], LANES), F32)
    return pl.pallas_call(
        functools.partial(moved_kernel, chips, len(displaced), width, groups, per),
        in_specs=[SMEM] + [ANY] * (len(displaced) + len(bufs)) + [VMEM] * 3,
        out_specs=VMEM,
        out_shape=jax.ShapeDtypeStruct((rows, groups, LANES), F32),
        scratch_shapes=[
            tab,
            tab,
            pltpu.VMEM((rows, groups, LANES), F32),
            pltpu.VMEM((2 * rows, 2 * width), BF16),
            pltpu.VMEM((rows * (groups + 1), LANES), F32),
            pltpu.SemaphoreType.DMA((len(bufs) // chips,)),
            pltpu.SemaphoreType.DMA((2,)),
        ],
        compiler_params=PARAMS,
        cost_estimate=cost(12 * rows * per * groups * LANES * LANES, 8 * rows * groups * LANES),
        name="moved",
    )(info, *displaced, *bufs, inv, u01, uhl)


def place_kernel(info_ref, spot_ref, f_ref, brow_ref, _, o_ref, sem):
    width = brow_ref.shape[0] // 2
    count = f_ref.shape[0]

    def put(k):
        return pltpu.make_async_copy(f_ref.at[k], o_ref.at[spot_ref[k]], sem.at[0])

    def start(k, carry):
        @pl.when(spot_ref[k] >= 0)
        def _():
            put(k).start()

        return carry

    def finish(k, carry):
        @pl.when(spot_ref[k] >= 0)
        def _():
            put(k).wait()

        return carry

    source = jnp.minimum(info_ref[0], 1)
    top = pltpu.make_async_copy(
        brow_ref.at[pl.ds(source * width, width)], o_ref.at[pl.ds(0, width)], sem.at[1]
    )

    @pl.when(info_ref[0] < 2)
    def _():
        top.start()

    lax.fori_loop(0, count, start, 0)
    lax.fori_loop(0, count, finish, 0)

    @pl.when(info_ref[0] < 2)
    def _():
        top.wait()


def place(info, spots, f3, brow, out):
    return pl.pallas_call(
        place_kernel,
        in_specs=[SMEM, SMEM, VMEM, VMEM, ANY],
        out_specs=ANY,
        out_shape=jax.ShapeDtypeStruct(out.shape, F32),
        scratch_shapes=[pltpu.SemaphoreType.DMA((2,))],
        input_output_aliases={4: 0},
        compiler_params=PARAMS,
        cost_estimate=cost(0, 8 * (f3.size + brow.size)),
        name="place",
    )(info, spots, f3, brow, out)


def plan(pivots, width, procs, me):
    p0, p1 = pivots[0], pivots[1]
    count = jnp.arange(width, dtype=jnp.int32)
    hit = p0[:, None] == p1[None, :]
    back = p0[:, None] == width + count[None, :]
    src1 = jnp.where(hit.any(0), jnp.sum(jnp.where(hit, count[:, None], 0), 0), p1)
    dest0 = jnp.where(
        back.any(1),
        jnp.sum(jnp.where(back, p1[None, :], 0), 1),
        jnp.where(hit.any(1), -1, p0),
    )
    dest1 = jnp.where(back.any(0), -1, p1)
    src = jnp.concatenate([p0, src1])
    dest = jnp.concatenate([dest0, dest1])
    src_owner = src // width % procs
    src_local = src // width // procs * width + src % width
    dest_owner = jnp.where(dest >= 0, dest // width % procs, -1)
    dest_local = dest // width // procs * width + dest % width
    order = jnp.arange(2 * width, dtype=jnp.int32)
    earlier = order[None, :] < order[:, None]
    same_half = (order[None, :] // width) == (order[:, None] // width)
    src_rank = jnp.sum(
        (earlier & (src_owner[None, :] == src_owner[:, None])).astype(jnp.int32), 1
    )
    dest_rank = jnp.sum(
        (earlier & same_half & (dest_owner[None, :] == dest_owner[:, None])).astype(jnp.int32), 1
    )
    src_most = jnp.max(src_rank) + 1
    dest_most = jnp.max(jnp.where(dest >= 0, dest_rank, -1)) + 1
    return src_owner, src_local, src_rank, dest_owner, dest_local, dest_rank, src_most, dest_most


def flip(procs, x):
    return [(s, s ^ x) for s in range(procs)]


def send(value, axis, pairs):
    flat = value.reshape(-1, LANES)
    return lax.ppermute(flat, axis, pairs).reshape(value.shape)


def exchange(cap, fcap, m3, width, info, src, dest):
    per = width // LANES
    procs = lax.axis_size("prow")
    me = info[0]
    src_owner, src_local, src_rank = src
    dest_owner, dest_local, dest_rank = dest

    src_rank = jnp.minimum(src_rank, cap - 1)
    slots = jnp.arange(cap, dtype=jnp.int32)
    mine = (src_owner == me)[None, :] & (src_rank[None, :] == slots[:, None])
    row_list = jnp.max(jnp.where(mine, src_local[None, :], 0), 1)

    fslots = jnp.arange(fcap, dtype=jnp.int32)
    owner2 = dest_owner.reshape(2, width)
    rank2 = dest_rank.reshape(2, width)
    local2 = dest_local.reshape(2, width)
    to = me ^ jnp.arange(procs, dtype=jnp.int32)
    out_owner = jnp.where(me == 0, owner2[0], owner2[1])
    out_rank = jnp.where(me == 0, rank2[0], rank2[1])
    chosen = (out_owner[None, None, :] == to[:, None, None]) & (
        out_rank[None, None, :] == fslots[None, :, None]
    )
    out_list = jnp.sum(jnp.where(chosen, jnp.arange(width, dtype=jnp.int32), 0), 2)
    landing = (owner2[:, None, :] == me) & (rank2[:, None, :] == fslots[None, :, None])
    spots = (jnp.sum(jnp.where(landing, local2[:, None, :] + 1, 0), 2) - 1).reshape(2 * fcap)

    sent, outgoing, heads = collect(info, row_list, out_list, m3, per, width)
    heads = [heads[0]] + [send(heads[x], "prow", flip(procs, x)) for x in range(1, procs)]
    gathered = lax.all_gather(sent.reshape(-1, LANES), "prow", axis=0, tiled=True)
    gathered = gathered.reshape((procs,) + sent.shape)
    displaced = [outgoing[0]] + [
        send(outgoing[x], "prow", [(s, s ^ x) for s in range(2)]) for x in range(1, procs)
    ]
    return info, src_owner, src_rank, heads, gathered, displaced, spots


def exchange_any(m3, width, info, src, dest):
    per = width // LANES
    me = info[0]
    src_owner, src_local, _ = src
    dest_owner, dest_local, _ = dest
    rows = jnp.where((src_owner == me)[:, None, None], m3[src_local], 0.0)
    rows = lax.psum(rows.reshape(-1, LANES), "prow").reshape(rows.shape)
    displaced = []
    for source in range(2):
        top = jnp.where(me == source, m3[:width], 0.0)
        displaced.append(lax.psum(top.reshape(-1, LANES), "prow").reshape(top.shape))
    heads = [jnp.concatenate([rows[:, :per], top[:, :per]]) for top in displaced]
    spots = jnp.where(dest_owner == me, dest_local, -1)
    order = jnp.arange(2 * width, dtype=jnp.int32)
    first = jnp.concatenate([jnp.zeros((1,), jnp.int32), info[1:]])
    return first, jnp.zeros_like(order), order, heads, rows[None], displaced, spots


def factor(cap, fcap, m3, inv, info, first, src, dest, out=None):
    rows, groups, _ = m3.shape
    width = inv.shape[1]
    chips = lax.axis_size("pcol") // 2
    per = width // LANES
    z = info[2]
    m2 = m3.reshape(rows * groups, LANES)
    m4 = m3.reshape(rows, groups // per, per, LANES)
    chunk = rows // CHUNKS
    hop = [(q, q + 2) for q in range(2 * chips - 2)]
    swap = [(q, q ^ 1) for q in range(2 * chips)]
    pieces = list(first) + list(panel(m4, CHAINS, CHUNKS - CHAINS, chunk))

    if cap is None:
        cap, fcap, moves = 2 * width, width, exchange_any(m3, width, info, src, dest)
    else:
        moves = exchange(cap, fcap, m3, width, info, src, dest)
    seen, owner, rank, heads, gathered, displaced, spots = moves
    share = -(-(width + 2 * fcap) // (chunk * CHAINS))
    table = tables(seen, owner, rank, heads, cap, width, share * CHAINS * chunk)

    items = [piece.reshape(chunk * per, LANES) for piece in pieces]
    table = table.reshape(share * CHAINS, chunk * per, LANES)
    at = TABLE_AT * CHAINS
    items[at:at] = [table[n] for n in range(share * CHAINS)]
    length = len(items) // CHAINS
    own = [[] for _ in range(CHAINS)]
    sib = [[] for _ in range(CHAINS)]
    for t in range(length + chips - 1):
        for k in range(CHAINS):
            cur = items[t * CHAINS + k] if t < length else None
            if t > 0:
                came = send(own[k][-1], "pcol", hop)
                cur = came if cur is None else jnp.where(z == 0, cur, came)
            own[k].append(cur)
            sib[k].append(send(cur, "pcol", swap))

    def held(t, count=1):
        bufs = []
        for n in range(t, t + count):
            for k in range(CHAINS):
                bufs += own[k][n : n + chips] + sib[k][n : n + chips]
        return bufs

    tabs = held(TABLE_AT, share)
    uhl, brow, u01 = solve(seen, owner, rank, gathered, chips, tabs, inv)
    fixed = moved(seen, displaced, chips, tabs, inv, u01, uhl)

    if out is not None:
        out = out.reshape(m2.shape)
    for n in range(CHUNKS // CHAINS):
        t = n if n < TABLE_AT else n + share
        out = bulk(info, chips, held(t), m2, inv, u01, uhl, out, n * CHAINS * chunk, groups)
    return place(info, spots, fixed, brow, out.reshape(rows, groups, LANES))


def shards(matrix, pivots, inverse_blocks):
    row_blocks, _, width, blocks, _, _ = matrix.shape
    procs = lax.axis_size("prow")
    me = lax.axis_index("prow").astype(jnp.int32)
    mc = lax.axis_index("pcol").astype(jnp.int32)
    info = jnp.stack([me, mc, mc // 2, mc % 2])
    m3 = matrix.reshape(row_blocks * width, -1, LANES)
    m4 = matrix.reshape(row_blocks * width, blocks, -1, LANES)
    first = panel(m4, 0, CHAINS, row_blocks * width // CHUNKS)
    pivots, first = lax.optimization_barrier((pivots, first))
    so, sl, sr, do, dl, dr, src_most, dest_most = plan(pivots, width, procs, me)
    mean = 2 * width // procs
    cap = min(2 * width, (mean + 3 * mean // 8 + 7) // 8 * 8)
    fmean = width // procs
    fcap = min(width, (fmean + fmean // 2 + 7) // 8 * 8)
    again = (src_most > cap) | (dest_most > fcap)
    args = (m3, inverse_blocks, info, tuple(first), (so, sl, sr), (do, dl, dr))
    out = factor(cap, fcap, *args)

    out = lax.cond(
        again,
        lambda done, *rest: factor(None, None, *rest, done),
        lambda done, *rest: done,
        out,
        *args,
    )
    return out.reshape(matrix.shape)


def solution(mesh):
    return jax.shard_map(
        shards,
        mesh=mesh,
        in_specs=(P(None, "prow", None, None, "pcol", None), P(), P()),
        out_specs=P(None, "prow", None, None, "pcol", None),
        check_vma=False,
    )
```

```python
import functools

import jax
import jax.numpy as jnp
from jax import lax
from jax.experimental import pallas as pl
from jax.experimental.pallas import tpu as pltpu
from jax.sharding import PartitionSpec as P

LANES = 128
CHUNKS = 16
CHAINS = 2
TABLE_AT = 2
SOLVE_AFTER = 2
F32 = jnp.float32
BF16 = jnp.bfloat16
ANY = pl.BlockSpec(memory_space=pl.ANY)
VMEM = pl.BlockSpec(memory_space=pltpu.VMEM)
SMEM = pl.BlockSpec(memory_space=pltpu.SMEM)
PARAMS = pltpu.CompilerParams(vmem_limit_bytes=56 << 20)


def cost(nbytes):
    return pl.CostEstimate(flops=0, bytes_accessed=int(nbytes), transcendentals=0)


def split(x):
    high = x.astype(BF16)
    return high, (x - high.astype(F32)).astype(BF16)


def dot3(left, right):
    out = jnp.dot(left[0], right[0], preferred_element_type=F32)
    out += jnp.dot(left[0], right[1], preferred_element_type=F32)
    return out + jnp.dot(left[1], right[0], preferred_element_type=F32)


def upper(packed):
    row = lax.broadcasted_iota(jnp.int32, packed.shape, 0)
    col = lax.broadcasted_iota(jnp.int32, packed.shape, 1)
    return jnp.where(col >= row, packed, 0.0)


def unit_lower(packed):
    row = lax.broadcasted_iota(jnp.int32, packed.shape, 0)
    col = lax.broadcasted_iota(jnp.int32, packed.shape, 1)
    return jnp.where(col < row, packed, jnp.where(col == row, 1.0, 0.0))


def get_block(ref, start, count, groups, block, per):
    parts = [
        ref[pl.ds(start * groups + block * per + h, count, stride=groups), :] for h in range(per)
    ]
    return jnp.concatenate(parts, axis=1)


def put_block(ref, start, count, groups, block, per, value):
    for h in range(per):
        ref[pl.ds(start * groups + block * per + h, count, stride=groups), :] = value[
            :, h * LANES : (h + 1) * LANES
        ]


def panel_copies(info_ref, chips, bufs, c0_ref, c1_ref, sem, act):
    rows = bufs[0].shape[0]
    for h in range(chips):
        for core in range(2):

            @pl.when((info_ref[2] == h) & (info_ref[3] == core))
            def _():
                for n in range(len(bufs) // (2 * chips)):
                    own, sib = bufs[2 * n * chips + h], bufs[(2 * n + 1) * chips + h]
                    first, second = (own, sib) if core == 0 else (sib, own)
                    spot = pl.ds(n * rows, rows)
                    act(pltpu.make_async_copy(first, c0_ref.at[spot], sem.at[2 * n]))
                    act(pltpu.make_async_copy(second, c1_ref.at[spot], sem.at[2 * n + 1]))


def start(copy):
    copy.start()


def wait(copy):
    copy.wait()


def panel(m4, first, count, rows):
    shape = (rows,) + m4.shape[2:]

    def kernel(m_ref, *rest):
        outs, sem = rest[:count], rest[count]
        copies = [
            pltpu.make_async_copy(m_ref.at[pl.ds((first + k) * rows, rows), 0], outs[k], sem.at[k])
            for k in range(count)
        ]
        for copy in copies:
            copy.start()
        for copy in copies:
            copy.wait()

    return pl.pallas_call(
        kernel,
        in_specs=[ANY],
        out_specs=[VMEM] * count,
        out_shape=[jax.ShapeDtypeStruct(shape, F32)] * count,
        scratch_shapes=[pltpu.SemaphoreType.DMA((count,))],
        compiler_params=PARAMS,
        cost_estimate=cost(1 << 18),
        name="panel",
    )(m4)


def collect_kernel(procs, per, info_ref, list_ref, out_list_ref, m_ref, *rest):
    row_ref = rest[0]
    out_refs, head_refs = rest[1 : 1 + procs], rest[1 + procs : 1 + 2 * procs]
    top_ref, sem = rest[1 + 2 * procs :]
    cap = row_ref.shape[0]
    width = top_ref.shape[0]
    fcap = out_refs[0].shape[0]
    top = pltpu.make_async_copy(m_ref.at[pl.ds(0, width)], top_ref, sem.at[0])
    top.start()

    def fetch(k, carry):
        pltpu.make_async_copy(m_ref.at[list_ref[k]], row_ref.at[k], sem.at[1]).start()
        return carry

    lax.fori_loop(0, cap, fetch, 0)
    top.wait()

    @pl.when(info_ref[0] < 2)
    def _():
        for x in range(procs):

            def give(k, carry):
                row = top_ref[out_list_ref[x, k]]
                out_refs[x][k] = row
                head_refs[x][cap + k] = row[0:per]
                return carry

            lax.fori_loop(0, fcap, give, 0, unroll=4)

    pltpu.make_async_copy(row_ref, row_ref, sem.at[1]).wait()

    def keep(k, carry):
        row = row_ref[k, 0:per, :]
        for x in range(procs):
            head_refs[x][k] = row
        return carry

    lax.fori_loop(0, cap, keep, 0, unroll=4)


def collect(info, row_list, out_list, m3, per, width):
    cap = row_list.shape[0]
    procs, fcap = out_list.shape
    groups = m3.shape[1]
    out = jax.ShapeDtypeStruct((fcap, groups, LANES), F32)
    head = jax.ShapeDtypeStruct((cap + fcap, per, LANES), F32)
    outs = pl.pallas_call(
        functools.partial(collect_kernel, procs, per),
        in_specs=[SMEM, SMEM, SMEM, ANY],
        out_specs=[VMEM] * (1 + 2 * procs),
        out_shape=[jax.ShapeDtypeStruct((cap, groups, LANES), F32)] + [out] * procs + [head] * procs,
        scratch_shapes=[
            pltpu.VMEM((width, groups, LANES), F32),
            pltpu.SemaphoreType.DMA((2,)),
        ],
        compiler_params=PARAMS,
        cost_estimate=cost(1 << 18),
        name="collect",
    )(info, row_list, out_list, m3)
    return outs[0], outs[1 : 1 + procs], outs[1 + procs :]


def tables_kernel(procs, cap, width, info_ref, owner_ref, rank_ref, *rest):
    ins = rest[:procs]
    o_ref, buf_ref, sem = rest[procs:]
    fcap = buf_ref.shape[1] - cap
    copies = [
        pltpu.make_async_copy(ins[x], buf_ref.at[info_ref[0] ^ x], sem.at[x]) for x in range(procs)
    ]
    for copy in copies:
        copy.start()
    for copy in copies:
        copy.wait()
    base = jnp.where(info_ref[3] == 0, width, 0)

    def pivot(k, carry):
        o_ref[k] = buf_ref[owner_ref[base + k], rank_ref[base + k]]
        return carry

    lax.fori_loop(0, width, pivot, 0, unroll=4)
    for source in range(2):

        def other(k, carry):
            o_ref[width + source * fcap + k] = buf_ref[source, cap + k]
            return carry

        lax.fori_loop(0, fcap, other, 0, unroll=4)


def tables(info, owner, rank, heads, cap, width, rows):
    procs = len(heads)
    both, per, _ = heads[0].shape
    return pl.pallas_call(
        functools.partial(tables_kernel, procs, cap, width),
        in_specs=[SMEM, SMEM, SMEM] + [ANY] * procs,
        out_specs=VMEM,
        out_shape=jax.ShapeDtypeStruct((rows, per, LANES), F32),
        scratch_shapes=[
            pltpu.VMEM((procs, both, per, LANES), F32),
            pltpu.SemaphoreType.DMA((procs,)),
        ],
        compiler_params=PARAMS,
        cost_estimate=cost(1 << 18),
        name="tables",
    )(info, owner, rank, *heads)


def head_kernel(chips, info_ref, *rest):
    (*bufs, inv_ref, c0_ref, c1_ref, u01_ref, l01_ref, every_ref, low1_ref, sem) = rest
    width = inv_ref.shape[1]
    per = width // LANES
    panel_copies(info_ref, chips, bufs, c0_ref, c1_ref, sem, start)
    panel_copies(info_ref, chips, bufs, c0_ref, c1_ref, sem, wait)
    z1c0 = get_block(c0_ref, 0, width, per, 0, per)
    g0c1 = get_block(c1_ref, 0, width, per, 0, per)
    low0, low1 = split(unit_lower(inv_ref[0])), split(unit_lower(inv_ref[1]))
    l01 = dot3(split(z1c0), split(upper(inv_ref[0])))
    l01_ref[...] = l01
    u01_ref[...] = dot3(low0, split(g0c1))
    back = split(dot3(low1, split(dot3(split(l01), low0))))
    for n, part in enumerate((low0[0], back[0], low0[1], back[1])):
        every_ref[n * width : (n + 1) * width] = part
    for n in range(2):
        low1_ref[n * width : (n + 1) * width] = low1[n]


def head(info, chips, bufs, inv):
    width = inv.shape[1]
    count = len(bufs) // (2 * chips)
    tab = jax.ShapeDtypeStruct((count * bufs[0].shape[0], LANES), F32)
    square = jax.ShapeDtypeStruct((width, width), F32)
    return pl.pallas_call(
        functools.partial(head_kernel, chips),
        in_specs=[SMEM] + [ANY] * len(bufs) + [VMEM],
        out_specs=[VMEM] * 6,
        out_shape=[
            tab,
            tab,
            square,
            square,
            jax.ShapeDtypeStruct((4 * width, width), BF16),
            jax.ShapeDtypeStruct((2 * width, width), BF16),
        ],
        scratch_shapes=[pltpu.SemaphoreType.DMA((2 * count,))],
        compiler_params=PARAMS,
        cost_estimate=cost(1 << 20),
        name="head",
    )(info, *bufs, inv)


def solve_kernel(
    groups, info_ref, owner_ref, rank_ref, a_ref, l01_ref, every_ref, low1_ref, uhl_ref, brow_ref, s_ref
):
    width = l01_ref.shape[0]
    per = width // LANES
    me, mc = info_ref[0], info_ref[1]

    def line_up(k, carry):
        spot = pl.ds(pl.multiple_of(k * groups, groups), groups)
        s_ref[spot, :] = a_ref[owner_ref[k], rank_ref[k]]
        return carry

    lax.fori_loop(0, 2 * width, line_up, 0, unroll=8)

    def solved(block):
        g0 = get_block(s_ref, 0, width, groups, block, per)
        z1 = get_block(s_ref, width, width, groups, block, per)
        g0s, z1s = split(g0), split(z1)
        first = jnp.dot(every_ref[...], g0s[0], preferred_element_type=F32)
        second = jnp.dot(every_ref[: 2 * width], g0s[1], preferred_element_type=F32)
        both = first[: 2 * width] + second + first[2 * width :]
        third = jnp.dot(low1_ref[...], z1s[0], preferred_element_type=F32)
        fourth = jnp.dot(low1_ref[:width], z1s[1], preferred_element_type=F32)
        u0 = both[:width]
        u1 = third[:width] + third[width:] + fourth - both[width:]
        cols = pl.ds(pl.multiple_of(block * width, width), width)
        for spot, value in ((pl.ds(0, width), u0), (pl.ds(width, width), u1)):
            high, low = split(value)
            uhl_ref[0, spot, cols] = high
            uhl_ref[1, spot, cols] = low
        return g0, z1, u0, u1

    def step(block, carry):
        _, _, u0, u1 = solved(block)
        put_block(brow_ref, 0, width, groups, block, per, jnp.where(me == 0, u0, u1))
        return carry

    lax.fori_loop(0, groups // per, step, 0)

    @pl.when((mc == 0) & (me == 0))
    def _():
        g0 = get_block(s_ref, 0, width, groups, 0, per)
        put_block(brow_ref, 0, width, groups, 0, per, g0)

    @pl.when((mc == 0) & (me == 1))
    def _():
        put_block(brow_ref, 0, width, groups, 0, per, l01_ref[...])

    @pl.when((mc == 1) & (me == 1))
    def _():
        z1 = get_block(s_ref, width, width, groups, 0, per)
        u0 = (uhl_ref[0, :width, :width], uhl_ref[1, :width, :width])
        a1 = z1 - dot3(split(l01_ref[...]), u0)
        put_block(brow_ref, 0, width, groups, 0, per, a1)


def solve(info, owner, rank, gathered, l01, every, low1s):
    groups = gathered.shape[2]
    width = l01.shape[0]
    cols = groups * LANES
    return pl.pallas_call(
        functools.partial(solve_kernel, groups),
        in_specs=[SMEM, SMEM, SMEM] + [VMEM] * 4,
        out_specs=[VMEM, VMEM],
        out_shape=[
            jax.ShapeDtypeStruct((2, 2 * width, cols), BF16),
            jax.ShapeDtypeStruct((width * groups, LANES), F32),
        ],
        scratch_shapes=[pltpu.VMEM((2 * width * groups, LANES), F32)],
        compiler_params=PARAMS,
        cost_estimate=cost(1 << 20),
        name="solve",
    )(info, owner, rank, gathered, l01, every, low1s)


def lower_kernel(
    chips, number, tile, info_ref, order_ref, spot_ref, first_ref, *rest
):
    bufs = rest[:number]
    t0_ref, t1_ref, inv_ref, u01_ref, stack_ref, c0_ref, c1_ref, sem = rest[number:]
    width = inv_ref.shape[1]
    per = width // LANES
    count = stack_ref.shape[0] // 2
    panel_copies(info_ref, chips, bufs, c0_ref, c1_ref, sem, start)
    panel_copies(info_ref, chips, bufs, c0_ref, c1_ref, sem, wait)

    def replace(n, carry):
        k = order_ref[n]
        here = pl.ds((spot_ref[k] - tile * count) * per, per)
        there = pl.ds((width + k) * per, per)
        c0_ref[here, :] = t0_ref[there, :]
        c1_ref[here, :] = t1_ref[there, :]
        return carry

    lax.fori_loop(first_ref[tile], first_ref[tile + 1], replace, 0)
    c0 = get_block(c0_ref, 0, count, per, 0, per)
    c1 = get_block(c1_ref, 0, count, per, 0, per)
    l0 = split(dot3(split(c0), split(upper(inv_ref[0]))))
    rest_ = c1 - dot3(l0, split(u01_ref[...]))
    l1 = split(dot3(split(rest_), split(upper(inv_ref[1]))))
    for part in range(2):
        stack_ref[part * count : (part + 1) * count, :width] = l0[part]
        stack_ref[part * count : (part + 1) * count, width:] = l1[part]


def lower(info, lists, chips, bufs, tabs, inv, u01, tile):
    width = inv.shape[1]
    pieces = len(bufs) // (2 * chips)
    count = pieces * bufs[0].shape[0] * LANES // width
    panels = pltpu.VMEM((pieces * bufs[0].shape[0], LANES), F32)
    return pl.pallas_call(
        functools.partial(lower_kernel, chips, len(bufs), tile),
        in_specs=[SMEM] * 4 + [ANY] * len(bufs) + [VMEM] * 4,
        out_specs=VMEM,
        out_shape=jax.ShapeDtypeStruct((2 * count, 2 * width), BF16),
        scratch_shapes=[panels, panels, pltpu.SemaphoreType.DMA((2 * pieces,))],
        compiler_params=PARAMS,
        cost_estimate=cost(1 << 20),
        name="lower",
    )(info, *lists, *bufs, *tabs, inv, u01)


def bulk_kernel(first, tiles, groups, width, info_ref, order_ref, spot_ref, first_ref, *rest):
    stacks, (m_ref, uhl_ref, f_ref, brow_ref) = rest[:tiles], rest[tiles : tiles + 4]
    o_ref, u_ref, moved_ref, row_ref, stack_ref, in_sem, out_sem, sem = rest[-8:]
    count = stack_ref.shape[1] // 2
    per = width // LANES
    mc = info_ref[1]
    u_copy = pltpu.make_async_copy(uhl_ref, u_ref, sem.at[0])
    f_copy = pltpu.make_async_copy(f_ref, moved_ref, sem.at[1])

    def span(n):
        return pl.ds((first + n) * count * groups, count * groups)

    def loads(n):
        slot = n % 2
        return (
            pltpu.make_async_copy(stacks[n], stack_ref.at[slot], in_sem.at[slot, 0]),
            pltpu.make_async_copy(m_ref.at[span(n)], row_ref.at[slot], in_sem.at[slot, 1]),
        )

    def store(n):
        return pltpu.make_async_copy(row_ref.at[n % 2], o_ref.at[span(n)], out_sem.at[n % 2])

    for copy in loads(0):
        copy.start()
    f_copy.start()
    u_copy.start()
    for n in range(tiles):
        slot = n % 2
        for copy in loads(n):
            copy.wait()
        if n == 0:
            f_copy.wait()
            u_copy.wait()
        if n + 1 < tiles:
            if n > 0:
                store(n - 1).wait()
            for copy in loads(n + 1):
                copy.start()
        rows, stack = row_ref.at[slot], stack_ref.at[slot]

        def replace(e, carry):
            k = order_ref[e]
            here = (spot_ref[k] - (first + n) * count) * groups
            rows[pl.ds(pl.multiple_of(here, groups), groups), :] = moved_ref[k]
            return carry

        lax.fori_loop(first_ref[first + n], first_ref[first + n + 1], replace, 0)

        def step(block, carry):
            cols = pl.ds(pl.multiple_of(block * width, width), width)
            both = jnp.dot(stack[...], u_ref[0, :, cols], preferred_element_type=F32)
            acc = jnp.dot(stack[:count], u_ref[1, :, cols], preferred_element_type=F32)
            new = get_block(rows, 0, count, groups, block, per) - (acc + both[:count] + both[count:])
            put_block(rows, 0, count, groups, block, per, new)
            return carry

        lax.fori_loop(0, groups // per, step, 0)
        for panel_at in range(2):

            @pl.when(mc == panel_at)
            def _():
                cols = slice(panel_at * width, (panel_at + 1) * width)
                own = stack[:count, cols].astype(F32) + stack[count:, cols].astype(F32)
                put_block(rows, 0, count, groups, 0, per, own)

        top = (first + n) * count
        if top < width:

            @pl.when(info_ref[0] < 2)
            def _():
                many = min(count, width - top) * groups
                copy = pltpu.make_async_copy(
                    brow_ref.at[pl.ds(top * groups, many)], rows.at[pl.ds(0, many)], sem.at[0]
                )
                copy.start()
                copy.wait()

        store(n).start()
    for n in range(max(0, tiles - 2), tiles):
        store(n).wait()


def bulk(info, lists, stacks, m2, uhl, moved, brow, out, first):
    tiles = len(stacks)
    groups = moved.shape[1]
    width = stacks[0].shape[1] // 2
    count = stacks[0].shape[0] // 2
    in_specs = [SMEM] * 4 + [ANY] * (tiles + 4)
    args = [info, *lists, *stacks, m2, uhl, moved, brow]
    aliases = {}
    if out is not None:
        in_specs.append(ANY)
        aliases = {len(args): 0}
        args.append(out)
    return pl.pallas_call(
        functools.partial(bulk_kernel, first, tiles, groups, width),
        in_specs=in_specs,
        out_specs=ANY,
        out_shape=jax.ShapeDtypeStruct(m2.shape, F32),
        scratch_shapes=[
            pltpu.VMEM(uhl.shape, BF16),
            pltpu.VMEM(moved.shape, F32),
            pltpu.VMEM((2, count * groups, LANES), F32),
            pltpu.VMEM((2,) + stacks[0].shape, BF16),
            pltpu.SemaphoreType.DMA((2, 2)),
            pltpu.SemaphoreType.DMA((2,)),
            pltpu.SemaphoreType.DMA((2,)),
        ],
        input_output_aliases=aliases,
        compiler_params=PARAMS,
        cost_estimate=cost(1 << 20),
        name="bulk",
    )(*args)


def fetch_kernel(procs, info_ref, *rest):
    ins = rest[:procs]
    o_ref, sem = rest[procs:]
    rows = o_ref.shape[0] // 2
    for act in (start, wait):
        for source in range(2):
            spot = pl.ds(source * rows, rows)
            for x in range(procs):

                @pl.when((info_ref[0] ^ source) == x)
                def _():
                    act(pltpu.make_async_copy(ins[x], o_ref.at[spot], sem.at[source]))


def fetch(info, displaced):
    rows, groups, _ = displaced[0].shape
    return pl.pallas_call(
        functools.partial(fetch_kernel, len(displaced)),
        in_specs=[SMEM] + [ANY] * len(displaced),
        out_specs=VMEM,
        out_shape=jax.ShapeDtypeStruct((2 * rows, groups, LANES), F32),
        scratch_shapes=[pltpu.SemaphoreType.DMA((2,))],
        compiler_params=PARAMS,
        cost_estimate=cost(1 << 20),
        name="fetch",
    )(info, *displaced)


def plan(pivots, width, procs, me):
    p0, p1 = pivots[0], pivots[1]
    count = jnp.arange(width, dtype=jnp.int32)
    hit = p0[:, None] == p1[None, :]
    back = p0[:, None] == width + count[None, :]
    src1 = jnp.where(hit.any(0), jnp.sum(jnp.where(hit, count[:, None], 0), 0), p1)
    dest0 = jnp.where(
        back.any(1),
        jnp.sum(jnp.where(back, p1[None, :], 0), 1),
        jnp.where(hit.any(1), -1, p0),
    )
    dest1 = jnp.where(back.any(0), -1, p1)
    src = jnp.concatenate([p0, src1])
    dest = jnp.concatenate([dest0, dest1])
    src_owner = src // width % procs
    src_local = src // width // procs * width + src % width
    dest_owner = jnp.where(dest >= 0, dest // width % procs, -1)
    dest_local = dest // width // procs * width + dest % width
    order = jnp.arange(2 * width, dtype=jnp.int32)
    earlier = order[None, :] < order[:, None]
    same_half = (order[None, :] // width) == (order[:, None] // width)
    src_rank = jnp.sum(
        (earlier & (src_owner[None, :] == src_owner[:, None])).astype(jnp.int32), 1
    )
    dest_rank = jnp.sum(
        (earlier & same_half & (dest_owner[None, :] == dest_owner[:, None])).astype(jnp.int32), 1
    )
    src_most = jnp.max(src_rank) + 1
    dest_most = jnp.max(jnp.where(dest >= 0, dest_rank, -1)) + 1
    return src_owner, src_local, src_rank, dest_owner, dest_local, dest_rank, src_most, dest_most


def flip(procs, x):
    return [(s, s ^ x) for s in range(procs)]


def send(value, axis, pairs):
    flat = value.reshape(-1, LANES)
    return lax.ppermute(flat, axis, pairs).reshape(value.shape)


def exchange(cap, fcap, m3, width, info, src, dest):
    per = width // LANES
    procs = lax.axis_size("prow")
    me = info[0]
    src_owner, src_local, src_rank = src
    dest_owner, dest_local, dest_rank = dest

    src_rank = jnp.minimum(src_rank, cap - 1)
    slots = jnp.arange(cap, dtype=jnp.int32)
    mine = (src_owner == me)[None, :] & (src_rank[None, :] == slots[:, None])
    row_list = jnp.max(jnp.where(mine, src_local[None, :], 0), 1)

    fslots = jnp.arange(fcap, dtype=jnp.int32)
    owner2 = dest_owner.reshape(2, width)
    rank2 = dest_rank.reshape(2, width)
    local2 = dest_local.reshape(2, width)
    to = me ^ jnp.arange(procs, dtype=jnp.int32)
    out_owner = jnp.where(me == 0, owner2[0], owner2[1])
    out_rank = jnp.where(me == 0, rank2[0], rank2[1])
    chosen = (out_owner[None, None, :] == to[:, None, None]) & (
        out_rank[None, None, :] == fslots[None, :, None]
    )
    out_list = jnp.sum(jnp.where(chosen, jnp.arange(width, dtype=jnp.int32), 0), 2)
    landing = (owner2[:, None, :] == me) & (rank2[:, None, :] == fslots[None, :, None])
    spots = (jnp.sum(jnp.where(landing, local2[:, None, :] + 1, 0), 2) - 1).reshape(2 * fcap)

    sent, outgoing, heads = collect(info, row_list, out_list, m3, per, width)
    heads = [heads[0]] + [send(heads[x], "prow", flip(procs, x)) for x in range(1, procs)]
    gathered = lax.all_gather(sent.reshape(-1, LANES), "prow", axis=0, tiled=True)
    gathered = gathered.reshape((procs,) + sent.shape)
    displaced = [outgoing[0]] + [
        send(outgoing[x], "prow", [(s, s ^ x) for s in range(2)]) for x in range(1, procs)
    ]
    return info, src_owner, src_rank, heads, gathered, displaced, spots


def exchange_any(m3, width, info, src, dest):
    per = width // LANES
    me = info[0]
    src_owner, src_local, _ = src
    dest_owner, dest_local, _ = dest
    rows = jnp.where((src_owner == me)[:, None, None], m3[src_local], 0.0)
    rows = lax.psum(rows.reshape(-1, LANES), "prow").reshape(rows.shape)
    displaced = []
    for source in range(2):
        top = jnp.where(me == source, m3[:width], 0.0)
        displaced.append(lax.psum(top.reshape(-1, LANES), "prow").reshape(top.shape))
    heads = [jnp.concatenate([rows[:, :per], top[:, :per]]) for top in displaced]
    spots = jnp.where(dest_owner == me, dest_local, -1)
    order = jnp.arange(2 * width, dtype=jnp.int32)
    first = jnp.concatenate([jnp.zeros((1,), jnp.int32), info[1:]])
    return first, jnp.zeros_like(order), order, heads, rows[None], displaced, spots


def factor(cap, fcap, m3, inv, info, first, src, dest, out=None):
    rows, groups, _ = m3.shape
    width = inv.shape[1]
    chips = lax.axis_size("pcol") // 2
    per = width // LANES
    z = info[2]
    m2 = m3.reshape(rows * groups, LANES)
    m4 = m3.reshape(rows, groups // per, per, LANES)
    chunk = rows // CHUNKS
    hop = [(q, q + 2) for q in range(2 * chips - 2)]
    swap = [(q, q ^ 1) for q in range(2 * chips)]
    pieces = list(first) + list(panel(m4, CHAINS, CHUNKS - CHAINS, chunk))

    if cap is None:
        cap, fcap, moves = 2 * width, width, exchange_any(m3, width, info, src, dest)
    else:
        moves = exchange(cap, fcap, m3, width, info, src, dest)
    seen, owner, rank, heads, gathered, displaced, spots = moves
    share = -(-(width + 2 * fcap) // (chunk * CHAINS))
    table = tables(seen, owner, rank, heads, cap, width, share * CHAINS * chunk)

    tiles = CHUNKS // CHAINS
    tile_of = jnp.where(spots < 0, tiles, spots // (CHAINS * chunk))
    place = jnp.arange(spots.shape[0], dtype=jnp.int32)
    before = (tile_of[None, :] < tile_of[:, None]) | (
        (tile_of[None, :] == tile_of[:, None]) & (place[None, :] < place[:, None])
    )
    at = jnp.sum(before.astype(jnp.int32), 1)
    order = jnp.sum(jnp.where(at[None, :] == place[:, None], place[None, :], 0), 1)
    starts = jnp.sum(
        (tile_of[None, :] < jnp.arange(tiles + 1, dtype=jnp.int32)[:, None]).astype(jnp.int32), 1
    )
    lists = (order, spots, starts)

    items = [piece.reshape(chunk * per, LANES) for piece in pieces]
    table = table.reshape(share * CHAINS, chunk * per, LANES)
    at = TABLE_AT * CHAINS
    items[at:at] = [table[n] for n in range(share * CHAINS)]
    length = len(items) // CHAINS
    position = [n if n < TABLE_AT else n + share for n in range(tiles)]
    own = [[] for _ in range(CHAINS)]
    sib = [[] for _ in range(CHAINS)]

    def held(t, count=1):
        bufs = []
        for n in range(t, t + count):
            for k in range(CHAINS):
                bufs += own[k][n : n + chips] + sib[k][n : n + chips]
        return bufs

    heads_of = uhl = brow = moved = None
    stacks, done = [], 0

    def work(t):
        nonlocal heads_of, uhl, brow, moved, done, out
        last = t >= length + chips - 1
        fresh = []
        if t == TABLE_AT + share + chips:
            heads_of = head(info, chips, held(TABLE_AT, share), inv)
            moved = fetch(seen, displaced)
            fresh += [heads_of[0], moved]
        if heads_of is not None:
            t0, t1, u01, l01, every, low1s = heads_of
            while len(stacks) < tiles and (last or position[len(stacks)] + chips < t):
                n = len(stacks)
                bufs = held(position[n])
                stacks.append(lower(info, lists, chips, bufs, (t0, t1), inv, u01, n))
                fresh.append(stacks[-1])
                if len(stacks) % 2 == 0 and not last:
                    break
        if uhl is None and heads_of is not None and (last or t == TABLE_AT + share + chips + SOLVE_AFTER):
            uhl, brow = solve(info, owner, rank, gathered, l01, every, low1s)
            fresh.append(brow)
        elif uhl is not None:
            while done < len(stacks) and (last or done + 2 <= len(stacks)):
                many = 2 if done + 4 <= tiles else 1
                out = bulk(info, lists, stacks[done : done + many], m2, uhl, moved, brow, out, done)
                done += many
                fresh.append(out)
                if not last:
                    break
        return fresh

    if out is not None:
        out = out.reshape(m2.shape)
    for t in range(length + chips - 1):
        fresh = work(t)
        if fresh:
            tied = lax.optimization_barrier(tuple(own[k][-1] for k in range(CHAINS)) + tuple(fresh))
            ends = tied[:CHAINS]
        else:
            ends = [own[k][-1] if t else None for k in range(CHAINS)]
        for k in range(CHAINS):
            cur = items[t * CHAINS + k] if t < length else None
            if t > 0:
                came = send(ends[k], "pcol", hop)
                cur = came if cur is None else jnp.where(z == 0, cur, came)
            own[k].append(cur)
            sib[k].append(send(cur, "pcol", swap))
    work(length + chips - 1)
    work(length + chips)
    return out.reshape(rows, groups, LANES)


def shards(matrix, pivots, inverse_blocks):
    row_blocks, _, width, blocks, _, _ = matrix.shape
    procs = lax.axis_size("prow")
    me = lax.axis_index("prow").astype(jnp.int32)
    mc = lax.axis_index("pcol").astype(jnp.int32)
    info = jnp.stack([me, mc, mc // 2, mc % 2])
    m3 = matrix.reshape(row_blocks * width, -1, LANES)
    m4 = matrix.reshape(row_blocks * width, blocks, -1, LANES)
    first = panel(m4, 0, CHAINS, row_blocks * width // CHUNKS)
    pivots, first = lax.optimization_barrier((pivots, first))
    so, sl, sr, do, dl, dr, src_most, dest_most = plan(pivots, width, procs, me)
    mean = 2 * width // procs
    cap = min(2 * width, (mean + 3 * mean // 8 + 7) // 8 * 8)
    fmean = width // procs
    fcap = min(width, (fmean + fmean // 2 + 7) // 8 * 8)
    again = (src_most > cap) | (dest_most > fcap)
    args = (m3, inverse_blocks, info, tuple(first), (so, sl, sr), (do, dl, dr))
    out = factor(cap, fcap, *args)

    out = lax.cond(
        again,
        lambda done, *rest: factor(None, None, *rest, done),
        lambda done, *rest: done,
        out,
        *args,
    )
    return out.reshape(matrix.shape)


def solution(mesh):
    return jax.shard_map(
        shards,
        mesh=mesh,
        in_specs=(P(None, "prow", None, None, "pcol", None), P(), P()),
        out_specs=P(None, "prow", None, None, "pcol", None),
        check_vma=False,
    )
```

```python
import functools

import jax
import jax.numpy as jnp
from jax import lax
from jax.experimental import pallas as pl
from jax.experimental.pallas import tpu as pltpu
from jax.sharding import PartitionSpec as P

LANES = 128
CHUNKS = 16
CHAINS = 2
TABLE_AT = 2
TILE = 256
F32 = jnp.float32
BF16 = jnp.bfloat16
ANY = pl.BlockSpec(memory_space=pl.ANY)
VMEM = pl.BlockSpec(memory_space=pltpu.VMEM)
SMEM = pl.BlockSpec(memory_space=pltpu.SMEM)
PARAMS = pltpu.CompilerParams(vmem_limit_bytes=56 << 20)


def cost(nbytes):
    return pl.CostEstimate(flops=0, bytes_accessed=int(nbytes), transcendentals=0)


def split(x):
    high = x.astype(BF16)
    return high, (x - high.astype(F32)).astype(BF16)


def dot3(left, right):
    out = jnp.dot(left[0], right[0], preferred_element_type=F32)
    out += jnp.dot(left[0], right[1], preferred_element_type=F32)
    return out + jnp.dot(left[1], right[0], preferred_element_type=F32)


def upper(packed):
    row = lax.broadcasted_iota(jnp.int32, packed.shape, 0)
    col = lax.broadcasted_iota(jnp.int32, packed.shape, 1)
    return jnp.where(col >= row, packed, 0.0)


def unit_lower(packed):
    row = lax.broadcasted_iota(jnp.int32, packed.shape, 0)
    col = lax.broadcasted_iota(jnp.int32, packed.shape, 1)
    return jnp.where(col < row, packed, jnp.where(col == row, 1.0, 0.0))


def get_block(ref, start, count, groups, block, per):
    parts = [
        ref[pl.ds(start * groups + block * per + h, count, stride=groups), :] for h in range(per)
    ]
    return jnp.concatenate(parts, axis=1)


def put_block(ref, start, count, groups, block, per, value):
    for h in range(per):
        ref[pl.ds(start * groups + block * per + h, count, stride=groups), :] = value[
            :, h * LANES : (h + 1) * LANES
        ]


def panel_copies(info_ref, chips, bufs, c0_ref, c1_ref, sem, act):
    rows = bufs[0].shape[0]
    for h in range(chips):
        for core in range(2):

            @pl.when((info_ref[2] == h) & (info_ref[3] == core))
            def _():
                for n in range(len(bufs) // (2 * chips)):
                    own, sib = bufs[2 * n * chips + h], bufs[(2 * n + 1) * chips + h]
                    first, second = (own, sib) if core == 0 else (sib, own)
                    spot = pl.ds(n * rows, rows)
                    act(pltpu.make_async_copy(first, c0_ref.at[spot], sem.at[2 * n]))
                    act(pltpu.make_async_copy(second, c1_ref.at[spot], sem.at[2 * n + 1]))


def start(copy):
    copy.start()


def wait(copy):
    copy.wait()


def panel(m4, first, count, rows):
    shape = (rows,) + m4.shape[2:]

    def kernel(m_ref, *rest):
        outs, sem = rest[:count], rest[count]
        copies = [
            pltpu.make_async_copy(m_ref.at[pl.ds((first + k) * rows, rows), 0], outs[k], sem.at[k])
            for k in range(count)
        ]
        for copy in copies:
            copy.start()
        for copy in copies:
            copy.wait()

    return pl.pallas_call(
        kernel,
        in_specs=[ANY],
        out_specs=[VMEM] * count,
        out_shape=[jax.ShapeDtypeStruct(shape, F32)] * count,
        scratch_shapes=[pltpu.SemaphoreType.DMA((count,))],
        compiler_params=PARAMS,
        cost_estimate=cost(1 << 18),
        name="panel",
    )(m4)


def collect_kernel(procs, per, info_ref, list_ref, out_list_ref, m_ref, *rest):
    a_ref, b_ref = rest[:2]
    out_refs, head_refs = rest[2 : 2 + procs], rest[2 + procs : 2 + 2 * procs]
    row_ref, top_ref, sem = rest[2 + 2 * procs :]
    cap, groups, _ = row_ref.shape
    width = top_ref.shape[0]
    fcap = out_refs[0].shape[0]
    top = pltpu.make_async_copy(m_ref.at[pl.ds(0, width)], top_ref, sem.at[0])
    top.start()

    def fetch(k, carry):
        pltpu.make_async_copy(m_ref.at[list_ref[k]], row_ref.at[k], sem.at[1]).start()
        return carry

    lax.fori_loop(0, cap, fetch, 0)
    top.wait()

    @pl.when(info_ref[0] < 2)
    def _():
        for x in range(procs):

            def give(k, carry):
                row = top_ref[out_list_ref[x, k]]
                out_refs[x][k] = row
                head_refs[x][cap + k] = row[0:per]
                return carry

            lax.fori_loop(0, fcap, give, 0, unroll=4)

    pltpu.make_async_copy(row_ref, row_ref, sem.at[1]).wait()

    def keep(k, carry):
        row = row_ref[k]
        a_ref[k] = row[: groups // 2]
        b_ref[k] = row[groups // 2 :]
        for x in range(procs):
            head_refs[x][k] = row[0:per]
        return carry

    lax.fori_loop(0, cap, keep, 0, unroll=2)


def collect(info, row_list, out_list, m3, per, width):
    cap = row_list.shape[0]
    procs, fcap = out_list.shape
    groups = m3.shape[1]
    half = jax.ShapeDtypeStruct((cap, groups // 2, LANES), F32)
    out = jax.ShapeDtypeStruct((fcap, groups, LANES), F32)
    head = jax.ShapeDtypeStruct((cap + fcap, per, LANES), F32)
    outs = pl.pallas_call(
        functools.partial(collect_kernel, procs, per),
        in_specs=[SMEM, SMEM, SMEM, ANY],
        out_specs=[VMEM] * (2 + 2 * procs),
        out_shape=[half, half] + [out] * procs + [head] * procs,
        scratch_shapes=[
            pltpu.VMEM((cap, groups, LANES), F32),
            pltpu.VMEM((width, groups, LANES), F32),
            pltpu.SemaphoreType.DMA((2,)),
        ],
        compiler_params=PARAMS,
        cost_estimate=cost(1 << 18),
        name="collect",
    )(info, row_list, out_list, m3)
    return outs[:2], outs[2 : 2 + procs], outs[2 + procs :]


def tables_kernel(procs, cap, width, info_ref, owner_ref, rank_ref, *rest):
    ins = rest[:procs]
    o_ref, buf_ref, sem = rest[procs:]
    fcap = buf_ref.shape[1] - cap
    copies = [
        pltpu.make_async_copy(ins[x], buf_ref.at[info_ref[0] ^ x], sem.at[x]) for x in range(procs)
    ]
    for copy in copies:
        copy.start()
    for copy in copies:
        copy.wait()
    base = jnp.where(info_ref[3] == 0, width, 0)

    def pivot(k, carry):
        o_ref[k] = buf_ref[owner_ref[base + k], rank_ref[base + k]]
        return carry

    lax.fori_loop(0, width, pivot, 0, unroll=4)
    for source in range(2):

        def other(k, carry):
            o_ref[width + source * fcap + k] = buf_ref[source, cap + k]
            return carry

        lax.fori_loop(0, fcap, other, 0, unroll=4)


def tables(info, owner, rank, heads, cap, width, rows):
    procs = len(heads)
    both, per, _ = heads[0].shape
    return pl.pallas_call(
        functools.partial(tables_kernel, procs, cap, width),
        in_specs=[SMEM, SMEM, SMEM] + [ANY] * procs,
        out_specs=VMEM,
        out_shape=jax.ShapeDtypeStruct((rows, per, LANES), F32),
        scratch_shapes=[
            pltpu.VMEM((procs, both, per, LANES), F32),
            pltpu.SemaphoreType.DMA((procs,)),
        ],
        compiler_params=PARAMS,
        cost_estimate=cost(1 << 18),
        name="tables",
    )(info, owner, rank, *heads)


def head_kernel(chips, info_ref, *rest):
    (*bufs, inv_ref, c0_ref, c1_ref, l01_ref, own_ref, w_ref, left_ref, sem) = rest
    width = inv_ref.shape[1]
    per = width // LANES
    me, mc = info_ref[0], info_ref[1]
    panel_copies(info_ref, chips, bufs, c0_ref, c1_ref, sem, start)
    panel_copies(info_ref, chips, bufs, c0_ref, c1_ref, sem, wait)
    z1c0 = get_block(c0_ref, 0, width, per, 0, per)
    g0c1 = get_block(c1_ref, 0, width, per, 0, per)
    one0, one1 = unit_lower(inv_ref[0]), unit_lower(inv_ref[1])
    up0, up1 = upper(inv_ref[0]), upper(inv_ref[1])
    low0, low1, v0, v1 = split(one0), split(one1), split(up0), split(up1)
    l01 = dot3(split(z1c0), v0)
    l01_ref[...] = l01
    u01 = dot3(low0, split(g0c1))
    back = dot3(low1, split(dot3(split(l01), low0)))
    cross = dot3(v0, split(u01))
    crosses = split(cross)
    parts = (
        split(dot3(v0, low0)),
        split(dot3(v1, split(back))),
        split(dot3(v1, low1)),
        crosses,
    )
    for n, part in enumerate(parts):
        for k in range(2):
            w_ref[(2 * n + k) * width : (2 * n + k + 1) * width] = part[k]
    mine = (split(jnp.where(me == 0, one0, -back)), split(jnp.where(me == 0, 0.0, one1)))
    for n, part in enumerate(mine):
        for k in range(2):
            own_ref[(2 * n + k) * width : (2 * n + k + 1) * width] = part[k]
    left_ref[:width] = jnp.where(mc == 0, -up0, dot3(crosses, v1))
    left_ref[width:] = jnp.where(mc == 0, 0.0, -up1)


def head(info, chips, bufs, inv):
    width = inv.shape[1]
    count = len(bufs) // (2 * chips)
    tab = jax.ShapeDtypeStruct((count * bufs[0].shape[0], LANES), F32)
    return pl.pallas_call(
        functools.partial(head_kernel, chips),
        in_specs=[SMEM] + [ANY] * len(bufs) + [VMEM],
        out_specs=[VMEM] * 6,
        out_shape=[
            tab,
            tab,
            jax.ShapeDtypeStruct((width, width), F32),
            jax.ShapeDtypeStruct((4 * width, width), BF16),
            jax.ShapeDtypeStruct((8 * width, width), BF16),
            jax.ShapeDtypeStruct((2 * width, width), F32),
        ],
        scratch_shapes=[pltpu.SemaphoreType.DMA((2 * count,))],
        compiler_params=PARAMS,
        cost_estimate=cost(1 << 20),
        name="head",
    )(info, *bufs, inv)


def triple(value):
    high, low = split(value)
    return high, high, low


def solve_kernel(procs, order_a, order_b, groups, info_ref, owner_ref, rank_ref, *rest):
    a_ins, b_ins = rest[:procs], rest[procs : 2 * procs]
    l01_ref, own_ref, w_ref, left_ref, inv_ref, u3_ref, brow_ref, a_ref, b_ref, s_ref, sem = rest[2 * procs :]
    width = l01_ref.shape[0]
    per = width // LANES
    seen, mc, me = info_ref[0], info_ref[1], info_ref[4]
    copies = []
    for n in range(procs):
        copies.append(pltpu.make_async_copy(a_ins[n], a_ref.at[seen ^ order_a[n]], sem.at[n]))
        copies.append(
            pltpu.make_async_copy(b_ins[n], b_ref.at[seen ^ order_b[n]], sem.at[procs + n])
        )
    for copy in copies:
        copy.start()
    for copy in copies:
        copy.wait()

    def line_up(k, carry):
        owner, rank = owner_ref[k], rank_ref[k]
        half = groups // 2
        s_ref[pl.ds(pl.multiple_of(k * groups, half), half), :] = a_ref[owner, rank]
        s_ref[pl.ds(pl.multiple_of(k * groups + half, half), half), :] = b_ref[owner, rank]
        return carry

    lax.fori_loop(0, 2 * width, line_up, 0, unroll=8)

    def pair(ref, n):
        return ref[2 * n * width : (2 * n + 1) * width], ref[(2 * n + 1) * width : (2 * n + 2) * width]

    def keep(block, value, first):
        for n, part in enumerate(triple(value)):
            at = 2 * n * width + first
            u3_ref[at : at + width, block * width : (block + 1) * width] = part

    for block in range(groups // per):
        g0 = split(get_block(s_ref, 0, width, groups, block, per))
        z1 = split(get_block(s_ref, width, width, groups, block, per))
        w1 = dot3(pair(w_ref, 2), z1) - dot3(pair(w_ref, 1), g0)
        w0 = dot3(pair(w_ref, 0), g0) - dot3(pair(w_ref, 3), split(w1))
        if block == 0:
            w0 = jnp.where(mc < 2, left_ref[:width], w0)
            w1 = jnp.where(mc < 2, left_ref[width:], w1)
        keep(block, w0, 0)
        keep(block, w1, width)

    @pl.when(me < 2)
    def _():
        def step(block, carry):
            g0 = split(get_block(s_ref, 0, width, groups, block, per))
            z1 = split(get_block(s_ref, width, width, groups, block, per))
            u = dot3(pair(own_ref, 0), g0) + dot3(pair(own_ref, 1), z1)
            put_block(brow_ref, 0, width, groups, block, per, u)
            return carry

        lax.fori_loop(0, groups // per, step, 0)

    @pl.when((mc == 0) & (me == 0))
    def _():
        put_block(brow_ref, 0, width, groups, 0, per, get_block(s_ref, 0, width, groups, 0, per))

    @pl.when((mc == 0) & (me == 1))
    def _():
        put_block(brow_ref, 0, width, groups, 0, per, l01_ref[...])

    @pl.when((mc == 1) & (me == 1))
    def _():
        g0 = split(get_block(s_ref, 0, width, groups, 0, per))
        z1 = get_block(s_ref, width, width, groups, 0, per)
        u0 = split(dot3(split(unit_lower(inv_ref[0])), g0))
        put_block(brow_ref, 0, width, groups, 0, per, z1 - dot3(split(l01_ref[...]), u0))


def solve(info, owner, rank, gathered, l01, own, w, left, inv):
    (a_bufs, order_a), (b_bufs, order_b) = gathered
    procs = len(a_bufs)
    cap, half, _ = a_bufs[0].shape
    groups = 2 * half
    width = l01.shape[0]
    cols = groups * LANES
    part = pltpu.VMEM((procs, cap, half, LANES), F32)
    return pl.pallas_call(
        functools.partial(solve_kernel, procs, order_a, order_b, groups),
        in_specs=[SMEM, SMEM, SMEM] + [ANY] * (2 * procs) + [VMEM] * 5,
        out_specs=[VMEM, VMEM],
        out_shape=[
            jax.ShapeDtypeStruct((6 * width, cols), BF16),
            jax.ShapeDtypeStruct((width * groups, LANES), F32),
        ],
        scratch_shapes=[
            part,
            part,
            pltpu.VMEM((2 * width * groups, LANES), F32),
            pltpu.SemaphoreType.DMA((2 * procs,)),
        ],
        compiler_params=PARAMS,
        cost_estimate=cost(1 << 20),
        name="solve",
    )(info, owner, rank, *a_bufs, *b_bufs, l01, own, w, left, inv)


def make_bulk(chips, first, tiles, number, groups, width):
    def kernel(info_ref, order_ref, spot_ref, first_ref, *rest):
        bufs = rest[:number]
        m_ref, u3_ref, f_ref, brow_ref, t0_ref, t1_ref = rest[number : number + 6]
        o_ref, u_ref, moved_ref, row_ref, c0_ref, c1_ref, left_ref = rest[-11:-4]
        c_sem, in_sem, out_sem, sem = rest[-4:]
        each = number // tiles
        count = left_ref.shape[0]
        per = width // LANES
        mc = info_ref[1]
        half = min(TILE, count)
        u_copy = pltpu.make_async_copy(u3_ref, u_ref, sem.at[0])
        f_copy = pltpu.make_async_copy(f_ref, moved_ref, sem.at[1])

        def span(n):
            return pl.ds((first + n) * count * groups, count * groups)

        def panels(n, act):
            slot = n % 2
            panel_copies(
                info_ref, chips, bufs[n * each : (n + 1) * each], c0_ref.at[slot], c1_ref.at[slot],
                c_sem.at[slot], act,
            )

        def rows_in(n):
            return pltpu.make_async_copy(m_ref.at[span(n)], row_ref.at[n % 2], in_sem.at[n % 2])

        def store(n):
            return pltpu.make_async_copy(row_ref.at[n % 2], o_ref.at[span(n)], out_sem.at[n % 2])

        panels(0, start)
        f_copy.start()
        u_copy.start()
        rows_in(0).start()
        for n in range(tiles):
            slot = n % 2
            rows, c0, c1 = row_ref.at[slot], c0_ref.at[slot], c1_ref.at[slot]
            panels(n, wait)
            if n == 0:
                f_copy.wait()
            if n + 1 < tiles:
                panels(n + 1, start)

            def replace(e, carry):
                k = order_ref[e]
                here = pl.ds((spot_ref[k] - (first + n) * count) * per, per)
                there = pl.ds((width + k) * per, per)
                c0[here, :] = t0_ref[there, :]
                c1[here, :] = t1_ref[there, :]
                return carry

            lax.fori_loop(first_ref[first + n], first_ref[first + n + 1], replace, 0)
            for k, c in enumerate((c0, c1)):
                for part, value in enumerate(split(get_block(c, 0, count, per, 0, per))):
                    left_ref[:, (2 * part + k) * width : (2 * part + k + 1) * width] = value
                    if part == 0:
                        left_ref[:, (4 + k) * width : (5 + k) * width] = value
            rows_in(n).wait()

            def replace_row(e, carry):
                k = order_ref[e]
                here = (spot_ref[k] - (first + n) * count) * groups
                rows[pl.ds(pl.multiple_of(here, groups), groups), :] = moved_ref[k]
                return carry

            lax.fori_loop(first_ref[first + n], first_ref[first + n + 1], replace_row, 0)
            if n == 0:
                u_copy.wait()
            else:
                store(n - 1).wait()
            if n + 1 < tiles:
                rows_in(n + 1).start()

            def step(m, carry):
                left = left_ref[pl.ds(pl.multiple_of(m * half, half), half), :]
                for block in range(groups // per):
                    cols = slice(block * width, (block + 1) * width)
                    acc = jnp.dot(left, u_ref[:, cols], preferred_element_type=F32)
                    old = get_block(rows, m * half, half, groups, block, per)
                    if block == 0:
                        old = jnp.where(mc < 2, 0.0, old)
                    put_block(rows, m * half, half, groups, block, per, old - acc)
                return carry

            lax.fori_loop(0, count // half, step, 0)
            top = (first + n) * count
            if top < width:

                @pl.when(info_ref[0] < 2)
                def _():
                    many = min(count, width - top) * groups
                    copy = pltpu.make_async_copy(
                        brow_ref.at[pl.ds(top * groups, many)], rows.at[pl.ds(0, many)], sem.at[0]
                    )
                    copy.start()
                    copy.wait()

            store(n).start()
        store(tiles - 1).wait()

    return kernel


def bulk(info, lists, chips, bufs, tabs, m2, u3, moved, brow, out, first, tiles):
    groups = moved.shape[1]
    width = u3.shape[0] // 6
    per = width // LANES
    pieces = len(bufs) // (2 * chips * tiles)
    count = pieces * bufs[0].shape[0] // per
    in_specs = [SMEM] * 4 + [ANY] * (len(bufs) + 4) + [VMEM] * 2
    args = [info, *lists, *bufs, m2, u3, moved, brow, *tabs]
    aliases = {}
    if out is not None:
        in_specs.append(ANY)
        aliases = {len(args): 0}
        args.append(out)
    panels = pltpu.VMEM((2, count * per, LANES), F32)
    return pl.pallas_call(
        make_bulk(chips, first, tiles, len(bufs), groups, width),
        in_specs=in_specs,
        out_specs=ANY,
        out_shape=jax.ShapeDtypeStruct(m2.shape, F32),
        scratch_shapes=[
            pltpu.VMEM(u3.shape, BF16),
            pltpu.VMEM(moved.shape, F32),
            pltpu.VMEM((2, count * groups, LANES), F32),
            panels,
            panels,
            pltpu.VMEM((count, 6 * width), BF16),
            pltpu.SemaphoreType.DMA((2, 2 * pieces)),
            pltpu.SemaphoreType.DMA((2,)),
            pltpu.SemaphoreType.DMA((2,)),
            pltpu.SemaphoreType.DMA((2,)),
        ],
        input_output_aliases=aliases,
        compiler_params=PARAMS,
        cost_estimate=cost(1 << 20),
        name="bulk",
    )(*args)


def fetch_kernel(procs, info_ref, *rest):
    ins = rest[:procs]
    o_ref, sem = rest[procs:]
    rows = o_ref.shape[0] // 2
    for act in (start, wait):
        for source in range(2):
            spot = pl.ds(source * rows, rows)
            for x in range(procs):

                @pl.when((info_ref[0] ^ source) == x)
                def _():
                    act(pltpu.make_async_copy(ins[x], o_ref.at[spot], sem.at[source]))


def fetch(info, displaced):
    rows, groups, _ = displaced[0].shape
    return pl.pallas_call(
        functools.partial(fetch_kernel, len(displaced)),
        in_specs=[SMEM] + [ANY] * len(displaced),
        out_specs=VMEM,
        out_shape=jax.ShapeDtypeStruct((2 * rows, groups, LANES), F32),
        scratch_shapes=[pltpu.SemaphoreType.DMA((2,))],
        compiler_params=PARAMS,
        cost_estimate=cost(1 << 20),
        name="fetch",
    )(info, *displaced)


def plan(pivots, width, procs, me):
    p0, p1 = pivots[0], pivots[1]
    count = jnp.arange(width, dtype=jnp.int32)
    hit = p0[:, None] == p1[None, :]
    back = p0[:, None] == width + count[None, :]
    src1 = jnp.where(hit.any(0), jnp.sum(jnp.where(hit, count[:, None], 0), 0), p1)
    dest0 = jnp.where(
        back.any(1),
        jnp.sum(jnp.where(back, p1[None, :], 0), 1),
        jnp.where(hit.any(1), -1, p0),
    )
    dest1 = jnp.where(back.any(0), -1, p1)
    src = jnp.concatenate([p0, src1])
    dest = jnp.concatenate([dest0, dest1])
    src_owner = src // width % procs
    src_local = src // width // procs * width + src % width
    dest_owner = jnp.where(dest >= 0, dest // width % procs, -1)
    dest_local = dest // width // procs * width + dest % width
    order = jnp.arange(2 * width, dtype=jnp.int32)
    earlier = order[None, :] < order[:, None]
    same_half = (order[None, :] // width) == (order[:, None] // width)
    src_rank = jnp.sum(
        (earlier & (src_owner[None, :] == src_owner[:, None])).astype(jnp.int32), 1
    )
    dest_rank = jnp.sum(
        (earlier & same_half & (dest_owner[None, :] == dest_owner[:, None])).astype(jnp.int32), 1
    )
    src_most = jnp.max(src_rank) + 1
    dest_most = jnp.max(jnp.where(dest >= 0, dest_rank, -1)) + 1
    return src_owner, src_local, src_rank, dest_owner, dest_local, dest_rank, src_most, dest_most


def flip(procs, x):
    return [(s, s ^ x) for s in range(procs)]


def send(value, axis, pairs):
    flat = value.reshape(-1, LANES)
    return lax.ppermute(flat, axis, pairs).reshape(value.shape)


def exchange(cap, fcap, m3, width, info, src, dest):
    per = width // LANES
    procs = lax.axis_size("prow")
    me = info[0]
    src_owner, src_local, src_rank = src
    dest_owner, dest_local, dest_rank = dest

    src_rank = jnp.minimum(src_rank, cap - 1)
    slots = jnp.arange(cap, dtype=jnp.int32)
    mine = (src_owner == me)[None, :] & (src_rank[None, :] == slots[:, None])
    row_list = jnp.max(jnp.where(mine, src_local[None, :], 0), 1)

    fslots = jnp.arange(fcap, dtype=jnp.int32)
    owner2 = dest_owner.reshape(2, width)
    rank2 = dest_rank.reshape(2, width)
    local2 = dest_local.reshape(2, width)
    to = me ^ jnp.arange(procs, dtype=jnp.int32)
    out_owner = jnp.where(me == 0, owner2[0], owner2[1])
    out_rank = jnp.where(me == 0, rank2[0], rank2[1])
    chosen = (out_owner[None, None, :] == to[:, None, None]) & (
        out_rank[None, None, :] == fslots[None, :, None]
    )
    out_list = jnp.sum(jnp.where(chosen, jnp.arange(width, dtype=jnp.int32), 0), 2)
    landing = (owner2[:, None, :] == me) & (rank2[:, None, :] == fslots[None, :, None])
    spots = (jnp.sum(jnp.where(landing, local2[:, None, :] + 1, 0), 2) - 1).reshape(2 * fcap)

    halves, outgoing, heads = collect(info, row_list, out_list, m3, per, width)
    heads = [heads[0]] + [send(heads[x], "prow", flip(procs, x)) for x in range(1, procs)]
    bits = [1 << b for b in range(procs.bit_length() - 1)]
    turned = bits[len(bits) // 2 :] + bits[: len(bits) // 2]
    gathered = []
    for half, order in zip(halves, (bits, turned)):
        bufs, kinds = [half], [0]
        for bit in order:
            bufs = bufs + [send(buf, "prow", flip(procs, bit)) for buf in bufs]
            kinds = kinds + [kind ^ bit for kind in kinds]
        gathered.append((bufs, tuple(kinds)))
    displaced = [outgoing[0]] + [
        send(outgoing[x], "prow", [(s, s ^ x) for s in range(2)]) for x in range(1, procs)
    ]
    return info, src_owner, src_rank, heads, gathered, displaced, spots


def exchange_any(m3, width, info, src, dest):
    per = width // LANES
    me = info[0]
    src_owner, src_local, _ = src
    dest_owner, dest_local, _ = dest
    rows = jnp.where((src_owner == me)[:, None, None], m3[src_local], 0.0)
    rows = lax.psum(rows.reshape(-1, LANES), "prow").reshape(rows.shape)
    displaced = []
    for source in range(2):
        top = jnp.where(me == source, m3[:width], 0.0)
        displaced.append(lax.psum(top.reshape(-1, LANES), "prow").reshape(top.shape))
    heads = [jnp.concatenate([rows[:, :per], top[:, :per]]) for top in displaced]
    spots = jnp.where(dest_owner == me, dest_local, -1)
    order = jnp.arange(2 * width, dtype=jnp.int32)
    first = jnp.concatenate([jnp.zeros((1,), jnp.int32), info[1:]])
    half = m3.shape[1] // 2
    gathered = [([rows[:, :half]], (0,)), ([rows[:, half:]], (0,))]
    return first, jnp.zeros_like(order), order, heads, gathered, displaced, spots


def factor(cap, fcap, m3, inv, info, first, src, dest, out=None):
    rows, groups, _ = m3.shape
    width = inv.shape[1]
    chips = lax.axis_size("pcol") // 2
    per = width // LANES
    z = info[2]
    m2 = m3.reshape(rows * groups, LANES)
    m4 = m3.reshape(rows, groups // per, per, LANES)
    chunk = rows // CHUNKS
    hop = [(q, q + 2) for q in range(2 * chips - 2)]
    swap = [(q, q ^ 1) for q in range(2 * chips)]
    pieces = list(first) + list(panel(m4, CHAINS, CHUNKS - CHAINS, chunk))

    if cap is None:
        cap, fcap, moves = 2 * width, width, exchange_any(m3, width, info, src, dest)
    else:
        moves = exchange(cap, fcap, m3, width, info, src, dest)
    seen, owner, rank, heads, gathered, displaced, spots = moves
    share = -(-(width + 2 * fcap) // (chunk * CHAINS))
    table = tables(seen, owner, rank, heads, cap, width, share * CHAINS * chunk)

    tiles = CHUNKS // CHAINS
    tile_of = jnp.where(spots < 0, tiles, spots // (CHAINS * chunk))
    place = jnp.arange(spots.shape[0], dtype=jnp.int32)
    before = (tile_of[None, :] < tile_of[:, None]) | (
        (tile_of[None, :] == tile_of[:, None]) & (place[None, :] < place[:, None])
    )
    at = jnp.sum(before.astype(jnp.int32), 1)
    order = jnp.sum(jnp.where(at[None, :] == place[:, None], place[None, :], 0), 1)
    starts = jnp.sum(
        (tile_of[None, :] < jnp.arange(tiles + 1, dtype=jnp.int32)[:, None]).astype(jnp.int32), 1
    )
    lists = (order, spots, starts)

    items = [piece.reshape(chunk * per, LANES) for piece in pieces]
    table = table.reshape(share * CHAINS, chunk * per, LANES)
    at = TABLE_AT * CHAINS
    items[at:at] = [table[n] for n in range(share * CHAINS)]
    length = len(items) // CHAINS
    position = [n if n < TABLE_AT else n + share for n in range(tiles)]
    own = [[] for _ in range(CHAINS)]
    sib = [[] for _ in range(CHAINS)]

    def held(t, count=1):
        bufs = []
        for n in range(t, t + count):
            for k in range(CHAINS):
                bufs += own[k][n : n + chips] + sib[k][n : n + chips]
        return bufs

    known = solved = moved = None
    done = 0

    def update(many):
        nonlocal out, done
        bufs = []
        for n in range(done, done + many):
            bufs += held(position[n])
        u3, brow = solved
        out = bulk(info, lists, chips, bufs, known[:2], m2, u3, moved, brow, out, done, many)
        done += many
        return out

    def work(t):
        nonlocal known, solved, moved
        if t == 3:
            return [buf for bufs, _ in gathered for buf in bufs[1:2]]
        if known is None and t >= TABLE_AT + share + chips - 1:
            known = head(info, chips, held(TABLE_AT, share), inv)
            return [known[0]]
        if known is not None and solved is None:
            solved = solve(seen, owner, rank, gathered, *known[2:], inv)
            moved = fetch(seen, displaced)
            return [solved[1]]
        ready = [n for n in range(done, tiles) if position[n] + chips < t]
        if solved is not None and ready:
            return [update(min(2, len(ready)))]
        return []

    if out is not None:
        out = out.reshape(m2.shape)
    for t in range(length + chips - 1):
        fresh = work(t)
        if fresh:
            tied = lax.optimization_barrier(tuple(own[k][-1] for k in range(CHAINS)) + tuple(fresh))
            ends = tied[:CHAINS]
        else:
            ends = [own[k][-1] if t else None for k in range(CHAINS)]
        for k in range(CHAINS):
            cur = items[t * CHAINS + k] if t < length else None
            if t > 0:
                came = send(ends[k], "pcol", hop)
                cur = came if cur is None else jnp.where(z == 0, cur, came)
            own[k].append(cur)
            sib[k].append(send(cur, "pcol", swap))
    while known is None or solved is None:
        work(length + chips)
    while done < tiles:
        update(1)
    return out.reshape(rows, groups, LANES)


def shards(matrix, pivots, inverse_blocks):
    row_blocks, _, width, blocks, _, _ = matrix.shape
    procs = lax.axis_size("prow")
    me = lax.axis_index("prow").astype(jnp.int32)
    mc = lax.axis_index("pcol").astype(jnp.int32)
    info = jnp.stack([me, mc, mc // 2, mc % 2, me])
    m3 = matrix.reshape(row_blocks * width, -1, LANES)
    m4 = matrix.reshape(row_blocks * width, blocks, -1, LANES)
    first = panel(m4, 0, CHAINS, row_blocks * width // CHUNKS)
    pivots, first = lax.optimization_barrier((pivots, first))
    so, sl, sr, do, dl, dr, src_most, dest_most = plan(pivots, width, procs, me)
    mean = 2 * width // procs
    cap = min(2 * width, (mean + mean // 4 + 7) // 8 * 8)
    fmean = width // procs
    fcap = min(width, (fmean + fmean // 2 + 7) // 8 * 8)
    again = (src_most > cap) | (dest_most > fcap)
    args = (m3, inverse_blocks, info, tuple(first), (so, sl, sr), (do, dl, dr))
    out = factor(cap, fcap, *args)

    out = lax.cond(
        again,
        lambda done, *rest: factor(None, None, *rest, done),
        lambda done, *rest: done,
        out,
        *args,
    )
    return out.reshape(matrix.shape)


def solution(mesh):
    return jax.shard_map(
        shards,
        mesh=mesh,
        in_specs=(P(None, "prow", None, None, "pcol", None), P(), P()),
        out_specs=P(None, "prow", None, None, "pcol", None),
        check_vma=False,
    )
```

```python
import functools

import jax
import jax.numpy as jnp
from jax import lax
from jax.experimental import pallas as pl
from jax.experimental.pallas import tpu as pltpu
from jax.sharding import PartitionSpec as P

LANES = 128
CHUNKS = 16
CHAINS = 2
TABLE_AT = 2
TILE = 512
DELIVER_AT = 7
SOLVE_AT = 9
AT_ONCE = 2
AT_LAST = 2
F32 = jnp.float32
BF16 = jnp.bfloat16
ANY = pl.BlockSpec(memory_space=pl.ANY)
VMEM = pl.BlockSpec(memory_space=pltpu.VMEM)
SMEM = pl.BlockSpec(memory_space=pltpu.SMEM)
PARAMS = pltpu.CompilerParams(vmem_limit_bytes=56 << 20)


def cost(nbytes):
    return pl.CostEstimate(flops=0, bytes_accessed=int(nbytes), transcendentals=0)


def split(x):
    high = x.astype(BF16)
    return high, (x - high.astype(F32)).astype(BF16)


def dot3(left, right):
    out = jnp.dot(left[0], right[0], preferred_element_type=F32)
    out += jnp.dot(left[0], right[1], preferred_element_type=F32)
    return out + jnp.dot(left[1], right[0], preferred_element_type=F32)


def upper(packed):
    row = lax.broadcasted_iota(jnp.int32, packed.shape, 0)
    col = lax.broadcasted_iota(jnp.int32, packed.shape, 1)
    return jnp.where(col >= row, packed, 0.0)


def unit_lower(packed):
    row = lax.broadcasted_iota(jnp.int32, packed.shape, 0)
    col = lax.broadcasted_iota(jnp.int32, packed.shape, 1)
    return jnp.where(col < row, packed, jnp.where(col == row, 1.0, 0.0))


def get_block(ref, start, count, groups, block, per):
    parts = [
        ref[pl.ds(start * groups + block * per + h, count, stride=groups), :] for h in range(per)
    ]
    return jnp.concatenate(parts, axis=1)


def put_block(ref, start, count, groups, block, per, value):
    for h in range(per):
        ref[pl.ds(start * groups + block * per + h, count, stride=groups), :] = value[
            :, h * LANES : (h + 1) * LANES
        ]


def panel_copies(info_ref, chips, bufs, c0_ref, c1_ref, sem, act):
    rows = bufs[0].shape[0]
    for h in range(chips):
        for core in range(2):

            @pl.when((info_ref[2] == h) & (info_ref[3] == core))
            def _():
                for n in range(len(bufs) // (2 * chips)):
                    own, sib = bufs[2 * n * chips + h], bufs[(2 * n + 1) * chips + h]
                    first, second = (own, sib) if core == 0 else (sib, own)
                    spot = pl.ds(n * rows, rows)
                    act(pltpu.make_async_copy(first, c0_ref.at[spot], sem.at[2 * n]))
                    act(pltpu.make_async_copy(second, c1_ref.at[spot], sem.at[2 * n + 1]))


def start(copy):
    copy.start()


def wait(copy):
    copy.wait()


def panel(m4, first, count, rows):
    shape = (rows,) + m4.shape[2:]

    def kernel(m_ref, *rest):
        outs, sem = rest[:count], rest[count]
        copies = [
            pltpu.make_async_copy(m_ref.at[pl.ds((first + k) * rows, rows), 0], outs[k], sem.at[k])
            for k in range(count)
        ]
        for copy in copies:
            copy.start()
        for copy in copies:
            copy.wait()

    return pl.pallas_call(
        kernel,
        in_specs=[ANY],
        out_specs=[VMEM] * count,
        out_shape=[jax.ShapeDtypeStruct(shape, F32)] * count,
        scratch_shapes=[pltpu.SemaphoreType.DMA((count,))],
        compiler_params=PARAMS,
        cost_estimate=cost(1 << 18),
        name="panel",
    )(m4)


def collect_kernel(procs, per, info_ref, list_ref, out_list_ref, m_ref, *rest):
    row_ref = rest[0]
    out_refs, head_refs = rest[1 : 1 + procs], rest[1 + procs : 1 + 2 * procs]
    top_ref, sem = rest[1 + 2 * procs :]
    cap = row_ref.shape[0]
    width = top_ref.shape[0]
    fcap = out_refs[0].shape[0]
    top = pltpu.make_async_copy(m_ref.at[pl.ds(0, width)], top_ref, sem.at[0])
    top.start()

    def fetch(k, carry):
        pltpu.make_async_copy(m_ref.at[list_ref[k]], row_ref.at[k], sem.at[1]).start()
        return carry

    lax.fori_loop(0, cap, fetch, 0)
    top.wait()

    @pl.when(info_ref[0] < 2)
    def _():
        for x in range(procs):

            def give(k, carry):
                row = top_ref[out_list_ref[x, k]]
                out_refs[x][k] = row
                head_refs[x][cap + k] = row[0:per]
                return carry

            lax.fori_loop(0, fcap, give, 0, unroll=4)

    pltpu.make_async_copy(row_ref, row_ref, sem.at[1]).wait()

    def keep(k, carry):
        row = row_ref[k, 0:per, :]
        for x in range(procs):
            head_refs[x][k] = row
        return carry

    lax.fori_loop(0, cap, keep, 0, unroll=4)


def collect(info, row_list, out_list, m3, per, width):
    cap = row_list.shape[0]
    procs, fcap = out_list.shape
    groups = m3.shape[1]
    out = jax.ShapeDtypeStruct((fcap, groups, LANES), F32)
    head = jax.ShapeDtypeStruct((cap + fcap, per, LANES), F32)
    outs = pl.pallas_call(
        functools.partial(collect_kernel, procs, per),
        in_specs=[SMEM, SMEM, SMEM, ANY],
        out_specs=[VMEM] * (1 + 2 * procs),
        out_shape=[jax.ShapeDtypeStruct((cap, groups, LANES), F32)] + [out] * procs + [head] * procs,
        scratch_shapes=[
            pltpu.VMEM((width, groups, LANES), F32),
            pltpu.SemaphoreType.DMA((2,)),
        ],
        compiler_params=PARAMS,
        cost_estimate=cost(1 << 18),
        name="collect",
    )(info, row_list, out_list, m3)
    return outs[0], outs[1 : 1 + procs], outs[1 + procs :]


def tables_kernel(procs, cap, width, info_ref, owner_ref, rank_ref, *rest):
    ins = rest[:procs]
    o_ref, buf_ref, sem = rest[procs:]
    fcap = buf_ref.shape[1] - cap
    copies = [
        pltpu.make_async_copy(ins[x], buf_ref.at[info_ref[0] ^ x], sem.at[x]) for x in range(procs)
    ]
    for copy in copies:
        copy.start()
    for copy in copies:
        copy.wait()
    base = jnp.where(info_ref[3] == 0, width, 0)

    def pivot(k, carry):
        o_ref[k] = buf_ref[owner_ref[base + k], rank_ref[base + k]]
        return carry

    lax.fori_loop(0, width, pivot, 0, unroll=4)
    for source in range(2):

        def other(k, carry):
            o_ref[width + source * fcap + k] = buf_ref[source, cap + k]
            return carry

        lax.fori_loop(0, fcap, other, 0, unroll=4)


def tables(info, owner, rank, heads, cap, width, rows):
    procs = len(heads)
    both, per, _ = heads[0].shape
    return pl.pallas_call(
        functools.partial(tables_kernel, procs, cap, width),
        in_specs=[SMEM, SMEM, SMEM] + [ANY] * procs,
        out_specs=VMEM,
        out_shape=jax.ShapeDtypeStruct((rows, per, LANES), F32),
        scratch_shapes=[
            pltpu.VMEM((procs, both, per, LANES), F32),
            pltpu.SemaphoreType.DMA((procs,)),
        ],
        compiler_params=PARAMS,
        cost_estimate=cost(1 << 18),
        name="tables",
    )(info, owner, rank, *heads)


def head_kernel(chips, info_ref, *rest):
    (*bufs, inv_ref, c0_ref, c1_ref, l01_ref, own_ref, w_ref, left_ref, sem) = rest
    width = inv_ref.shape[1]
    per = width // LANES
    me, mc = info_ref[0], info_ref[1]
    panel_copies(info_ref, chips, bufs, c0_ref, c1_ref, sem, start)
    panel_copies(info_ref, chips, bufs, c0_ref, c1_ref, sem, wait)
    z1c0 = get_block(c0_ref, 0, width, per, 0, per)
    g0c1 = get_block(c1_ref, 0, width, per, 0, per)
    one0, one1 = unit_lower(inv_ref[0]), unit_lower(inv_ref[1])
    up0, up1 = upper(inv_ref[0]), upper(inv_ref[1])
    low0, low1, v0, v1 = split(one0), split(one1), split(up0), split(up1)
    l01 = dot3(split(z1c0), v0)
    l01_ref[...] = l01
    u01 = dot3(low0, split(g0c1))
    back = dot3(low1, split(dot3(split(l01), low0)))
    cross = dot3(v0, split(u01))
    crosses = split(cross)
    parts = (
        split(dot3(v0, low0)),
        split(dot3(v1, split(back))),
        split(dot3(v1, low1)),
        crosses,
    )
    for n, part in enumerate(parts):
        for k in range(2):
            w_ref[(2 * n + k) * width : (2 * n + k + 1) * width] = part[k]
    mine = (split(jnp.where(me == 0, one0, -back)), split(jnp.where(me == 0, 0.0, one1)))
    for n, part in enumerate(mine):
        for k in range(2):
            own_ref[(2 * n + k) * width : (2 * n + k + 1) * width] = part[k]
    left_ref[:width] = jnp.where(mc == 0, -up0, dot3(crosses, v1))
    left_ref[width:] = jnp.where(mc == 0, 0.0, -up1)


def head(info, chips, bufs, inv):
    width = inv.shape[1]
    count = len(bufs) // (2 * chips)
    tab = jax.ShapeDtypeStruct((count * bufs[0].shape[0], LANES), F32)
    return pl.pallas_call(
        functools.partial(head_kernel, chips),
        in_specs=[SMEM] + [ANY] * len(bufs) + [VMEM],
        out_specs=[VMEM] * 6,
        out_shape=[
            tab,
            tab,
            jax.ShapeDtypeStruct((width, width), F32),
            jax.ShapeDtypeStruct((4 * width, width), BF16),
            jax.ShapeDtypeStruct((8 * width, width), BF16),
            jax.ShapeDtypeStruct((2 * width, width), F32),
        ],
        scratch_shapes=[pltpu.SemaphoreType.DMA((2 * count,))],
        compiler_params=PARAMS,
        cost_estimate=cost(1 << 20),
        name="head",
    )(info, *bufs, inv)


def triple(value):
    high, low = split(value)
    return high, high, low


def solve_kernel(groups, info_ref, owner_ref, rank_ref, *rest):
    g_ref, l01_ref, own_ref, w_ref, left_ref, inv_ref, u3_ref, brow_ref, s_ref = rest
    width = l01_ref.shape[0]
    per = width // LANES
    mc, me = info_ref[1], info_ref[4]
    def line_up(k, carry):
        spot = pl.ds(pl.multiple_of(k * groups, groups), groups)
        s_ref[spot, :] = g_ref[owner_ref[k], rank_ref[k]]
        return carry

    lax.fori_loop(0, 2 * width, line_up, 0, unroll=8)

    def pair(ref, n):
        return ref[2 * n * width : (2 * n + 1) * width], ref[(2 * n + 1) * width : (2 * n + 2) * width]

    def keep(block, value, first):
        for n, part in enumerate(triple(value)):
            at = 2 * n * width + first
            u3_ref[at : at + width, block * width : (block + 1) * width] = part

    for block in range(groups // per):
        g0 = split(get_block(s_ref, 0, width, groups, block, per))
        z1 = split(get_block(s_ref, width, width, groups, block, per))
        w1 = dot3(pair(w_ref, 2), z1) - dot3(pair(w_ref, 1), g0)
        w0 = dot3(pair(w_ref, 0), g0) - dot3(pair(w_ref, 3), split(w1))
        if block == 0:
            w0 = jnp.where(mc < 2, left_ref[:width], w0)
            w1 = jnp.where(mc < 2, left_ref[width:], w1)
        keep(block, w0, 0)
        keep(block, w1, width)

    for holder in range(2):

        @pl.when(me == holder)
        def _():
            def step(block, carry):
                u = dot3(pair(own_ref, 0), split(get_block(s_ref, 0, width, groups, block, per)))
                if holder == 1:
                    z1 = split(get_block(s_ref, width, width, groups, block, per))
                    u += dot3(pair(own_ref, 1), z1)
                put_block(brow_ref, 0, width, groups, block, per, u)
                return carry

            lax.fori_loop(0, groups // per, step, 0)

    @pl.when((mc == 0) & (me == 0))
    def _():
        put_block(brow_ref, 0, width, groups, 0, per, get_block(s_ref, 0, width, groups, 0, per))

    @pl.when((mc == 0) & (me == 1))
    def _():
        put_block(brow_ref, 0, width, groups, 0, per, l01_ref[...])

    @pl.when((mc == 1) & (me == 1))
    def _():
        g0 = split(get_block(s_ref, 0, width, groups, 0, per))
        z1 = get_block(s_ref, width, width, groups, 0, per)
        u0 = split(dot3(split(unit_lower(inv_ref[0])), g0))
        put_block(brow_ref, 0, width, groups, 0, per, z1 - dot3(split(l01_ref[...]), u0))


def solve(info, owner, rank, gathered, l01, own, w, left, inv):
    groups = gathered.shape[2]
    width = l01.shape[0]
    cols = groups * LANES
    return pl.pallas_call(
        functools.partial(solve_kernel, groups),
        in_specs=[SMEM, SMEM, SMEM] + [VMEM] * 6,
        out_specs=[VMEM, VMEM],
        out_shape=[
            jax.ShapeDtypeStruct((6 * width, cols), BF16),
            jax.ShapeDtypeStruct((width * groups, LANES), F32),
        ],
        scratch_shapes=[pltpu.VMEM((2 * width * groups, LANES), F32)],
        compiler_params=PARAMS,
        cost_estimate=cost(1 << 20),
        name="solve",
    )(info, owner, rank, gathered, l01, own, w, left, inv)


def make_bulk(chips, first, tiles, number, groups, width):
    def kernel(info_ref, order_ref, spot_ref, first_ref, *rest):
        bufs = rest[:number]
        m_ref, u3_ref, f_ref, brow_ref, t0_ref, t1_ref = rest[number : number + 6]
        o_ref, u_ref, moved_ref, row_ref, c0_ref, c1_ref, left_ref = rest[-11:-4]
        c_sem, in_sem, out_sem, sem = rest[-4:]
        each = number // tiles
        count = left_ref.shape[0]
        per = width // LANES
        mc = info_ref[1]
        half = min(TILE, count)
        u_copy = pltpu.make_async_copy(u3_ref, u_ref, sem.at[0])
        f_copy = pltpu.make_async_copy(f_ref, moved_ref, sem.at[1])

        def span(n):
            return pl.ds((first + n) * count * groups, count * groups)

        def panels(n, act):
            slot = n % 2
            panel_copies(
                info_ref, chips, bufs[n * each : (n + 1) * each], c0_ref.at[slot], c1_ref.at[slot],
                c_sem.at[slot], act,
            )

        def rows_in(n):
            return pltpu.make_async_copy(m_ref.at[span(n)], row_ref.at[n % 2], in_sem.at[n % 2])

        def store(n):
            return pltpu.make_async_copy(row_ref.at[n % 2], o_ref.at[span(n)], out_sem.at[n % 2])

        panels(0, start)
        f_copy.start()
        u_copy.start()
        rows_in(0).start()
        for n in range(tiles):
            slot = n % 2
            rows, c0, c1 = row_ref.at[slot], c0_ref.at[slot], c1_ref.at[slot]
            panels(n, wait)
            if n == 0:
                f_copy.wait()
            if n + 1 < tiles:
                panels(n + 1, start)

            def replace(e, carry):
                k = order_ref[e]
                here = pl.ds((spot_ref[k] - (first + n) * count) * per, per)
                there = pl.ds((width + k) * per, per)
                c0[here, :] = t0_ref[there, :]
                c1[here, :] = t1_ref[there, :]
                return carry

            lax.fori_loop(first_ref[first + n], first_ref[first + n + 1], replace, 0)
            for k, c in enumerate((c0, c1)):
                for part, value in enumerate(split(get_block(c, 0, count, per, 0, per))):
                    left_ref[:, (2 * part + k) * width : (2 * part + k + 1) * width] = value
                    if part == 0:
                        left_ref[:, (4 + k) * width : (5 + k) * width] = value
            rows_in(n).wait()

            def replace_row(e, carry):
                k = order_ref[e]
                here = (spot_ref[k] - (first + n) * count) * groups
                rows[pl.ds(pl.multiple_of(here, groups), groups), :] = moved_ref[k]
                return carry

            lax.fori_loop(first_ref[first + n], first_ref[first + n + 1], replace_row, 0)
            if n == 0:
                u_copy.wait()
            else:
                store(n - 1).wait()
            if n + 1 < tiles:
                rows_in(n + 1).start()

            def step(m, carry):
                left = left_ref[pl.ds(pl.multiple_of(m * half, half), half), :]
                for block in range(groups // per):
                    cols = slice(block * width, (block + 1) * width)
                    acc = jnp.dot(left, u_ref[:, cols], preferred_element_type=F32)
                    old = get_block(rows, m * half, half, groups, block, per)
                    if block == 0:
                        old = jnp.where(mc < 2, 0.0, old)
                    put_block(rows, m * half, half, groups, block, per, old - acc)
                return carry

            lax.fori_loop(0, count // half, step, 0)
            top = (first + n) * count
            if top < width:

                @pl.when(info_ref[0] < 2)
                def _():
                    many = min(count, width - top) * groups
                    copy = pltpu.make_async_copy(
                        brow_ref.at[pl.ds(top * groups, many)], rows.at[pl.ds(0, many)], sem.at[0]
                    )
                    copy.start()
                    copy.wait()

            store(n).start()
        store(tiles - 1).wait()

    return kernel


def bulk(info, lists, chips, bufs, tabs, m2, u3, moved, brow, out, first, tiles):
    groups = moved.shape[1]
    width = u3.shape[0] // 6
    per = width // LANES
    pieces = len(bufs) // (2 * chips * tiles)
    count = pieces * bufs[0].shape[0] // per
    in_specs = [SMEM] * 4 + [ANY] * (len(bufs) + 4) + [VMEM] * 2
    args = [info, *lists, *bufs, m2, u3, moved, brow, *tabs]
    aliases = {}
    if out is not None:
        in_specs.append(ANY)
        aliases = {len(args): 0}
        args.append(out)
    panels = pltpu.VMEM((2, count * per, LANES), F32)
    return pl.pallas_call(
        make_bulk(chips, first, tiles, len(bufs), groups, width),
        in_specs=in_specs,
        out_specs=ANY,
        out_shape=jax.ShapeDtypeStruct(m2.shape, F32),
        scratch_shapes=[
            pltpu.VMEM(u3.shape, BF16),
            pltpu.VMEM(moved.shape, F32),
            pltpu.VMEM((2, count * groups, LANES), F32),
            panels,
            panels,
            pltpu.VMEM((count, 6 * width), BF16),
            pltpu.SemaphoreType.DMA((2, 2 * pieces)),
            pltpu.SemaphoreType.DMA((2,)),
            pltpu.SemaphoreType.DMA((2,)),
            pltpu.SemaphoreType.DMA((2,)),
        ],
        input_output_aliases=aliases,
        compiler_params=PARAMS,
        cost_estimate=cost(1 << 20),
        name="bulk",
    )(*args)


def fetch_kernel(procs, info_ref, *rest):
    ins = rest[:procs]
    o_ref, sem = rest[procs:]
    rows = o_ref.shape[0] // 2
    for act in (start, wait):
        for source in range(2):
            spot = pl.ds(source * rows, rows)
            for x in range(procs):

                @pl.when((info_ref[0] ^ source) == x)
                def _():
                    act(pltpu.make_async_copy(ins[x], o_ref.at[spot], sem.at[source]))


def fetch(info, displaced):
    rows, groups, _ = displaced[0].shape
    return pl.pallas_call(
        functools.partial(fetch_kernel, len(displaced)),
        in_specs=[SMEM] + [ANY] * len(displaced),
        out_specs=VMEM,
        out_shape=jax.ShapeDtypeStruct((2 * rows, groups, LANES), F32),
        scratch_shapes=[pltpu.SemaphoreType.DMA((2,))],
        compiler_params=PARAMS,
        cost_estimate=cost(1 << 20),
        name="fetch",
    )(info, *displaced)


def plan(pivots, width, procs, me):
    p0, p1 = pivots[0], pivots[1]
    count = jnp.arange(width, dtype=jnp.int32)
    hit = p0[:, None] == p1[None, :]
    back = p0[:, None] == width + count[None, :]
    src1 = jnp.where(hit.any(0), jnp.sum(jnp.where(hit, count[:, None], 0), 0), p1)
    dest0 = jnp.where(
        back.any(1),
        jnp.sum(jnp.where(back, p1[None, :], 0), 1),
        jnp.where(hit.any(1), -1, p0),
    )
    dest1 = jnp.where(back.any(0), -1, p1)
    src = jnp.concatenate([p0, src1])
    dest = jnp.concatenate([dest0, dest1])
    src_owner = src // width % procs
    src_local = src // width // procs * width + src % width
    dest_owner = jnp.where(dest >= 0, dest // width % procs, -1)
    dest_local = dest // width // procs * width + dest % width
    order = jnp.arange(2 * width, dtype=jnp.int32)
    earlier = order[None, :] < order[:, None]
    same_half = (order[None, :] // width) == (order[:, None] // width)
    src_rank = jnp.sum(
        (earlier & (src_owner[None, :] == src_owner[:, None])).astype(jnp.int32), 1
    )
    dest_rank = jnp.sum(
        (earlier & same_half & (dest_owner[None, :] == dest_owner[:, None])).astype(jnp.int32), 1
    )
    src_most = jnp.max(src_rank) + 1
    dest_most = jnp.max(jnp.where(dest >= 0, dest_rank, -1)) + 1
    return src_owner, src_local, src_rank, dest_owner, dest_local, dest_rank, src_most, dest_most


def flip(procs, x):
    return [(s, s ^ x) for s in range(procs)]


def send(value, axis, pairs):
    flat = value.reshape(-1, LANES)
    return lax.ppermute(flat, axis, pairs).reshape(value.shape)


def exchange(cap, fcap, m3, width, info, src, dest):
    per = width // LANES
    procs = lax.axis_size("prow")
    me = info[0]
    src_owner, src_local, src_rank = src
    dest_owner, dest_local, dest_rank = dest

    src_rank = jnp.minimum(src_rank, cap - 1)
    slots = jnp.arange(cap, dtype=jnp.int32)
    mine = (src_owner == me)[None, :] & (src_rank[None, :] == slots[:, None])
    row_list = jnp.max(jnp.where(mine, src_local[None, :], 0), 1)

    fslots = jnp.arange(fcap, dtype=jnp.int32)
    owner2 = dest_owner.reshape(2, width)
    rank2 = dest_rank.reshape(2, width)
    local2 = dest_local.reshape(2, width)
    to = me ^ jnp.arange(procs, dtype=jnp.int32)
    out_owner = jnp.where(me == 0, owner2[0], owner2[1])
    out_rank = jnp.where(me == 0, rank2[0], rank2[1])
    chosen = (out_owner[None, None, :] == to[:, None, None]) & (
        out_rank[None, None, :] == fslots[None, :, None]
    )
    out_list = jnp.sum(jnp.where(chosen, jnp.arange(width, dtype=jnp.int32), 0), 2)
    landing = (owner2[:, None, :] == me) & (rank2[:, None, :] == fslots[None, :, None])
    spots = (jnp.sum(jnp.where(landing, local2[:, None, :] + 1, 0), 2) - 1).reshape(2 * fcap)

    sent, outgoing, heads = collect(info, row_list, out_list, m3, per, width)
    heads = [heads[0]] + [send(heads[x], "prow", flip(procs, x)) for x in range(1, procs)]
    gathered = lax.all_gather(sent.reshape(-1, LANES), "prow", axis=0, tiled=True)
    gathered = gathered.reshape((procs,) + sent.shape)
    return info, src_owner, src_rank, heads, gathered, outgoing, spots


def deliver(outgoing):
    procs = lax.axis_size("prow")
    return [outgoing[0]] + [
        send(outgoing[x], "prow", [(s, s ^ x) for s in range(2)]) for x in range(1, procs)
    ]


def exchange_any(m3, width, info, src, dest):
    per = width // LANES
    me = info[0]
    src_owner, src_local, _ = src
    dest_owner, dest_local, _ = dest
    rows = jnp.where((src_owner == me)[:, None, None], m3[src_local], 0.0)
    rows = lax.psum(rows.reshape(-1, LANES), "prow").reshape(rows.shape)
    displaced = []
    for source in range(2):
        top = jnp.where(me == source, m3[:width], 0.0)
        displaced.append(lax.psum(top.reshape(-1, LANES), "prow").reshape(top.shape))
    heads = [jnp.concatenate([rows[:, :per], top[:, :per]]) for top in displaced]
    spots = jnp.where(dest_owner == me, dest_local, -1)
    order = jnp.arange(2 * width, dtype=jnp.int32)
    first = jnp.concatenate([jnp.zeros((1,), jnp.int32), info[1:]])
    gathered = rows[None]
    return first, jnp.zeros_like(order), order, heads, gathered, displaced, spots


def factor(cap, fcap, m3, inv, info, first, src, dest, out=None):
    rows, groups, _ = m3.shape
    width = inv.shape[1]
    chips = lax.axis_size("pcol") // 2
    per = width // LANES
    z = info[2]
    m2 = m3.reshape(rows * groups, LANES)
    m4 = m3.reshape(rows, groups // per, per, LANES)
    chunk = rows // CHUNKS
    hop = [(q, q + 2) for q in range(2 * chips - 2)]
    swap = [(q, q ^ 1) for q in range(2 * chips)]
    pieces = list(first) + list(panel(m4, CHAINS, CHUNKS - CHAINS, chunk))

    later = cap is not None
    if cap is None:
        cap, fcap, moves = 2 * width, width, exchange_any(m3, width, info, src, dest)
    else:
        moves = exchange(cap, fcap, m3, width, info, src, dest)
    seen, owner, rank, heads, gathered, displaced, spots = moves
    share = -(-(width + 2 * fcap) // (chunk * CHAINS))
    table = tables(seen, owner, rank, heads, cap, width, share * CHAINS * chunk)

    tiles = CHUNKS // CHAINS
    tile_of = jnp.where(spots < 0, tiles, spots // (CHAINS * chunk))
    place = jnp.arange(spots.shape[0], dtype=jnp.int32)
    before = (tile_of[None, :] < tile_of[:, None]) | (
        (tile_of[None, :] == tile_of[:, None]) & (place[None, :] < place[:, None])
    )
    at = jnp.sum(before.astype(jnp.int32), 1)
    order = jnp.sum(jnp.where(at[None, :] == place[:, None], place[None, :], 0), 1)
    starts = jnp.sum(
        (tile_of[None, :] < jnp.arange(tiles + 1, dtype=jnp.int32)[:, None]).astype(jnp.int32), 1
    )
    lists = (order, spots, starts)

    items = [piece.reshape(chunk * per, LANES) for piece in pieces]
    table = table.reshape(share * CHAINS, chunk * per, LANES)
    at = TABLE_AT * CHAINS
    items[at:at] = [table[n] for n in range(share * CHAINS)]
    length = len(items) // CHAINS
    position = [n if n < TABLE_AT else n + share for n in range(tiles)]
    own = [[] for _ in range(CHAINS)]
    sib = [[] for _ in range(CHAINS)]

    def held(t, count=1):
        bufs = []
        for n in range(t, t + count):
            for k in range(CHAINS):
                bufs += own[k][n : n + chips] + sib[k][n : n + chips]
        return bufs

    known = solved = moved = None
    done = 0

    def update(many):
        nonlocal out, done, moved
        if moved is None:
            moved = fetch(seen, deliver(displaced) if later else displaced)
        bufs = []
        for n in range(done, done + many):
            bufs += held(position[n])
        u3, brow = solved
        out = bulk(info, lists, chips, bufs, known[:2], m2, u3, moved, brow, out, done, many)
        done += many
        return out

    def work(t):
        nonlocal known, solved, moved, displaced
        if t == DELIVER_AT:
            return displaced if later else []
        if known is None and t >= TABLE_AT + share + chips - 1:
            known = head(info, chips, held(TABLE_AT, share), inv)
            return [known[0]]
        if known is not None and solved is None:
            if t < SOLVE_AT:
                return []
            solved = solve(seen, owner, rank, gathered, *known[2:], inv)
            return [solved[1]]
        ready = [n for n in range(done, tiles) if position[n] + chips < t]
        if solved is not None and ready:
            return [update(min(AT_ONCE, len(ready)))]
        return []

    if out is not None:
        out = out.reshape(m2.shape)
    for t in range(length + chips - 1):
        fresh = work(t)
        if fresh:
            tied = lax.optimization_barrier(tuple(own[k][-1] for k in range(CHAINS)) + tuple(fresh))
            ends = tied[:CHAINS]
            if later and t == DELIVER_AT:
                moved = fetch(seen, deliver(tied[CHAINS:]))
        else:
            ends = [own[k][-1] if t else None for k in range(CHAINS)]
        for k in range(CHAINS):
            cur = items[t * CHAINS + k] if t < length else None
            if t > 0:
                came = send(ends[k], "pcol", hop)
                cur = came if cur is None else jnp.where(z == 0, cur, came)
            own[k].append(cur)
            sib[k].append(send(cur, "pcol", swap))
    while solved is None:
        work(length + chips)
    while done < tiles:
        update(min(AT_LAST, tiles - done))
    return out.reshape(rows, groups, LANES)


def shards(matrix, pivots, inverse_blocks):
    row_blocks, _, width, blocks, _, _ = matrix.shape
    procs = lax.axis_size("prow")
    me = lax.axis_index("prow").astype(jnp.int32)
    mc = lax.axis_index("pcol").astype(jnp.int32)
    info = jnp.stack([me, mc, mc // 2, mc % 2, me])
    m3 = matrix.reshape(row_blocks * width, -1, LANES)
    m4 = matrix.reshape(row_blocks * width, blocks, -1, LANES)
    first = panel(m4, 0, CHAINS, row_blocks * width // CHUNKS)
    pivots, first = lax.optimization_barrier((pivots, first))
    so, sl, sr, do, dl, dr, src_most, dest_most = plan(pivots, width, procs, me)
    mean = 2 * width // procs
    cap = min(2 * width, (mean + mean // 4 + 7) // 8 * 8)
    fmean = width // procs
    fcap = min(width, (fmean + fmean // 2 + 7) // 8 * 8)
    again = (src_most > cap) | (dest_most > fcap)
    args = (m3, inverse_blocks, info, tuple(first), (so, sl, sr), (do, dl, dr))
    out = factor(cap, fcap, *args)

    out = lax.cond(
        again,
        lambda done, *rest: factor(None, None, *rest, done),
        lambda done, *rest: done,
        out,
        *args,
    )
    return out.reshape(matrix.shape)


def solution(mesh):
    return jax.shard_map(
        shards,
        mesh=mesh,
        in_specs=(P(None, "prow", None, None, "pcol", None), P(), P()),
        out_specs=P(None, "prow", None, None, "pcol", None),
        check_vma=False,
    )
```

```python
import functools

import jax
import jax.numpy as jnp
from jax import lax
from jax.experimental import pallas as pl
from jax.experimental.pallas import tpu as pltpu
from jax.sharding import PartitionSpec as P

LANES = 128
CHUNKS = 16
CHAINS = 2
TABLE_AT = 2
TILE = 256
DELIVER_AT = 8
SOLVE_AT = 9
AT_ONCE = 2
AT_LAST = 2
F32 = jnp.float32
BF16 = jnp.bfloat16
ANY = pl.BlockSpec(memory_space=pl.ANY)
VMEM = pl.BlockSpec(memory_space=pltpu.VMEM)
SMEM = pl.BlockSpec(memory_space=pltpu.SMEM)
PARAMS = pltpu.CompilerParams(vmem_limit_bytes=56 << 20)


def cost(nbytes):
    return pl.CostEstimate(flops=0, bytes_accessed=int(nbytes), transcendentals=0)


def split(x):
    high = x.astype(BF16)
    return high, (x - high.astype(F32)).astype(BF16)


def dot3(left, right):
    out = jnp.dot(left[0], right[0], preferred_element_type=F32)
    out += jnp.dot(left[0], right[1], preferred_element_type=F32)
    return out + jnp.dot(left[1], right[0], preferred_element_type=F32)


def upper(packed):
    row = lax.broadcasted_iota(jnp.int32, packed.shape, 0)
    col = lax.broadcasted_iota(jnp.int32, packed.shape, 1)
    return jnp.where(col >= row, packed, 0.0)


def unit_lower(packed):
    row = lax.broadcasted_iota(jnp.int32, packed.shape, 0)
    col = lax.broadcasted_iota(jnp.int32, packed.shape, 1)
    return jnp.where(col < row, packed, jnp.where(col == row, 1.0, 0.0))


def get_block(ref, start, count, groups, block, per):
    parts = [
        ref[pl.ds(start * groups + block * per + h, count, stride=groups), :] for h in range(per)
    ]
    return jnp.concatenate(parts, axis=1)


def put_block(ref, start, count, groups, block, per, value):
    for h in range(per):
        ref[pl.ds(start * groups + block * per + h, count, stride=groups), :] = value[
            :, h * LANES : (h + 1) * LANES
        ]


def panel_copies(info_ref, chips, bufs, c0_ref, c1_ref, sem, act):
    rows = bufs[0].shape[0]
    for h in range(chips):
        for core in range(2):

            @pl.when((info_ref[2] == h) & (info_ref[3] == core))
            def _():
                for n in range(len(bufs) // (2 * chips)):
                    own, sib = bufs[2 * n * chips + h], bufs[(2 * n + 1) * chips + h]
                    first, second = (own, sib) if core == 0 else (sib, own)
                    spot = pl.ds(n * rows, rows)
                    act(pltpu.make_async_copy(first, c0_ref.at[spot], sem.at[2 * n]))
                    act(pltpu.make_async_copy(second, c1_ref.at[spot], sem.at[2 * n + 1]))


def start(copy):
    copy.start()


def wait(copy):
    copy.wait()


def panel(m4, first, count, rows):
    shape = (rows,) + m4.shape[2:]

    def kernel(m_ref, *rest):
        outs, sem = rest[:count], rest[count]
        copies = [
            pltpu.make_async_copy(m_ref.at[pl.ds((first + k) * rows, rows), 0], outs[k], sem.at[k])
            for k in range(count)
        ]
        for copy in copies:
            copy.start()
        for copy in copies:
            copy.wait()

    return pl.pallas_call(
        kernel,
        in_specs=[ANY],
        out_specs=[VMEM] * count,
        out_shape=[jax.ShapeDtypeStruct(shape, F32)] * count,
        scratch_shapes=[pltpu.SemaphoreType.DMA((count,))],
        compiler_params=PARAMS,
        cost_estimate=cost(1 << 18),
        name="panel",
    )(m4)


def collect_kernel(procs, per, info_ref, list_ref, out_list_ref, m_ref, *rest):
    row_ref = rest[0]
    out_refs, head_refs = rest[1 : 1 + procs], rest[1 + procs : 1 + 2 * procs]
    top_ref, sem = rest[1 + 2 * procs :]
    cap = row_ref.shape[0]
    width = top_ref.shape[0]
    fcap = out_refs[0].shape[0]
    top = pltpu.make_async_copy(m_ref.at[pl.ds(0, width)], top_ref, sem.at[0])
    top.start()

    def fetch(k, carry):
        pltpu.make_async_copy(m_ref.at[list_ref[k]], row_ref.at[k], sem.at[1]).start()
        return carry

    lax.fori_loop(0, cap, fetch, 0)
    top.wait()

    @pl.when(info_ref[0] < 2)
    def _():
        for x in range(procs):

            def give(k, carry):
                row = top_ref[out_list_ref[x, k]]
                out_refs[x][k] = row
                head_refs[x][cap + k] = row[0:per]
                return carry

            lax.fori_loop(0, fcap, give, 0, unroll=4)

    pltpu.make_async_copy(row_ref, row_ref, sem.at[1]).wait()

    def keep(k, carry):
        row = row_ref[k, 0:per, :]
        for x in range(procs):
            head_refs[x][k] = row
        return carry

    lax.fori_loop(0, cap, keep, 0, unroll=4)


def collect(info, row_list, out_list, m3, per, width):
    cap = row_list.shape[0]
    procs, fcap = out_list.shape
    groups = m3.shape[1]
    out = jax.ShapeDtypeStruct((fcap, groups, LANES), F32)
    head = jax.ShapeDtypeStruct((cap + fcap, per, LANES), F32)
    outs = pl.pallas_call(
        functools.partial(collect_kernel, procs, per),
        in_specs=[SMEM, SMEM, SMEM, ANY],
        out_specs=[VMEM] * (1 + 2 * procs),
        out_shape=[jax.ShapeDtypeStruct((cap, groups, LANES), F32)] + [out] * procs + [head] * procs,
        scratch_shapes=[
            pltpu.VMEM((width, groups, LANES), F32),
            pltpu.SemaphoreType.DMA((2,)),
        ],
        compiler_params=PARAMS,
        cost_estimate=cost(1 << 18),
        name="collect",
    )(info, row_list, out_list, m3)
    return outs[0], outs[1 : 1 + procs], outs[1 + procs :]


def tables_kernel(procs, cap, width, info_ref, owner_ref, rank_ref, *rest):
    ins = rest[:procs]
    o_ref, buf_ref, sem = rest[procs:]
    fcap = buf_ref.shape[1] - cap
    copies = [
        pltpu.make_async_copy(ins[x], buf_ref.at[info_ref[0] ^ x], sem.at[x]) for x in range(procs)
    ]
    for copy in copies:
        copy.start()
    for copy in copies:
        copy.wait()
    base = jnp.where(info_ref[3] == 0, width, 0)

    def pivot(k, carry):
        o_ref[k] = buf_ref[owner_ref[base + k], rank_ref[base + k]]
        return carry

    lax.fori_loop(0, width, pivot, 0, unroll=4)
    for source in range(2):

        def other(k, carry):
            o_ref[width + source * fcap + k] = buf_ref[source, cap + k]
            return carry

        lax.fori_loop(0, fcap, other, 0, unroll=4)


def tables(info, owner, rank, heads, cap, width, rows):
    procs = len(heads)
    both, per, _ = heads[0].shape
    return pl.pallas_call(
        functools.partial(tables_kernel, procs, cap, width),
        in_specs=[SMEM, SMEM, SMEM] + [ANY] * procs,
        out_specs=VMEM,
        out_shape=jax.ShapeDtypeStruct((rows, per, LANES), F32),
        scratch_shapes=[
            pltpu.VMEM((procs, both, per, LANES), F32),
            pltpu.SemaphoreType.DMA((procs,)),
        ],
        compiler_params=PARAMS,
        cost_estimate=cost(1 << 18),
        name="tables",
    )(info, owner, rank, *heads)


def head_kernel(chips, info_ref, *rest):
    (*bufs, inv_ref, c0_ref, c1_ref, l01_ref, own_ref, w_ref, left_ref, sem) = rest
    width = inv_ref.shape[1]
    per = width // LANES
    me, mc = info_ref[0], info_ref[1]
    panel_copies(info_ref, chips, bufs, c0_ref, c1_ref, sem, start)
    panel_copies(info_ref, chips, bufs, c0_ref, c1_ref, sem, wait)
    z1c0 = get_block(c0_ref, 0, width, per, 0, per)
    g0c1 = get_block(c1_ref, 0, width, per, 0, per)
    one0, one1 = unit_lower(inv_ref[0]), unit_lower(inv_ref[1])
    up0, up1 = upper(inv_ref[0]), upper(inv_ref[1])
    low0, low1, v0, v1 = split(one0), split(one1), split(up0), split(up1)
    l01 = dot3(split(z1c0), v0)
    l01_ref[...] = l01
    u01 = dot3(low0, split(g0c1))
    back = dot3(low1, split(dot3(split(l01), low0)))
    cross = dot3(v0, split(u01))
    crosses = split(cross)
    parts = (
        split(dot3(v0, low0)),
        split(dot3(v1, split(back))),
        split(dot3(v1, low1)),
        crosses,
    )
    for n, part in enumerate(parts):
        for k in range(2):
            w_ref[(2 * n + k) * width : (2 * n + k + 1) * width] = part[k]
    mine = (split(jnp.where(me == 0, one0, -back)), split(jnp.where(me == 0, 0.0, one1)))
    for n, part in enumerate(mine):
        for k in range(2):
            own_ref[(2 * n + k) * width : (2 * n + k + 1) * width] = part[k]
    left_ref[:width] = jnp.where(mc == 0, -up0, dot3(crosses, v1))
    left_ref[width:] = jnp.where(mc == 0, 0.0, -up1)


def head(info, chips, bufs, inv):
    width = inv.shape[1]
    count = len(bufs) // (2 * chips)
    tab = jax.ShapeDtypeStruct((count * bufs[0].shape[0], LANES), F32)
    return pl.pallas_call(
        functools.partial(head_kernel, chips),
        in_specs=[SMEM] + [ANY] * len(bufs) + [VMEM],
        out_specs=[VMEM] * 6,
        out_shape=[
            tab,
            tab,
            jax.ShapeDtypeStruct((width, width), F32),
            jax.ShapeDtypeStruct((4 * width, width), BF16),
            jax.ShapeDtypeStruct((8 * width, width), BF16),
            jax.ShapeDtypeStruct((2 * width, width), F32),
        ],
        scratch_shapes=[pltpu.SemaphoreType.DMA((2 * count,))],
        compiler_params=PARAMS,
        cost_estimate=cost(1 << 20),
        name="head",
    )(info, *bufs, inv)


def solve_kernel(groups, info_ref, owner_ref, rank_ref, *rest):
    g_ref, l01_ref, own_ref, w_ref, left_ref, inv_ref, u_ref, brow_ref, s_ref = rest
    width = l01_ref.shape[0]
    per = width // LANES
    mc, me = info_ref[1], info_ref[4]
    def line_up(k, carry):
        spot = pl.ds(pl.multiple_of(k * groups, groups), groups)
        s_ref[spot, :] = g_ref[owner_ref[k], rank_ref[k]]
        return carry

    lax.fori_loop(0, 2 * width, line_up, 0, unroll=8)

    def pair(ref, n):
        return ref[2 * n * width : (2 * n + 1) * width], ref[(2 * n + 1) * width : (2 * n + 2) * width]

    def keep(block, value, first):
        for n, part in enumerate(split(value)):
            at = 2 * n * width + first
            u_ref[at : at + width, block * width : (block + 1) * width] = part

    for block in range(groups // per):
        g0 = split(get_block(s_ref, 0, width, groups, block, per))
        z1 = split(get_block(s_ref, width, width, groups, block, per))
        w1 = dot3(pair(w_ref, 2), z1) - dot3(pair(w_ref, 1), g0)
        w0 = dot3(pair(w_ref, 0), g0) - dot3(pair(w_ref, 3), split(w1))
        if block == 0:
            w0 = jnp.where(mc < 2, left_ref[:width], w0)
            w1 = jnp.where(mc < 2, left_ref[width:], w1)
        keep(block, w0, 0)
        keep(block, w1, width)

    for holder in range(2):

        @pl.when(me == holder)
        def _():
            def step(block, carry):
                u = dot3(pair(own_ref, 0), split(get_block(s_ref, 0, width, groups, block, per)))
                if holder == 1:
                    z1 = split(get_block(s_ref, width, width, groups, block, per))
                    u += dot3(pair(own_ref, 1), z1)
                put_block(brow_ref, 0, width, groups, block, per, u)
                return carry

            lax.fori_loop(0, groups // per, step, 0)

    @pl.when((mc == 0) & (me == 0))
    def _():
        put_block(brow_ref, 0, width, groups, 0, per, get_block(s_ref, 0, width, groups, 0, per))

    @pl.when((mc == 0) & (me == 1))
    def _():
        put_block(brow_ref, 0, width, groups, 0, per, l01_ref[...])

    @pl.when((mc == 1) & (me == 1))
    def _():
        g0 = split(get_block(s_ref, 0, width, groups, 0, per))
        z1 = get_block(s_ref, width, width, groups, 0, per)
        u0 = split(dot3(split(unit_lower(inv_ref[0])), g0))
        put_block(brow_ref, 0, width, groups, 0, per, z1 - dot3(split(l01_ref[...]), u0))


def solve(info, owner, rank, gathered, l01, own, w, left, inv):
    groups = gathered.shape[2]
    width = l01.shape[0]
    cols = groups * LANES
    return pl.pallas_call(
        functools.partial(solve_kernel, groups),
        in_specs=[SMEM, SMEM, SMEM] + [VMEM] * 6,
        out_specs=[VMEM, VMEM],
        out_shape=[
            jax.ShapeDtypeStruct((4 * width, cols), BF16),
            jax.ShapeDtypeStruct((width * groups, LANES), F32),
        ],
        scratch_shapes=[pltpu.VMEM((2 * width * groups, LANES), F32)],
        compiler_params=PARAMS,
        cost_estimate=cost(1 << 20),
        name="solve",
    )(info, owner, rank, gathered, l01, own, w, left, inv)


def make_bulk(chips, first, tiles, number, groups, width):
    def kernel(info_ref, order_ref, spot_ref, first_ref, *rest):
        bufs = rest[:number]
        m_ref, uhl_ref, f_ref, brow_ref, t0_ref, t1_ref = rest[number : number + 6]
        o_ref, u_ref, moved_ref, row_ref, c0_ref, c1_ref, left_ref = rest[-11:-4]
        c_sem, in_sem, out_sem, sem = rest[-4:]
        each = number // tiles
        count = left_ref.shape[0]
        per = width // LANES
        mc = info_ref[1]
        parts = row_ref.shape[1]
        half = count // parts
        u_copy = pltpu.make_async_copy(uhl_ref, u_ref, sem.at[0])
        f_copy = pltpu.make_async_copy(f_ref, moved_ref, sem.at[1])

        def span(n, part):
            return pl.ds(((first + n) * count + part * half) * groups, half * groups)

        def panels(n, act):
            slot = n % 2
            panel_copies(
                info_ref, chips, bufs[n * each : (n + 1) * each], c0_ref.at[slot], c1_ref.at[slot],
                c_sem.at[slot], act,
            )

        def rows_in(n, part):
            slot = n % 2
            return pltpu.make_async_copy(
                m_ref.at[span(n, part)], row_ref.at[slot, part], in_sem.at[slot, part]
            )

        def store(n, part):
            slot = n % 2
            return pltpu.make_async_copy(
                row_ref.at[slot, part], o_ref.at[span(n, part)], out_sem.at[slot, part]
            )

        panels(0, start)
        f_copy.start()
        u_copy.start()
        for part in range(parts):
            rows_in(0, part).start()
        for n in range(tiles):
            slot = n % 2
            c0, c1 = c0_ref.at[slot], c1_ref.at[slot]
            panels(n, wait)
            if n + 1 < tiles:
                panels(n + 1, start)

            def replace(e, carry):
                k = order_ref[e]
                here = pl.ds((spot_ref[k] - (first + n) * count) * per, per)
                there = pl.ds((width + k) * per, per)
                c0[here, :] = t0_ref[there, :]
                c1[here, :] = t1_ref[there, :]
                return carry

            lax.fori_loop(first_ref[first + n], first_ref[first + n + 1], replace, 0)
            for k, c in enumerate((c0, c1)):
                for part, value in enumerate(split(get_block(c, 0, count, per, 0, per))):
                    left_ref[:, (2 * part + k) * width : (2 * part + k + 1) * width] = value
            if n == 0:
                f_copy.wait()
                u_copy.wait()
            for part in range(parts):
                rows_in(n, part).wait()
                if n + 1 < tiles:
                    if n > 0:
                        store(n - 1, part).wait()
                    rows_in(n + 1, part).start()
                rows = row_ref.at[slot, part]
                base = (first + n) * count + part * half

                def replace_row(e, carry):
                    k = order_ref[e]
                    here = spot_ref[k] - base

                    @pl.when((here >= 0) & (here < half))
                    def _():
                        spot = pl.ds(pl.multiple_of(here * groups, groups), groups)
                        rows[spot, :] = moved_ref[k]

                    return carry

                lax.fori_loop(first_ref[first + n], first_ref[first + n + 1], replace_row, 0)
                high = left_ref[part * half : (part + 1) * half, : 2 * width]
                low = left_ref[part * half : (part + 1) * half, 2 * width :]
                for block in range(groups // per):
                    cols = slice(block * width, (block + 1) * width)
                    acc = dot3((high, low), (u_ref[: 2 * width, cols], u_ref[2 * width :, cols]))
                    old = get_block(rows, 0, half, groups, block, per)
                    if block == 0:
                        old = jnp.where(mc < 2, 0.0, old)
                    put_block(rows, 0, half, groups, block, per, old - acc)
                if base < width:

                    @pl.when(info_ref[0] < 2)
                    def _():
                        many = min(half, width - base) * groups
                        copy = pltpu.make_async_copy(
                            brow_ref.at[pl.ds(base * groups, many)],
                            rows.at[pl.ds(0, many)],
                            sem.at[0],
                        )
                        copy.start()
                        copy.wait()

                store(n, part).start()
        for n in range(max(0, tiles - 2), tiles):
            for part in range(parts):
                store(n, part).wait()

    return kernel


def bulk(info, lists, chips, bufs, tabs, m2, uhl, moved, brow, out, first, tiles):
    groups = moved.shape[1]
    width = uhl.shape[0] // 4
    per = width // LANES
    pieces = len(bufs) // (2 * chips * tiles)
    count = pieces * bufs[0].shape[0] // per
    parts = max(1, count // TILE)
    in_specs = [SMEM] * 4 + [ANY] * (len(bufs) + 4) + [VMEM] * 2
    args = [info, *lists, *bufs, m2, uhl, moved, brow, *tabs]
    aliases = {}
    if out is not None:
        in_specs.append(ANY)
        aliases = {len(args): 0}
        args.append(out)
    panels = pltpu.VMEM((2, count * per, LANES), F32)
    return pl.pallas_call(
        make_bulk(chips, first, tiles, len(bufs), groups, width),
        in_specs=in_specs,
        out_specs=ANY,
        out_shape=jax.ShapeDtypeStruct(m2.shape, F32),
        scratch_shapes=[
            pltpu.VMEM(uhl.shape, BF16),
            pltpu.VMEM(moved.shape, F32),
            pltpu.VMEM((2, parts, count // parts * groups, LANES), F32),
            panels,
            panels,
            pltpu.VMEM((count, 4 * width), BF16),
            pltpu.SemaphoreType.DMA((2, 2 * pieces)),
            pltpu.SemaphoreType.DMA((2, parts)),
            pltpu.SemaphoreType.DMA((2, parts)),
            pltpu.SemaphoreType.DMA((2,)),
        ],
        input_output_aliases=aliases,
        compiler_params=PARAMS,
        cost_estimate=cost(1 << 20),
        name="bulk",
    )(*args)


def fetch_kernel(procs, info_ref, *rest):
    ins = rest[:procs]
    o_ref, sem = rest[procs:]
    rows = o_ref.shape[0] // 2
    for act in (start, wait):
        for source in range(2):
            spot = pl.ds(source * rows, rows)
            for x in range(procs):

                @pl.when((info_ref[0] ^ source) == x)
                def _():
                    act(pltpu.make_async_copy(ins[x], o_ref.at[spot], sem.at[source]))


def fetch(info, displaced):
    rows, groups, _ = displaced[0].shape
    return pl.pallas_call(
        functools.partial(fetch_kernel, len(displaced)),
        in_specs=[SMEM] + [ANY] * len(displaced),
        out_specs=VMEM,
        out_shape=jax.ShapeDtypeStruct((2 * rows, groups, LANES), F32),
        scratch_shapes=[pltpu.SemaphoreType.DMA((2,))],
        compiler_params=PARAMS,
        cost_estimate=cost(1 << 20),
        name="fetch",
    )(info, *displaced)


def plan(pivots, width, procs, me):
    p0, p1 = pivots[0], pivots[1]
    count = jnp.arange(width, dtype=jnp.int32)
    hit = p0[:, None] == p1[None, :]
    back = p0[:, None] == width + count[None, :]
    src1 = jnp.where(hit.any(0), jnp.sum(jnp.where(hit, count[:, None], 0), 0), p1)
    dest0 = jnp.where(
        back.any(1),
        jnp.sum(jnp.where(back, p1[None, :], 0), 1),
        jnp.where(hit.any(1), -1, p0),
    )
    dest1 = jnp.where(back.any(0), -1, p1)
    src = jnp.concatenate([p0, src1])
    dest = jnp.concatenate([dest0, dest1])
    src_owner = src // width % procs
    src_local = src // width // procs * width + src % width
    dest_owner = jnp.where(dest >= 0, dest // width % procs, -1)
    dest_local = dest // width // procs * width + dest % width
    order = jnp.arange(2 * width, dtype=jnp.int32)
    earlier = order[None, :] < order[:, None]
    same_half = (order[None, :] // width) == (order[:, None] // width)
    src_rank = jnp.sum(
        (earlier & (src_owner[None, :] == src_owner[:, None])).astype(jnp.int32), 1
    )
    dest_rank = jnp.sum(
        (earlier & same_half & (dest_owner[None, :] == dest_owner[:, None])).astype(jnp.int32), 1
    )
    src_most = jnp.max(src_rank) + 1
    dest_most = jnp.max(jnp.where(dest >= 0, dest_rank, -1)) + 1
    return src_owner, src_local, src_rank, dest_owner, dest_local, dest_rank, src_most, dest_most


def flip(procs, x):
    return [(s, s ^ x) for s in range(procs)]


def send(value, axis, pairs):
    flat = value.reshape(-1, LANES)
    return lax.ppermute(flat, axis, pairs).reshape(value.shape)


def exchange(cap, fcap, m3, width, info, came1, src, dest):
    per = width // LANES
    procs = lax.axis_size("prow")
    me = info[0]
    src_owner, src_local, src_rank = src
    dest_owner, dest_local, dest_rank = dest

    src_rank = jnp.minimum(src_rank, cap - 1)
    slots = jnp.arange(cap, dtype=jnp.int32)
    mine = (src_owner == me)[None, :] & (src_rank[None, :] == slots[:, None])
    row_list = jnp.max(jnp.where(mine, src_local[None, :], 0), 1)

    fslots = jnp.arange(fcap, dtype=jnp.int32)
    owner2 = dest_owner.reshape(2, width)
    rank2 = dest_rank.reshape(2, width)
    local2 = dest_local.reshape(2, width)
    to = me ^ jnp.arange(procs, dtype=jnp.int32)
    out_owner = jnp.where(me == 0, owner2[0], owner2[1])
    out_rank = jnp.where(me == 0, rank2[0], rank2[1])
    chosen = (out_owner[None, None, :] == to[:, None, None]) & (
        out_rank[None, None, :] == fslots[None, :, None]
    )
    out_list = jnp.sum(jnp.where(chosen, jnp.arange(width, dtype=jnp.int32), 0), 2)
    landing = (owner2[:, None, :] == me) & (rank2[:, None, :] == fslots[None, :, None])
    spots = (jnp.sum(jnp.where(landing, local2[:, None, :] + 1, 0), 2) - 1).reshape(2 * fcap)

    sent, outgoing, heads = collect(info, row_list, out_list, m3, per, width)
    heads = [heads[0]] + [send(heads[x], "prow", flip(procs, x)) for x in range(1, procs)]
    sent, *came1 = lax.optimization_barrier((sent, *came1))
    gathered = lax.all_gather(sent.reshape(-1, LANES), "prow", axis=0, tiled=True)
    gathered = gathered.reshape((procs,) + sent.shape)
    return info, src_owner, src_rank, heads, gathered, outgoing, spots, came1


def deliver(outgoing):
    procs = lax.axis_size("prow")
    return [outgoing[0]] + [
        send(outgoing[x], "prow", [(s, s ^ x) for s in range(2)]) for x in range(1, procs)
    ]


def exchange_any(m3, width, info, src, dest):
    per = width // LANES
    me = info[0]
    src_owner, src_local, _ = src
    dest_owner, dest_local, _ = dest
    rows = jnp.where((src_owner == me)[:, None, None], m3[src_local], 0.0)
    rows = lax.psum(rows.reshape(-1, LANES), "prow").reshape(rows.shape)
    displaced = []
    for source in range(2):
        top = jnp.where(me == source, m3[:width], 0.0)
        displaced.append(lax.psum(top.reshape(-1, LANES), "prow").reshape(top.shape))
    heads = [jnp.concatenate([rows[:, :per], top[:, :per]]) for top in displaced]
    spots = jnp.where(dest_owner == me, dest_local, -1)
    order = jnp.arange(2 * width, dtype=jnp.int32)
    first = jnp.concatenate([jnp.zeros((1,), jnp.int32), info[1:]])
    gathered = rows[None]
    return first, jnp.zeros_like(order), order, heads, gathered, displaced, spots


def factor(cap, fcap, m3, inv, info, first, came1, src, dest, out=None):
    rows, groups, _ = m3.shape
    width = inv.shape[1]
    chips = lax.axis_size("pcol") // 2
    per = width // LANES
    z = info[2]
    m2 = m3.reshape(rows * groups, LANES)
    m4 = m3.reshape(rows, groups // per, per, LANES)
    chunk = rows // CHUNKS
    hop = [(q, q + 2) for q in range(2 * chips - 2)]
    swap = [(q, q ^ 1) for q in range(2 * chips)]
    pieces = list(first) + list(panel(m4, CHAINS, CHUNKS - CHAINS, chunk))

    later = cap is not None
    if cap is None:
        cap, fcap = 2 * width, width
        moves = exchange_any(m3, width, info, src, dest) + (came1,)
    else:
        moves = exchange(cap, fcap, m3, width, info, came1, src, dest)
    seen, owner, rank, heads, gathered, displaced, spots, came1 = moves
    share = -(-(width + 2 * fcap) // (chunk * CHAINS))
    table = tables(seen, owner, rank, heads, cap, width, share * CHAINS * chunk)

    tiles = CHUNKS // CHAINS
    tile_of = jnp.where(spots < 0, tiles, spots // (CHAINS * chunk))
    place = jnp.arange(spots.shape[0], dtype=jnp.int32)
    before = (tile_of[None, :] < tile_of[:, None]) | (
        (tile_of[None, :] == tile_of[:, None]) & (place[None, :] < place[:, None])
    )
    at = jnp.sum(before.astype(jnp.int32), 1)
    order = jnp.sum(jnp.where(at[None, :] == place[:, None], place[None, :], 0), 1)
    starts = jnp.sum(
        (tile_of[None, :] < jnp.arange(tiles + 1, dtype=jnp.int32)[:, None]).astype(jnp.int32), 1
    )
    lists = (order, spots, starts)

    items = [piece.reshape(chunk * per, LANES) for piece in pieces]
    table = table.reshape(share * CHAINS, chunk * per, LANES)
    at = TABLE_AT * CHAINS
    items[at:at] = [table[n] for n in range(share * CHAINS)]
    length = len(items) // CHAINS
    position = [n if n < TABLE_AT else n + share for n in range(tiles)]
    own = [[] for _ in range(CHAINS)]
    sib = [[] for _ in range(CHAINS)]

    def held(t, count=1):
        bufs = []
        for n in range(t, t + count):
            for k in range(CHAINS):
                bufs += own[k][n : n + chips] + sib[k][n : n + chips]
        return bufs

    known = solved = moved = None
    done = 0

    def update(many):
        nonlocal out, done, moved
        if moved is None:
            moved = fetch(seen, deliver(displaced) if later else displaced)
        bufs = []
        for n in range(done, done + many):
            bufs += held(position[n])
        uhl, brow = solved
        out = bulk(info, lists, chips, bufs, known[:2], m2, uhl, moved, brow, out, done, many)
        done += many
        return out

    def work(t):
        nonlocal known, solved, moved, displaced
        if t == DELIVER_AT:
            return displaced if later else []
        if known is None and t >= TABLE_AT + share + chips - 1:
            known = head(info, chips, held(TABLE_AT, share), inv)
            return [known[0]]
        if known is not None and solved is None:
            if t < SOLVE_AT:
                return []
            solved = solve(seen, owner, rank, gathered, *known[2:], inv)
            return [solved[1]]
        ready = [n for n in range(done, tiles) if position[n] + chips < t]
        if solved is not None and ready:
            return [update(min(AT_ONCE, len(ready)))]
        return []

    if out is not None:
        out = out.reshape(m2.shape)
    for t in range(length + chips - 1):
        fresh = work(t)
        if fresh:
            tied = lax.optimization_barrier(tuple(own[k][-1] for k in range(CHAINS)) + tuple(fresh))
            ends = tied[:CHAINS]
            if later and t == DELIVER_AT:
                moved = fetch(seen, deliver(tied[CHAINS:]))
        else:
            ends = [own[k][-1] if t else None for k in range(CHAINS)]
        for k in range(CHAINS):
            cur = items[t * CHAINS + k] if t < length else None
            if t > 0:
                came = came1[k] if t == 1 else send(ends[k], "pcol", hop)
                cur = came if cur is None else jnp.where(z == 0, cur, came)
            own[k].append(cur)
        if t == length + chips - 2 and solved is not None and position[done] + chips <= t:
            tied = lax.optimization_barrier(tuple(own[k][-1] for k in range(CHAINS)) + (update(AT_ONCE),))
            for k in range(CHAINS):
                own[k][-1] = tied[k]
            out = tied[-1]
        for k in range(CHAINS):
            sib[k].append(send(own[k][-1], "pcol", swap))
    while solved is None:
        work(length + chips)
    while done < tiles:
        update(min(AT_LAST, tiles - done))
    return out.reshape(rows, groups, LANES)


def shards(matrix, pivots, inverse_blocks):
    row_blocks, _, width, blocks, _, _ = matrix.shape
    procs = lax.axis_size("prow")
    me = lax.axis_index("prow").astype(jnp.int32)
    mc = lax.axis_index("pcol").astype(jnp.int32)
    info = jnp.stack([me, mc, mc // 2, mc % 2, me])
    m3 = matrix.reshape(row_blocks * width, -1, LANES)
    m4 = matrix.reshape(row_blocks * width, blocks, -1, LANES)
    first = panel(m4, 0, CHAINS, row_blocks * width // CHUNKS)
    pivots, first = lax.optimization_barrier((pivots, first))
    flat = [piece.reshape(-1, LANES) for piece in first]
    hop = [(q, q + 2) for q in range(lax.axis_size("pcol") - 2)]
    came = tuple(lax.ppermute(piece, "pcol", hop) for piece in flat)
    so, sl, sr, do, dl, dr, src_most, dest_most = plan(pivots, width, procs, me)
    mean = 2 * width // procs
    cap = min(2 * width, (mean + mean // 4 + 7) // 8 * 8)
    fmean = width // procs
    fcap = min(width, (fmean + fmean // 2 + 7) // 8 * 8)
    again = (src_most > cap) | (dest_most > fcap)
    args = (m3, inverse_blocks, info, tuple(first), came, (so, sl, sr), (do, dl, dr))
    out = factor(cap, fcap, *args)

    out = lax.cond(
        again,
        lambda done, *rest: factor(None, None, *rest, done),
        lambda done, *rest: done,
        out,
        *args,
    )
    return out.reshape(matrix.shape)


def solution(mesh):
    return jax.shard_map(
        shards,
        mesh=mesh,
        in_specs=(P(None, "prow", None, None, "pcol", None), P(), P()),
        out_specs=P(None, "prow", None, None, "pcol", None),
        check_vma=False,
    )
```

```python
import functools

import jax
import jax.numpy as jnp
from jax import lax
from jax.experimental import pallas as pl
from jax.experimental.pallas import tpu as pltpu
from jax.sharding import PartitionSpec as P

LANES = 128
CHUNKS = 16
CHAINS = 2
TABLE_AT = 3
TILE = 256
DELIVER_AT = 6
SOLVE_AT = 8
AT_ONCE = 2
AT_LAST = 2
F32 = jnp.float32
BF16 = jnp.bfloat16
ANY = pl.BlockSpec(memory_space=pl.ANY)
VMEM = pl.BlockSpec(memory_space=pltpu.VMEM)
SMEM = pl.BlockSpec(memory_space=pltpu.SMEM)
PARAMS = pltpu.CompilerParams(vmem_limit_bytes=56 << 20)


def cost(nbytes):
    return pl.CostEstimate(flops=0, bytes_accessed=int(nbytes), transcendentals=0)


def split(x):
    high = x.astype(BF16)
    return high, (x - high.astype(F32)).astype(BF16)


def dot3(left, right):
    out = jnp.dot(left[0], right[0], preferred_element_type=F32)
    out += jnp.dot(left[0], right[1], preferred_element_type=F32)
    return out + jnp.dot(left[1], right[0], preferred_element_type=F32)


def upper(packed):
    row = lax.broadcasted_iota(jnp.int32, packed.shape, 0)
    col = lax.broadcasted_iota(jnp.int32, packed.shape, 1)
    return jnp.where(col >= row, packed, 0.0)


def unit_lower(packed):
    row = lax.broadcasted_iota(jnp.int32, packed.shape, 0)
    col = lax.broadcasted_iota(jnp.int32, packed.shape, 1)
    return jnp.where(col < row, packed, jnp.where(col == row, 1.0, 0.0))


def get_block(ref, start, count, groups, block, per):
    parts = [
        ref[pl.ds(start * groups + block * per + h, count, stride=groups), :] for h in range(per)
    ]
    return jnp.concatenate(parts, axis=1)


def put_block(ref, start, count, groups, block, per, value):
    for h in range(per):
        ref[pl.ds(start * groups + block * per + h, count, stride=groups), :] = value[
            :, h * LANES : (h + 1) * LANES
        ]


def panel_copies(info_ref, chips, bufs, c0_ref, c1_ref, sem, act):
    rows = bufs[0].shape[0]
    for h in range(chips):
        for core in range(2):

            @pl.when((info_ref[2] == h) & (info_ref[3] == core))
            def _():
                for n in range(len(bufs) // (2 * chips)):
                    own, sib = bufs[2 * n * chips + h], bufs[(2 * n + 1) * chips + h]
                    first, second = (own, sib) if core == 0 else (sib, own)
                    spot = pl.ds(n * rows, rows)
                    act(pltpu.make_async_copy(first, c0_ref.at[spot], sem.at[2 * n]))
                    act(pltpu.make_async_copy(second, c1_ref.at[spot], sem.at[2 * n + 1]))


def start(copy):
    copy.start()


def wait(copy):
    copy.wait()


def panel(m4, first, count, rows):
    shape = (rows,) + m4.shape[2:]

    def kernel(m_ref, *rest):
        outs, sem = rest[:count], rest[count]
        copies = [
            pltpu.make_async_copy(m_ref.at[pl.ds((first + k) * rows, rows), 0], outs[k], sem.at[k])
            for k in range(count)
        ]
        for copy in copies:
            copy.start()
        for copy in copies:
            copy.wait()

    return pl.pallas_call(
        kernel,
        in_specs=[ANY],
        out_specs=[VMEM] * count,
        out_shape=[jax.ShapeDtypeStruct(shape, F32)] * count,
        scratch_shapes=[pltpu.SemaphoreType.DMA((count,))],
        compiler_params=PARAMS,
        cost_estimate=cost(1 << 18),
        name="panel",
    )(m4)


def collect_kernel(procs, per, info_ref, list_ref, out_list_ref, m_ref, *rest):
    row_ref = rest[0]
    out_refs, head_refs = rest[1 : 1 + procs], rest[1 + procs : 1 + 2 * procs]
    top_ref, sem = rest[1 + 2 * procs :]
    cap = row_ref.shape[0]
    width = top_ref.shape[0]
    fcap = out_refs[0].shape[0]
    top = pltpu.make_async_copy(m_ref.at[pl.ds(0, width)], top_ref, sem.at[0])
    top.start()

    def fetch(k, carry):
        pltpu.make_async_copy(m_ref.at[list_ref[k]], row_ref.at[k], sem.at[1]).start()
        return carry

    lax.fori_loop(0, cap, fetch, 0)
    top.wait()

    @pl.when(info_ref[0] < 2)
    def _():
        for x in range(procs):

            def give(k, carry):
                row = top_ref[out_list_ref[x, k]]
                out_refs[x][k] = row
                head_refs[x][cap + k] = row[0:per]
                return carry

            lax.fori_loop(0, fcap, give, 0, unroll=4)

    pltpu.make_async_copy(row_ref, row_ref, sem.at[1]).wait()

    def keep(k, carry):
        row = row_ref[k, 0:per, :]
        for x in range(procs):
            head_refs[x][k] = row
        return carry

    lax.fori_loop(0, cap, keep, 0, unroll=4)


def collect(info, row_list, out_list, m3, per, width):
    cap = row_list.shape[0]
    procs, fcap = out_list.shape
    groups = m3.shape[1]
    out = jax.ShapeDtypeStruct((fcap, groups, LANES), F32)
    head = jax.ShapeDtypeStruct((cap + fcap, per, LANES), F32)
    outs = pl.pallas_call(
        functools.partial(collect_kernel, procs, per),
        in_specs=[SMEM, SMEM, SMEM, ANY],
        out_specs=[VMEM] * (1 + 2 * procs),
        out_shape=[jax.ShapeDtypeStruct((cap, groups, LANES), F32)] + [out] * procs + [head] * procs,
        scratch_shapes=[
            pltpu.VMEM((width, groups, LANES), F32),
            pltpu.SemaphoreType.DMA((2,)),
        ],
        compiler_params=PARAMS,
        cost_estimate=cost(1 << 18),
        name="collect",
    )(info, row_list, out_list, m3)
    return outs[0], outs[1 : 1 + procs], outs[1 + procs :]


def tables_kernel(procs, cap, width, info_ref, owner_ref, rank_ref, *rest):
    ins = rest[:procs]
    o_ref, buf_ref, sem = rest[procs:]
    fcap = buf_ref.shape[1] - cap
    copies = [
        pltpu.make_async_copy(ins[x], buf_ref.at[info_ref[0] ^ x], sem.at[x]) for x in range(procs)
    ]
    for copy in copies:
        copy.start()
    for copy in copies:
        copy.wait()
    base = jnp.where(info_ref[3] == 0, width, 0)

    def pivot(k, carry):
        o_ref[k] = buf_ref[owner_ref[base + k], rank_ref[base + k]]
        return carry

    lax.fori_loop(0, width, pivot, 0, unroll=4)
    for source in range(2):

        def other(k, carry):
            o_ref[width + source * fcap + k] = buf_ref[source, cap + k]
            return carry

        lax.fori_loop(0, fcap, other, 0, unroll=4)


def tables(info, owner, rank, heads, cap, width, rows):
    procs = len(heads)
    both, per, _ = heads[0].shape
    return pl.pallas_call(
        functools.partial(tables_kernel, procs, cap, width),
        in_specs=[SMEM, SMEM, SMEM] + [ANY] * procs,
        out_specs=VMEM,
        out_shape=jax.ShapeDtypeStruct((rows, per, LANES), F32),
        scratch_shapes=[
            pltpu.VMEM((procs, both, per, LANES), F32),
            pltpu.SemaphoreType.DMA((procs,)),
        ],
        compiler_params=PARAMS,
        cost_estimate=cost(1 << 18),
        name="tables",
    )(info, owner, rank, *heads)


def head_kernel(chips, info_ref, *rest):
    (*bufs, inv_ref, c0_ref, c1_ref, l01_ref, own_ref, w_ref, left_ref, sem) = rest
    width = inv_ref.shape[1]
    per = width // LANES
    me, mc = info_ref[0], info_ref[1]
    panel_copies(info_ref, chips, bufs, c0_ref, c1_ref, sem, start)
    panel_copies(info_ref, chips, bufs, c0_ref, c1_ref, sem, wait)
    z1c0 = get_block(c0_ref, 0, width, per, 0, per)
    g0c1 = get_block(c1_ref, 0, width, per, 0, per)
    one0, one1 = unit_lower(inv_ref[0]), unit_lower(inv_ref[1])
    up0, up1 = upper(inv_ref[0]), upper(inv_ref[1])
    low0, low1, v0, v1 = split(one0), split(one1), split(up0), split(up1)
    l01 = dot3(split(z1c0), v0)
    l01_ref[...] = l01
    u01 = dot3(low0, split(g0c1))
    back = dot3(low1, split(dot3(split(l01), low0)))
    cross = dot3(v0, split(u01))
    crosses = split(cross)
    parts = (
        split(dot3(v0, low0)),
        split(dot3(v1, split(back))),
        split(dot3(v1, low1)),
        crosses,
    )
    for n, part in enumerate(parts):
        for k in range(2):
            w_ref[(2 * n + k) * width : (2 * n + k + 1) * width] = part[k]
    mine = (split(jnp.where(me == 0, one0, -back)), split(jnp.where(me == 0, 0.0, one1)))
    for n, part in enumerate(mine):
        for k in range(2):
            own_ref[(2 * n + k) * width : (2 * n + k + 1) * width] = part[k]
    left_ref[:width] = jnp.where(mc == 0, -up0, dot3(crosses, v1))
    left_ref[width:] = jnp.where(mc == 0, 0.0, -up1)


def head(info, chips, bufs, inv):
    width = inv.shape[1]
    count = len(bufs) // (2 * chips)
    tab = jax.ShapeDtypeStruct((count * bufs[0].shape[0], LANES), F32)
    return pl.pallas_call(
        functools.partial(head_kernel, chips),
        in_specs=[SMEM] + [ANY] * len(bufs) + [VMEM],
        out_specs=[VMEM] * 6,
        out_shape=[
            tab,
            tab,
            jax.ShapeDtypeStruct((width, width), F32),
            jax.ShapeDtypeStruct((4 * width, width), BF16),
            jax.ShapeDtypeStruct((8 * width, width), BF16),
            jax.ShapeDtypeStruct((2 * width, width), F32),
        ],
        scratch_shapes=[pltpu.SemaphoreType.DMA((2 * count,))],
        compiler_params=PARAMS,
        cost_estimate=cost(1 << 20),
        name="head",
    )(info, *bufs, inv)


def solve_kernel(groups, info_ref, owner_ref, rank_ref, *rest):
    g_ref, l01_ref, own_ref, w_ref, left_ref, inv_ref, u_ref, brow_ref, s_ref = rest
    width = l01_ref.shape[0]
    per = width // LANES
    mc, me = info_ref[1], info_ref[4]
    def line_up(k, carry):
        spot = pl.ds(pl.multiple_of(k * groups, groups), groups)
        s_ref[spot, :] = g_ref[owner_ref[k], rank_ref[k]]
        return carry

    lax.fori_loop(0, 2 * width, line_up, 0, unroll=8)

    def pair(ref, n):
        return ref[2 * n * width : (2 * n + 1) * width], ref[(2 * n + 1) * width : (2 * n + 2) * width]

    def keep(block, value, first):
        for n, part in enumerate(split(value)):
            at = 2 * n * width + first
            u_ref[at : at + width, block * width : (block + 1) * width] = part

    for block in range(groups // per):
        g0 = split(get_block(s_ref, 0, width, groups, block, per))
        z1 = split(get_block(s_ref, width, width, groups, block, per))
        w1 = dot3(pair(w_ref, 2), z1) - dot3(pair(w_ref, 1), g0)
        w0 = dot3(pair(w_ref, 0), g0) - dot3(pair(w_ref, 3), split(w1))
        if block == 0:
            w0 = jnp.where(mc < 2, left_ref[:width], w0)
            w1 = jnp.where(mc < 2, left_ref[width:], w1)
        keep(block, w0, 0)
        keep(block, w1, width)

    for holder in range(2):

        @pl.when(me == holder)
        def _():
            def step(block, carry):
                u = dot3(pair(own_ref, 0), split(get_block(s_ref, 0, width, groups, block, per)))
                if holder == 1:
                    z1 = split(get_block(s_ref, width, width, groups, block, per))
                    u += dot3(pair(own_ref, 1), z1)
                put_block(brow_ref, 0, width, groups, block, per, u)
                return carry

            lax.fori_loop(0, groups // per, step, 0)

    @pl.when((mc == 0) & (me == 0))
    def _():
        put_block(brow_ref, 0, width, groups, 0, per, get_block(s_ref, 0, width, groups, 0, per))

    @pl.when((mc == 0) & (me == 1))
    def _():
        put_block(brow_ref, 0, width, groups, 0, per, l01_ref[...])

    @pl.when((mc == 1) & (me == 1))
    def _():
        g0 = split(get_block(s_ref, 0, width, groups, 0, per))
        z1 = get_block(s_ref, width, width, groups, 0, per)
        u0 = split(dot3(split(unit_lower(inv_ref[0])), g0))
        put_block(brow_ref, 0, width, groups, 0, per, z1 - dot3(split(l01_ref[...]), u0))


def solve(info, owner, rank, gathered, l01, own, w, left, inv):
    groups = gathered.shape[2]
    width = l01.shape[0]
    cols = groups * LANES
    return pl.pallas_call(
        functools.partial(solve_kernel, groups),
        in_specs=[SMEM, SMEM, SMEM] + [VMEM] * 6,
        out_specs=[VMEM, VMEM],
        out_shape=[
            jax.ShapeDtypeStruct((4 * width, cols), BF16),
            jax.ShapeDtypeStruct((width * groups, LANES), F32),
        ],
        scratch_shapes=[pltpu.VMEM((2 * width * groups, LANES), F32)],
        compiler_params=PARAMS,
        cost_estimate=cost(1 << 20),
        name="solve",
    )(info, owner, rank, gathered, l01, own, w, left, inv)


def make_bulk(chips, first, tiles, number, groups, width):
    def kernel(info_ref, order_ref, spot_ref, first_ref, *rest):
        bufs = rest[:number]
        m_ref, uhl_ref, f_ref, brow_ref, t0_ref, t1_ref = rest[number : number + 6]
        o_ref, u_ref, moved_ref, row_ref, c0_ref, c1_ref, left_ref = rest[-11:-4]
        c_sem, in_sem, out_sem, sem = rest[-4:]
        each = number // tiles
        count = left_ref.shape[0]
        per = width // LANES
        mc = info_ref[1]
        parts = row_ref.shape[1]
        half = count // parts
        u_copy = pltpu.make_async_copy(uhl_ref, u_ref, sem.at[0])
        f_copy = pltpu.make_async_copy(f_ref, moved_ref, sem.at[1])

        def span(n, part):
            return pl.ds(((first + n) * count + part * half) * groups, half * groups)

        def panels(n, act):
            slot = n % 2
            panel_copies(
                info_ref, chips, bufs[n * each : (n + 1) * each], c0_ref.at[slot], c1_ref.at[slot],
                c_sem.at[slot], act,
            )

        def rows_in(n, part):
            slot = n % 2
            return pltpu.make_async_copy(
                m_ref.at[span(n, part)], row_ref.at[slot, part], in_sem.at[slot, part]
            )

        def store(n, part):
            slot = n % 2
            return pltpu.make_async_copy(
                row_ref.at[slot, part], o_ref.at[span(n, part)], out_sem.at[slot, part]
            )

        panels(0, start)
        f_copy.start()
        u_copy.start()
        for part in range(parts):
            rows_in(0, part).start()
        for n in range(tiles):
            slot = n % 2
            c0, c1 = c0_ref.at[slot], c1_ref.at[slot]
            panels(n, wait)
            if n + 1 < tiles:
                panels(n + 1, start)

            def replace(e, carry):
                k = order_ref[e]
                here = pl.ds((spot_ref[k] - (first + n) * count) * per, per)
                there = pl.ds((width + k) * per, per)
                c0[here, :] = t0_ref[there, :]
                c1[here, :] = t1_ref[there, :]
                return carry

            lax.fori_loop(first_ref[first + n], first_ref[first + n + 1], replace, 0)
            for k, c in enumerate((c0, c1)):
                for part, value in enumerate(split(get_block(c, 0, count, per, 0, per))):
                    left_ref[:, (2 * part + k) * width : (2 * part + k + 1) * width] = value
            if n == 0:
                f_copy.wait()
                u_copy.wait()
            for part in range(parts):
                rows_in(n, part).wait()
                if n + 1 < tiles:
                    if n > 0:
                        store(n - 1, part).wait()
                    rows_in(n + 1, part).start()
                rows = row_ref.at[slot, part]
                base = (first + n) * count + part * half

                def replace_row(e, carry):
                    k = order_ref[e]
                    here = spot_ref[k] - base

                    @pl.when((here >= 0) & (here < half))
                    def _():
                        spot = pl.ds(pl.multiple_of(here * groups, groups), groups)
                        rows[spot, :] = moved_ref[k]

                    return carry

                lax.fori_loop(first_ref[first + n], first_ref[first + n + 1], replace_row, 0)
                high = left_ref[part * half : (part + 1) * half, : 2 * width]
                low = left_ref[part * half : (part + 1) * half, 2 * width :]
                for block in range(groups // per):
                    cols = slice(block * width, (block + 1) * width)
                    acc = dot3((high, low), (u_ref[: 2 * width, cols], u_ref[2 * width :, cols]))
                    old = get_block(rows, 0, half, groups, block, per)
                    if block == 0:
                        old = jnp.where(mc < 2, 0.0, old)
                    put_block(rows, 0, half, groups, block, per, old - acc)
                if base < width:

                    @pl.when(info_ref[0] < 2)
                    def _():
                        many = min(half, width - base) * groups
                        copy = pltpu.make_async_copy(
                            brow_ref.at[pl.ds(base * groups, many)],
                            rows.at[pl.ds(0, many)],
                            sem.at[0],
                        )
                        copy.start()
                        copy.wait()

                store(n, part).start()
        for n in range(max(0, tiles - 2), tiles):
            for part in range(parts):
                store(n, part).wait()

    return kernel


def bulk(info, lists, chips, bufs, tabs, m2, uhl, moved, brow, out, first, tiles):
    groups = moved.shape[1]
    width = uhl.shape[0] // 4
    per = width // LANES
    pieces = len(bufs) // (2 * chips * tiles)
    count = pieces * bufs[0].shape[0] // per
    parts = max(1, count // TILE)
    in_specs = [SMEM] * 4 + [ANY] * (len(bufs) + 4) + [VMEM] * 2
    args = [info, *lists, *bufs, m2, uhl, moved, brow, *tabs]
    aliases = {}
    if out is not None:
        in_specs.append(ANY)
        aliases = {len(args): 0}
        args.append(out)
    panels = pltpu.VMEM((2, count * per, LANES), F32)
    return pl.pallas_call(
        make_bulk(chips, first, tiles, len(bufs), groups, width),
        in_specs=in_specs,
        out_specs=ANY,
        out_shape=jax.ShapeDtypeStruct(m2.shape, F32),
        scratch_shapes=[
            pltpu.VMEM(uhl.shape, BF16),
            pltpu.VMEM(moved.shape, F32),
            pltpu.VMEM((2, parts, count // parts * groups, LANES), F32),
            panels,
            panels,
            pltpu.VMEM((count, 4 * width), BF16),
            pltpu.SemaphoreType.DMA((2, 2 * pieces)),
            pltpu.SemaphoreType.DMA((2, parts)),
            pltpu.SemaphoreType.DMA((2, parts)),
            pltpu.SemaphoreType.DMA((2,)),
        ],
        input_output_aliases=aliases,
        compiler_params=PARAMS,
        cost_estimate=cost(1 << 20),
        name="bulk",
    )(*args)


def fetch_kernel(procs, info_ref, *rest):
    ins = rest[:procs]
    o_ref, sem = rest[procs:]
    rows = o_ref.shape[0] // 2
    for act in (start, wait):
        for source in range(2):
            spot = pl.ds(source * rows, rows)
            for x in range(procs):

                @pl.when((info_ref[0] ^ source) == x)
                def _():
                    act(pltpu.make_async_copy(ins[x], o_ref.at[spot], sem.at[source]))


def fetch(info, displaced):
    rows, groups, _ = displaced[0].shape
    return pl.pallas_call(
        functools.partial(fetch_kernel, len(displaced)),
        in_specs=[SMEM] + [ANY] * len(displaced),
        out_specs=VMEM,
        out_shape=jax.ShapeDtypeStruct((2 * rows, groups, LANES), F32),
        scratch_shapes=[pltpu.SemaphoreType.DMA((2,))],
        compiler_params=PARAMS,
        cost_estimate=cost(1 << 20),
        name="fetch",
    )(info, *displaced)


def plan(pivots, width, procs, me):
    p0, p1 = pivots[0], pivots[1]
    count = jnp.arange(width, dtype=jnp.int32)
    hit = p0[:, None] == p1[None, :]
    back = p0[:, None] == width + count[None, :]
    src1 = jnp.where(hit.any(0), jnp.sum(jnp.where(hit, count[:, None], 0), 0), p1)
    dest0 = jnp.where(
        back.any(1),
        jnp.sum(jnp.where(back, p1[None, :], 0), 1),
        jnp.where(hit.any(1), -1, p0),
    )
    dest1 = jnp.where(back.any(0), -1, p1)
    src = jnp.concatenate([p0, src1])
    dest = jnp.concatenate([dest0, dest1])
    src_owner = src // width % procs
    src_local = src // width // procs * width + src % width
    dest_owner = jnp.where(dest >= 0, dest // width % procs, -1)
    dest_local = dest // width // procs * width + dest % width
    order = jnp.arange(2 * width, dtype=jnp.int32)
    earlier = order[None, :] < order[:, None]
    same_half = (order[None, :] // width) == (order[:, None] // width)
    src_rank = jnp.sum(
        (earlier & (src_owner[None, :] == src_owner[:, None])).astype(jnp.int32), 1
    )
    dest_rank = jnp.sum(
        (earlier & same_half & (dest_owner[None, :] == dest_owner[:, None])).astype(jnp.int32), 1
    )
    src_most = jnp.max(src_rank) + 1
    dest_most = jnp.max(jnp.where(dest >= 0, dest_rank, -1)) + 1
    return src_owner, src_local, src_rank, dest_owner, dest_local, dest_rank, src_most, dest_most


def flip(procs, x):
    return [(s, s ^ x) for s in range(procs)]


def send(value, axis, pairs):
    flat = value.reshape(-1, LANES)
    return lax.ppermute(flat, axis, pairs).reshape(value.shape)


def exchange(cap, fcap, m3, width, info, came1, src, dest):
    per = width // LANES
    procs = lax.axis_size("prow")
    me = info[0]
    src_owner, src_local, src_rank = src
    dest_owner, dest_local, dest_rank = dest

    src_rank = jnp.minimum(src_rank, cap - 1)
    slots = jnp.arange(cap, dtype=jnp.int32)
    mine = (src_owner == me)[None, :] & (src_rank[None, :] == slots[:, None])
    row_list = jnp.max(jnp.where(mine, src_local[None, :], 0), 1)

    fslots = jnp.arange(fcap, dtype=jnp.int32)
    owner2 = dest_owner.reshape(2, width)
    rank2 = dest_rank.reshape(2, width)
    local2 = dest_local.reshape(2, width)
    to = me ^ jnp.arange(procs, dtype=jnp.int32)
    out_owner = jnp.where(me == 0, owner2[0], owner2[1])
    out_rank = jnp.where(me == 0, rank2[0], rank2[1])
    chosen = (out_owner[None, None, :] == to[:, None, None]) & (
        out_rank[None, None, :] == fslots[None, :, None]
    )
    out_list = jnp.sum(jnp.where(chosen, jnp.arange(width, dtype=jnp.int32), 0), 2)
    landing = (owner2[:, None, :] == me) & (rank2[:, None, :] == fslots[None, :, None])
    spots = (jnp.sum(jnp.where(landing, local2[:, None, :] + 1, 0), 2) - 1).reshape(2 * fcap)

    sent, outgoing, heads = collect(info, row_list, out_list, m3, per, width)
    heads = [heads[0]] + [send(heads[x], "prow", flip(procs, x)) for x in range(1, procs)]
    sent, *came1 = lax.optimization_barrier((sent, *came1))
    gathered = lax.all_gather(sent.reshape(-1, LANES), "prow", axis=0, tiled=True)
    gathered = gathered.reshape((procs,) + sent.shape)
    return info, src_owner, src_rank, heads, gathered, outgoing, spots, came1


def deliver(outgoing):
    procs = lax.axis_size("prow")
    return [outgoing[0]] + [
        send(outgoing[x], "prow", [(s, s ^ x) for s in range(2)]) for x in range(1, procs)
    ]


def exchange_any(m3, width, info, src, dest):
    per = width // LANES
    me = info[0]
    src_owner, src_local, _ = src
    dest_owner, dest_local, _ = dest
    rows = jnp.where((src_owner == me)[:, None, None], m3[src_local], 0.0)
    rows = lax.psum(rows.reshape(-1, LANES), "prow").reshape(rows.shape)
    displaced = []
    for source in range(2):
        top = jnp.where(me == source, m3[:width], 0.0)
        displaced.append(lax.psum(top.reshape(-1, LANES), "prow").reshape(top.shape))
    heads = [jnp.concatenate([rows[:, :per], top[:, :per]]) for top in displaced]
    spots = jnp.where(dest_owner == me, dest_local, -1)
    order = jnp.arange(2 * width, dtype=jnp.int32)
    first = jnp.concatenate([jnp.zeros((1,), jnp.int32), info[1:]])
    gathered = rows[None]
    return first, jnp.zeros_like(order), order, heads, gathered, displaced, spots


def factor(cap, fcap, m3, inv, info, first, came1, src, dest, out=None):
    rows, groups, _ = m3.shape
    width = inv.shape[1]
    chips = lax.axis_size("pcol") // 2
    per = width // LANES
    z = info[2]
    m2 = m3.reshape(rows * groups, LANES)
    m4 = m3.reshape(rows, groups // per, per, LANES)
    chunk = rows // CHUNKS
    hop = [(q, q + 2) for q in range(2 * chips - 2)]
    swap = [(q, q ^ 1) for q in range(2 * chips)]
    pieces = list(first) + list(panel(m4, CHAINS, CHUNKS - CHAINS, chunk))

    later = cap is not None
    if cap is None:
        cap, fcap = 2 * width, width
        moves = exchange_any(m3, width, info, src, dest) + (came1,)
    else:
        moves = exchange(cap, fcap, m3, width, info, came1, src, dest)
    seen, owner, rank, heads, gathered, displaced, spots, came1 = moves
    share = -(-(width + 2 * fcap) // (chunk * CHAINS))
    table = tables(seen, owner, rank, heads, cap, width, share * CHAINS * chunk)

    tiles = CHUNKS // CHAINS
    tile_of = jnp.where(spots < 0, tiles, spots // (CHAINS * chunk))
    place = jnp.arange(spots.shape[0], dtype=jnp.int32)
    before = (tile_of[None, :] < tile_of[:, None]) | (
        (tile_of[None, :] == tile_of[:, None]) & (place[None, :] < place[:, None])
    )
    at = jnp.sum(before.astype(jnp.int32), 1)
    order = jnp.sum(jnp.where(at[None, :] == place[:, None], place[None, :], 0), 1)
    starts = jnp.sum(
        (tile_of[None, :] < jnp.arange(tiles + 1, dtype=jnp.int32)[:, None]).astype(jnp.int32), 1
    )
    lists = (order, spots, starts)

    items = [piece.reshape(chunk * per, LANES) for piece in pieces]
    table = table.reshape(share * CHAINS, chunk * per, LANES)
    at = TABLE_AT * CHAINS
    items[at:at] = [table[n] for n in range(share * CHAINS)]
    length = len(items) // CHAINS
    position = [n if n < TABLE_AT else n + share for n in range(tiles)]
    own = [[] for _ in range(CHAINS)]
    sib = [[] for _ in range(CHAINS)]

    def held(t, count=1):
        bufs = []
        for n in range(t, t + count):
            for k in range(CHAINS):
                bufs += own[k][n : n + chips] + sib[k][n : n + chips]
        return bufs

    known = solved = moved = None
    done = 0

    def update(many):
        nonlocal out, done, moved
        if moved is None:
            moved = fetch(seen, deliver(displaced) if later else displaced)
        bufs = []
        for n in range(done, done + many):
            bufs += held(position[n])
        uhl, brow = solved
        out = bulk(info, lists, chips, bufs, known[:2], m2, uhl, moved, brow, out, done, many)
        done += many
        return out

    def work(t):
        nonlocal known, solved, moved, displaced
        if t == DELIVER_AT:
            return displaced if later else []
        if known is None and t >= TABLE_AT + share + chips - 1:
            known = head(info, chips, held(TABLE_AT, share), inv)
            return [known[0]]
        if known is not None and solved is None:
            if t < SOLVE_AT:
                return []
            solved = solve(seen, owner, rank, gathered, *known[2:], inv)
            return [solved[1]]
        ready = [n for n in range(done, tiles) if position[n] + chips < t]
        if solved is not None and ready:
            return [update(min(AT_ONCE, len(ready)))]
        return []

    if out is not None:
        out = out.reshape(m2.shape)
    for t in range(length + chips - 1):
        fresh = work(t)
        if fresh:
            tied = lax.optimization_barrier(tuple(own[k][-1] for k in range(CHAINS)) + tuple(fresh))
            ends = tied[:CHAINS]
            if later and t == DELIVER_AT:
                moved = fetch(seen, deliver(tied[CHAINS:]))
        else:
            ends = [own[k][-1] if t else None for k in range(CHAINS)]
        for k in range(CHAINS):
            cur = items[t * CHAINS + k] if t < length else None
            if t > 0:
                came = came1[k] if t == 1 else send(ends[k], "pcol", hop)
                cur = came if cur is None else jnp.where(z == 0, cur, came)
            own[k].append(cur)
        if t == length + chips - 2 and solved is not None and done < tiles and position[done] + chips <= t:
            ready = sum(position[n] + chips <= t for n in range(done, tiles))
            fresh = update(min(AT_ONCE, ready))
            tied = lax.optimization_barrier(tuple(own[k][-1] for k in range(CHAINS)) + (fresh,))
            for k in range(CHAINS):
                own[k][-1] = tied[k]
            out = tied[-1]
        for k in range(CHAINS):
            sib[k].append(send(own[k][-1], "pcol", swap))
    while solved is None:
        work(length + chips)
    while done < tiles:
        update(min(AT_LAST, tiles - done))
    return out.reshape(rows, groups, LANES)


def shards(matrix, pivots, inverse_blocks):
    row_blocks, _, width, blocks, _, _ = matrix.shape
    procs = lax.axis_size("prow")
    me = lax.axis_index("prow").astype(jnp.int32)
    mc = lax.axis_index("pcol").astype(jnp.int32)
    info = jnp.stack([me, mc, mc // 2, mc % 2, me])
    m3 = matrix.reshape(row_blocks * width, -1, LANES)
    m4 = matrix.reshape(row_blocks * width, blocks, -1, LANES)
    first = panel(m4, 0, CHAINS, row_blocks * width // CHUNKS)
    pivots, first = lax.optimization_barrier((pivots, first))
    flat = [piece.reshape(-1, LANES) for piece in first]
    hop = [(q, q + 2) for q in range(lax.axis_size("pcol") - 2)]
    came = tuple(lax.ppermute(piece, "pcol", hop) for piece in flat)
    so, sl, sr, do, dl, dr, src_most, dest_most = plan(pivots, width, procs, me)
    mean = 2 * width // procs
    cap = min(2 * width, (mean + mean // 4 + 7) // 8 * 8)
    fmean = width // procs
    fcap = min(width, (fmean + fmean // 2 + 7) // 8 * 8)
    again = (src_most > cap) | (dest_most > fcap)
    args = (m3, inverse_blocks, info, tuple(first), came, (so, sl, sr), (do, dl, dr))
    out = factor(cap, fcap, *args)

    out = lax.cond(
        again,
        lambda done, *rest: factor(None, None, *rest, done),
        lambda done, *rest: done,
        out,
        *args,
    )
    return out.reshape(matrix.shape)


def solution(mesh):
    return jax.shard_map(
        shards,
        mesh=mesh,
        in_specs=(P(None, "prow", None, None, "pcol", None), P(), P()),
        out_specs=P(None, "prow", None, None, "pcol", None),
        check_vma=False,
    )
```

```python
import functools

import jax
import jax.numpy as jnp
from jax import lax
from jax.experimental import pallas as pl
from jax.experimental.pallas import tpu as pltpu
from jax.sharding import PartitionSpec as P

LANES = 128
CHUNKS = 16
CHAINS = 2
TABLE_AT = 2
TILE = 256
DELIVER_AT = 5
AT_ONCE = 2
AT_LAST = 2
F32 = jnp.float32
BF16 = jnp.bfloat16
ANY = pl.BlockSpec(memory_space=pl.ANY)
VMEM = pl.BlockSpec(memory_space=pltpu.VMEM)
SMEM = pl.BlockSpec(memory_space=pltpu.SMEM)
PARAMS = pltpu.CompilerParams(vmem_limit_bytes=56 << 20)


def cost(nbytes):
    return pl.CostEstimate(flops=0, bytes_accessed=int(nbytes), transcendentals=0)


def split(x):
    high = x.astype(BF16)
    return high, (x - high.astype(F32)).astype(BF16)


def dot3(left, right):
    out = jnp.dot(left[0], right[0], preferred_element_type=F32)
    out += jnp.dot(left[0], right[1], preferred_element_type=F32)
    return out + jnp.dot(left[1], right[0], preferred_element_type=F32)


def upper(packed):
    row = lax.broadcasted_iota(jnp.int32, packed.shape, 0)
    col = lax.broadcasted_iota(jnp.int32, packed.shape, 1)
    return jnp.where(col >= row, packed, 0.0)


def unit_lower(packed):
    row = lax.broadcasted_iota(jnp.int32, packed.shape, 0)
    col = lax.broadcasted_iota(jnp.int32, packed.shape, 1)
    return jnp.where(col < row, packed, jnp.where(col == row, 1.0, 0.0))


def get_block(ref, start, count, groups, block, per):
    parts = [
        ref[pl.ds(start * groups + block * per + h, count, stride=groups), :] for h in range(per)
    ]
    return jnp.concatenate(parts, axis=1)


def put_block(ref, start, count, groups, block, per, value):
    for h in range(per):
        ref[pl.ds(start * groups + block * per + h, count, stride=groups), :] = value[
            :, h * LANES : (h + 1) * LANES
        ]


def panel_copies(info_ref, chips, bufs, c0_ref, c1_ref, sem, act):
    rows = bufs[0].shape[0]
    for h in range(chips):
        for core in range(2):

            @pl.when((info_ref[2] == h) & (info_ref[3] == core))
            def _():
                for n in range(len(bufs) // (2 * chips)):
                    own, sib = bufs[2 * n * chips + h], bufs[(2 * n + 1) * chips + h]
                    first, second = (own, sib) if core == 0 else (sib, own)
                    spot = pl.ds(n * rows, rows)
                    act(pltpu.make_async_copy(first, c0_ref.at[spot], sem.at[2 * n]))
                    act(pltpu.make_async_copy(second, c1_ref.at[spot], sem.at[2 * n + 1]))


def start(copy):
    copy.start()


def wait(copy):
    copy.wait()


def panel(m4, first, count, rows):
    shape = (rows,) + m4.shape[2:]

    def kernel(m_ref, *rest):
        outs, sem = rest[:count], rest[count]
        copies = [
            pltpu.make_async_copy(m_ref.at[pl.ds((first + k) * rows, rows), 0], outs[k], sem.at[k])
            for k in range(count)
        ]
        for copy in copies:
            copy.start()
        for copy in copies:
            copy.wait()

    return pl.pallas_call(
        kernel,
        in_specs=[ANY],
        out_specs=[VMEM] * count,
        out_shape=[jax.ShapeDtypeStruct(shape, F32)] * count,
        scratch_shapes=[pltpu.SemaphoreType.DMA((count,))],
        compiler_params=PARAMS,
        cost_estimate=cost(1 << 18),
        name="panel",
    )(m4)


def collect_kernel(procs, per, info_ref, list_ref, out_list_ref, m_ref, *rest):
    row_ref = rest[0]
    out_refs, head_refs = rest[1 : 1 + procs], rest[1 + procs : 1 + 2 * procs]
    top_ref, sem = rest[1 + 2 * procs :]
    cap = row_ref.shape[0]
    width = top_ref.shape[0]
    fcap = out_refs[0].shape[0]
    top = pltpu.make_async_copy(m_ref.at[pl.ds(0, width)], top_ref, sem.at[0])
    top.start()

    def fetch(k, carry):
        pltpu.make_async_copy(m_ref.at[list_ref[k]], row_ref.at[k], sem.at[1]).start()
        return carry

    lax.fori_loop(0, cap, fetch, 0)
    top.wait()

    @pl.when(info_ref[0] < 2)
    def _():
        for x in range(procs):

            def give(k, carry):
                row = top_ref[out_list_ref[x, k]]
                out_refs[x][k] = row
                head_refs[x][cap + k] = row[0:per]
                return carry

            lax.fori_loop(0, fcap, give, 0, unroll=4)

    pltpu.make_async_copy(row_ref, row_ref, sem.at[1]).wait()

    def keep(k, carry):
        row = row_ref[k, 0:per, :]
        for x in range(procs):
            head_refs[x][k] = row
        return carry

    lax.fori_loop(0, cap, keep, 0, unroll=4)


def collect(info, row_list, out_list, m3, per, width):
    cap = row_list.shape[0]
    procs, fcap = out_list.shape
    groups = m3.shape[1]
    out = jax.ShapeDtypeStruct((fcap, groups, LANES), F32)
    head = jax.ShapeDtypeStruct((cap + fcap, per, LANES), F32)
    outs = pl.pallas_call(
        functools.partial(collect_kernel, procs, per),
        in_specs=[SMEM, SMEM, SMEM, ANY],
        out_specs=[VMEM] * (1 + 2 * procs),
        out_shape=[jax.ShapeDtypeStruct((cap, groups, LANES), F32)] + [out] * procs + [head] * procs,
        scratch_shapes=[
            pltpu.VMEM((width, groups, LANES), F32),
            pltpu.SemaphoreType.DMA((2,)),
        ],
        compiler_params=PARAMS,
        cost_estimate=cost(1 << 18),
        name="collect",
    )(info, row_list, out_list, m3)
    return outs[0], outs[1 : 1 + procs], outs[1 + procs :]


def tables_kernel(procs, cap, width, info_ref, owner_ref, rank_ref, *rest):
    ins = rest[:procs]
    o_ref, buf_ref, sem = rest[procs:]
    fcap = buf_ref.shape[1] - cap
    copies = [
        pltpu.make_async_copy(ins[x], buf_ref.at[info_ref[0] ^ x], sem.at[x]) for x in range(procs)
    ]
    for copy in copies:
        copy.start()
    for copy in copies:
        copy.wait()
    base = jnp.where(info_ref[3] == 0, width, 0)

    def pivot(k, carry):
        o_ref[k] = buf_ref[owner_ref[base + k], rank_ref[base + k]]
        return carry

    lax.fori_loop(0, width, pivot, 0, unroll=4)
    for source in range(2):

        def other(k, carry):
            o_ref[width + source * fcap + k] = buf_ref[source, cap + k]
            return carry

        lax.fori_loop(0, fcap, other, 0, unroll=4)


def tables(info, owner, rank, heads, cap, width, rows):
    procs = len(heads)
    both, per, _ = heads[0].shape
    return pl.pallas_call(
        functools.partial(tables_kernel, procs, cap, width),
        in_specs=[SMEM, SMEM, SMEM] + [ANY] * procs,
        out_specs=VMEM,
        out_shape=jax.ShapeDtypeStruct((rows, per, LANES), F32),
        scratch_shapes=[
            pltpu.VMEM((procs, both, per, LANES), F32),
            pltpu.SemaphoreType.DMA((procs,)),
        ],
        compiler_params=PARAMS,
        cost_estimate=cost(1 << 18),
        name="tables",
    )(info, owner, rank, *heads)


def head_kernel(chips, info_ref, *rest):
    (*bufs, inv_ref, c0_ref, c1_ref, l01_ref, own_ref, w_ref, left_ref, sem) = rest
    width = inv_ref.shape[1]
    per = width // LANES
    me, mc = info_ref[0], info_ref[1]
    panel_copies(info_ref, chips, bufs, c0_ref, c1_ref, sem, start)
    panel_copies(info_ref, chips, bufs, c0_ref, c1_ref, sem, wait)
    z1c0 = get_block(c0_ref, 0, width, per, 0, per)
    g0c1 = get_block(c1_ref, 0, width, per, 0, per)
    one0, one1 = unit_lower(inv_ref[0]), unit_lower(inv_ref[1])
    up0, up1 = upper(inv_ref[0]), upper(inv_ref[1])
    low0, low1, v0, v1 = split(one0), split(one1), split(up0), split(up1)
    l01 = dot3(split(z1c0), v0)
    l01_ref[...] = l01
    u01 = dot3(low0, split(g0c1))
    back = dot3(low1, split(dot3(split(l01), low0)))
    cross = dot3(v0, split(u01))
    crosses = split(cross)
    parts = (
        split(dot3(v0, low0)),
        split(dot3(v1, split(back))),
        split(dot3(v1, low1)),
        crosses,
    )
    for n, part in enumerate(parts):
        for k in range(2):
            w_ref[(2 * n + k) * width : (2 * n + k + 1) * width] = part[k]
    mine = (split(jnp.where(me == 0, one0, -back)), split(jnp.where(me == 0, 0.0, one1)))
    for n, part in enumerate(mine):
        for k in range(2):
            own_ref[(2 * n + k) * width : (2 * n + k + 1) * width] = part[k]
    left_ref[:width] = jnp.where(mc == 0, -up0, dot3(crosses, v1))
    left_ref[width:] = jnp.where(mc == 0, 0.0, -up1)


def head(info, chips, bufs, inv):
    width = inv.shape[1]
    count = len(bufs) // (2 * chips)
    tab = jax.ShapeDtypeStruct((count * bufs[0].shape[0], LANES), F32)
    return pl.pallas_call(
        functools.partial(head_kernel, chips),
        in_specs=[SMEM] + [ANY] * len(bufs) + [VMEM],
        out_specs=[VMEM] * 6,
        out_shape=[
            tab,
            tab,
            jax.ShapeDtypeStruct((width, width), F32),
            jax.ShapeDtypeStruct((4 * width, width), BF16),
            jax.ShapeDtypeStruct((8 * width, width), BF16),
            jax.ShapeDtypeStruct((2 * width, width), F32),
        ],
        scratch_shapes=[pltpu.SemaphoreType.DMA((2 * count,))],
        compiler_params=PARAMS,
        cost_estimate=cost(1 << 20),
        name="head",
    )(info, *bufs, inv)


def solve_kernel(groups, info_ref, owner_ref, rank_ref, *rest):
    g_ref, l01_ref, own_ref, w_ref, left_ref, inv_ref, u_ref, brow_ref, s_ref = rest
    width = l01_ref.shape[0]
    per = width // LANES
    mc, me = info_ref[1], info_ref[4]
    def line_up(k, carry):
        spot = pl.ds(pl.multiple_of(k * groups, groups), groups)
        s_ref[spot, :] = g_ref[owner_ref[k], rank_ref[k]]
        return carry

    lax.fori_loop(0, 2 * width, line_up, 0, unroll=8)

    def pair(ref, n):
        return ref[2 * n * width : (2 * n + 1) * width], ref[(2 * n + 1) * width : (2 * n + 2) * width]

    def keep(block, value, first):
        for n, part in enumerate(split(value)):
            at = 2 * n * width + first
            u_ref[at : at + width, block * width : (block + 1) * width] = part

    for block in range(groups // per):
        g0 = split(get_block(s_ref, 0, width, groups, block, per))
        z1 = split(get_block(s_ref, width, width, groups, block, per))
        w1 = dot3(pair(w_ref, 2), z1) - dot3(pair(w_ref, 1), g0)
        w0 = dot3(pair(w_ref, 0), g0) - dot3(pair(w_ref, 3), split(w1))
        if block == 0:
            w0 = jnp.where(mc < 2, left_ref[:width], w0)
            w1 = jnp.where(mc < 2, left_ref[width:], w1)
        keep(block, w0, 0)
        keep(block, w1, width)

    for holder in range(2):

        @pl.when(me == holder)
        def _():
            def step(block, carry):
                u = dot3(pair(own_ref, 0), split(get_block(s_ref, 0, width, groups, block, per)))
                if holder == 1:
                    z1 = split(get_block(s_ref, width, width, groups, block, per))
                    u += dot3(pair(own_ref, 1), z1)
                put_block(brow_ref, 0, width, groups, block, per, u)
                return carry

            lax.fori_loop(0, groups // per, step, 0)

    @pl.when((mc == 0) & (me == 0))
    def _():
        put_block(brow_ref, 0, width, groups, 0, per, get_block(s_ref, 0, width, groups, 0, per))

    @pl.when((mc == 0) & (me == 1))
    def _():
        put_block(brow_ref, 0, width, groups, 0, per, l01_ref[...])

    @pl.when((mc == 1) & (me == 1))
    def _():
        g0 = split(get_block(s_ref, 0, width, groups, 0, per))
        z1 = get_block(s_ref, width, width, groups, 0, per)
        u0 = split(dot3(split(unit_lower(inv_ref[0])), g0))
        put_block(brow_ref, 0, width, groups, 0, per, z1 - dot3(split(l01_ref[...]), u0))


def solve(info, owner, rank, gathered, l01, own, w, left, inv):
    groups = gathered.shape[2]
    width = l01.shape[0]
    cols = groups * LANES
    return pl.pallas_call(
        functools.partial(solve_kernel, groups),
        in_specs=[SMEM, SMEM, SMEM] + [VMEM] * 6,
        out_specs=[VMEM, VMEM],
        out_shape=[
            jax.ShapeDtypeStruct((4 * width, cols), BF16),
            jax.ShapeDtypeStruct((width * groups, LANES), F32),
        ],
        scratch_shapes=[pltpu.VMEM((2 * width * groups, LANES), F32)],
        compiler_params=PARAMS,
        cost_estimate=cost(50 << 20),
        name="solve",
    )(info, owner, rank, gathered, l01, own, w, left, inv)


def make_bulk(chips, first, tiles, number, groups, width):
    def kernel(info_ref, order_ref, spot_ref, first_ref, *rest):
        bufs = rest[:number]
        m_ref, uhl_ref, f_ref, brow_ref, t0_ref, t1_ref = rest[number : number + 6]
        o_ref, u_ref, moved_ref, row_ref, c0_ref, c1_ref, left_ref = rest[-11:-4]
        c_sem, in_sem, out_sem, sem = rest[-4:]
        each = number // tiles
        count = left_ref.shape[0]
        per = width // LANES
        mc = info_ref[1]
        parts = row_ref.shape[1]
        half = count // parts
        u_copy = pltpu.make_async_copy(uhl_ref, u_ref, sem.at[0])
        f_copy = pltpu.make_async_copy(f_ref, moved_ref, sem.at[1])

        def span(n, part):
            return pl.ds(((first + n) * count + part * half) * groups, half * groups)

        def panels(n, act):
            slot = n % 2
            panel_copies(
                info_ref, chips, bufs[n * each : (n + 1) * each], c0_ref.at[slot], c1_ref.at[slot],
                c_sem.at[slot], act,
            )

        def rows_in(n, part):
            slot = n % 2
            return pltpu.make_async_copy(
                m_ref.at[span(n, part)], row_ref.at[slot, part], in_sem.at[slot, part]
            )

        def store(n, part):
            slot = n % 2
            return pltpu.make_async_copy(
                row_ref.at[slot, part], o_ref.at[span(n, part)], out_sem.at[slot, part]
            )

        panels(0, start)
        f_copy.start()
        u_copy.start()
        for part in range(parts):
            rows_in(0, part).start()
        for n in range(tiles):
            slot = n % 2
            c0, c1 = c0_ref.at[slot], c1_ref.at[slot]
            panels(n, wait)
            if n + 1 < tiles:
                panels(n + 1, start)

            def replace(e, carry):
                k = order_ref[e]
                here = pl.ds((spot_ref[k] - (first + n) * count) * per, per)
                there = pl.ds((width + k) * per, per)
                c0[here, :] = t0_ref[there, :]
                c1[here, :] = t1_ref[there, :]
                return carry

            lax.fori_loop(first_ref[first + n], first_ref[first + n + 1], replace, 0)
            for k, c in enumerate((c0, c1)):
                for part, value in enumerate(split(get_block(c, 0, count, per, 0, per))):
                    left_ref[:, (2 * part + k) * width : (2 * part + k + 1) * width] = value
            if n == 0:
                f_copy.wait()
                u_copy.wait()
            for part in range(parts):
                rows_in(n, part).wait()
                if n + 1 < tiles:
                    if n > 0:
                        store(n - 1, part).wait()
                    rows_in(n + 1, part).start()
                rows = row_ref.at[slot, part]
                base = (first + n) * count + part * half

                def replace_row(e, carry):
                    k = order_ref[e]
                    here = spot_ref[k] - base

                    @pl.when((here >= 0) & (here < half))
                    def _():
                        spot = pl.ds(pl.multiple_of(here * groups, groups), groups)
                        rows[spot, :] = moved_ref[k]

                    return carry

                lax.fori_loop(first_ref[first + n], first_ref[first + n + 1], replace_row, 0)
                high = left_ref[part * half : (part + 1) * half, : 2 * width]
                low = left_ref[part * half : (part + 1) * half, 2 * width :]
                for block in range(groups // per):
                    cols = slice(block * width, (block + 1) * width)
                    acc = dot3((high, low), (u_ref[: 2 * width, cols], u_ref[2 * width :, cols]))
                    old = get_block(rows, 0, half, groups, block, per)
                    if block == 0:
                        old = jnp.where(mc < 2, 0.0, old)
                    put_block(rows, 0, half, groups, block, per, old - acc)
                if base < width:

                    @pl.when(info_ref[0] < 2)
                    def _():
                        many = min(half, width - base) * groups
                        copy = pltpu.make_async_copy(
                            brow_ref.at[pl.ds(base * groups, many)],
                            rows.at[pl.ds(0, many)],
                            sem.at[0],
                        )
                        copy.start()
                        copy.wait()

                store(n, part).start()
        for n in range(max(0, tiles - 2), tiles):
            for part in range(parts):
                store(n, part).wait()

    return kernel


def bulk(info, lists, chips, bufs, tabs, m2, uhl, moved, brow, out, first, tiles):
    groups = moved.shape[1]
    width = uhl.shape[0] // 4
    per = width // LANES
    pieces = len(bufs) // (2 * chips * tiles)
    count = pieces * bufs[0].shape[0] // per
    parts = max(1, count // TILE)
    in_specs = [SMEM] * 4 + [ANY] * (len(bufs) + 4) + [VMEM] * 2
    args = [info, *lists, *bufs, m2, uhl, moved, brow, *tabs]
    aliases = {}
    if out is not None:
        in_specs.append(ANY)
        aliases = {len(args): 0}
        args.append(out)
    panels = pltpu.VMEM((2, count * per, LANES), F32)
    return pl.pallas_call(
        make_bulk(chips, first, tiles, len(bufs), groups, width),
        in_specs=in_specs,
        out_specs=ANY,
        out_shape=jax.ShapeDtypeStruct(m2.shape, F32),
        scratch_shapes=[
            pltpu.VMEM(uhl.shape, BF16),
            pltpu.VMEM(moved.shape, F32),
            pltpu.VMEM((2, parts, count // parts * groups, LANES), F32),
            panels,
            panels,
            pltpu.VMEM((count, 4 * width), BF16),
            pltpu.SemaphoreType.DMA((2, 2 * pieces)),
            pltpu.SemaphoreType.DMA((2, parts)),
            pltpu.SemaphoreType.DMA((2, parts)),
            pltpu.SemaphoreType.DMA((2,)),
        ],
        input_output_aliases=aliases,
        compiler_params=PARAMS,
        cost_estimate=cost(tiles * (20 << 20)),
        name="bulk",
    )(*args)


def fetch_kernel(procs, info_ref, *rest):
    ins = rest[:procs]
    o_ref, sem = rest[procs:]
    rows = o_ref.shape[0] // 2
    for act in (start, wait):
        for source in range(2):
            spot = pl.ds(source * rows, rows)
            for x in range(procs):

                @pl.when((info_ref[0] ^ source) == x)
                def _():
                    act(pltpu.make_async_copy(ins[x], o_ref.at[spot], sem.at[source]))


def fetch(info, displaced):
    rows, groups, _ = displaced[0].shape
    return pl.pallas_call(
        functools.partial(fetch_kernel, len(displaced)),
        in_specs=[SMEM] + [ANY] * len(displaced),
        out_specs=VMEM,
        out_shape=jax.ShapeDtypeStruct((2 * rows, groups, LANES), F32),
        scratch_shapes=[pltpu.SemaphoreType.DMA((2,))],
        compiler_params=PARAMS,
        cost_estimate=cost(1 << 20),
        name="fetch",
    )(info, *displaced)


def plan(pivots, width, procs, me):
    p0, p1 = pivots[0], pivots[1]
    count = jnp.arange(width, dtype=jnp.int32)
    hit = p0[:, None] == p1[None, :]
    back = p0[:, None] == width + count[None, :]
    src1 = jnp.where(hit.any(0), jnp.sum(jnp.where(hit, count[:, None], 0), 0), p1)
    dest0 = jnp.where(
        back.any(1),
        jnp.sum(jnp.where(back, p1[None, :], 0), 1),
        jnp.where(hit.any(1), -1, p0),
    )
    dest1 = jnp.where(back.any(0), -1, p1)
    src = jnp.concatenate([p0, src1])
    dest = jnp.concatenate([dest0, dest1])
    src_owner = src // width % procs
    src_local = src // width // procs * width + src % width
    dest_owner = jnp.where(dest >= 0, dest // width % procs, -1)
    dest_local = dest // width // procs * width + dest % width
    order = jnp.arange(2 * width, dtype=jnp.int32)
    earlier = order[None, :] < order[:, None]
    same_half = (order[None, :] // width) == (order[:, None] // width)
    src_rank = jnp.sum(
        (earlier & (src_owner[None, :] == src_owner[:, None])).astype(jnp.int32), 1
    )
    dest_rank = jnp.sum(
        (earlier & same_half & (dest_owner[None, :] == dest_owner[:, None])).astype(jnp.int32), 1
    )
    src_most = jnp.max(src_rank) + 1
    dest_most = jnp.max(jnp.where(dest >= 0, dest_rank, -1)) + 1
    return src_owner, src_local, src_rank, dest_owner, dest_local, dest_rank, src_most, dest_most


def flip(procs, x):
    return [(s, s ^ x) for s in range(procs)]


def send(value, axis, pairs):
    flat = value.reshape(-1, LANES)
    return lax.ppermute(flat, axis, pairs).reshape(value.shape)


def exchange(cap, fcap, m3, width, info, came1, src, dest):
    per = width // LANES
    procs = lax.axis_size("prow")
    me = info[0]
    src_owner, src_local, src_rank = src
    dest_owner, dest_local, dest_rank = dest

    src_rank = jnp.minimum(src_rank, cap - 1)
    slots = jnp.arange(cap, dtype=jnp.int32)
    mine = (src_owner == me)[None, :] & (src_rank[None, :] == slots[:, None])
    row_list = jnp.max(jnp.where(mine, src_local[None, :], 0), 1)

    fslots = jnp.arange(fcap, dtype=jnp.int32)
    owner2 = dest_owner.reshape(2, width)
    rank2 = dest_rank.reshape(2, width)
    local2 = dest_local.reshape(2, width)
    to = me ^ jnp.arange(procs, dtype=jnp.int32)
    out_owner = jnp.where(me == 0, owner2[0], owner2[1])
    out_rank = jnp.where(me == 0, rank2[0], rank2[1])
    chosen = (out_owner[None, None, :] == to[:, None, None]) & (
        out_rank[None, None, :] == fslots[None, :, None]
    )
    out_list = jnp.sum(jnp.where(chosen, jnp.arange(width, dtype=jnp.int32), 0), 2)
    landing = (owner2[:, None, :] == me) & (rank2[:, None, :] == fslots[None, :, None])
    spots = (jnp.sum(jnp.where(landing, local2[:, None, :] + 1, 0), 2) - 1).reshape(2 * fcap)

    sent, outgoing, heads = collect(info, row_list, out_list, m3, per, width)
    heads = [heads[0]] + [send(heads[x], "prow", flip(procs, x)) for x in range(1, procs)]
    sent, *came1 = lax.optimization_barrier((sent, *came1))
    gathered = lax.all_gather(sent.reshape(-1, LANES), "prow", axis=0, tiled=True)
    gathered = gathered.reshape((procs,) + sent.shape)
    return info, src_owner, src_rank, heads, gathered, outgoing, spots, came1


def deliver(outgoing):
    procs = lax.axis_size("prow")
    return [outgoing[0]] + [
        send(outgoing[x], "prow", [(s, s ^ x) for s in range(2)]) for x in range(1, procs)
    ]


def exchange_any(m3, width, info, src, dest):
    per = width // LANES
    me = info[0]
    src_owner, src_local, _ = src
    dest_owner, dest_local, _ = dest
    rows = jnp.where((src_owner == me)[:, None, None], m3[src_local], 0.0)
    rows = lax.psum(rows.reshape(-1, LANES), "prow").reshape(rows.shape)
    displaced = []
    for source in range(2):
        top = jnp.where(me == source, m3[:width], 0.0)
        displaced.append(lax.psum(top.reshape(-1, LANES), "prow").reshape(top.shape))
    heads = [jnp.concatenate([rows[:, :per], top[:, :per]]) for top in displaced]
    spots = jnp.where(dest_owner == me, dest_local, -1)
    order = jnp.arange(2 * width, dtype=jnp.int32)
    first = jnp.concatenate([jnp.zeros((1,), jnp.int32), info[1:]])
    gathered = rows[None]
    return first, jnp.zeros_like(order), order, heads, gathered, displaced, spots


def factor(cap, fcap, m3, inv, info, first, came1, src, dest, out=None):
    rows, groups, _ = m3.shape
    width = inv.shape[1]
    chips = lax.axis_size("pcol") // 2
    per = width // LANES
    z = info[2]
    m2 = m3.reshape(rows * groups, LANES)
    m4 = m3.reshape(rows, groups // per, per, LANES)
    chunk = rows // CHUNKS
    hop = [(q, q + 2) for q in range(2 * chips - 2)]
    swap = [(q, q ^ 1) for q in range(2 * chips)]
    pieces = list(first) + list(panel(m4, CHAINS, CHUNKS - CHAINS, chunk))

    later = cap is not None
    if cap is None:
        cap, fcap = 2 * width, width
        moves = exchange_any(m3, width, info, src, dest) + (came1,)
    else:
        moves = exchange(cap, fcap, m3, width, info, came1, src, dest)
    seen, owner, rank, heads, gathered, displaced, spots, came1 = moves
    share = -(-(width + 2 * fcap) // (chunk * CHAINS))
    table = tables(seen, owner, rank, heads, cap, width, share * CHAINS * chunk)

    tiles = CHUNKS // CHAINS
    tile_of = jnp.where(spots < 0, tiles, spots // (CHAINS * chunk))
    place = jnp.arange(spots.shape[0], dtype=jnp.int32)
    before = (tile_of[None, :] < tile_of[:, None]) | (
        (tile_of[None, :] == tile_of[:, None]) & (place[None, :] < place[:, None])
    )
    at = jnp.sum(before.astype(jnp.int32), 1)
    order = jnp.sum(jnp.where(at[None, :] == place[:, None], place[None, :], 0), 1)
    starts = jnp.sum(
        (tile_of[None, :] < jnp.arange(tiles + 1, dtype=jnp.int32)[:, None]).astype(jnp.int32), 1
    )
    lists = (order, spots, starts)

    items = [piece.reshape(chunk * per, LANES) for piece in pieces]
    table = table.reshape(share * CHAINS, chunk * per, LANES)
    at = TABLE_AT * CHAINS
    items[at:at] = [table[n] for n in range(share * CHAINS)]
    length = len(items) // CHAINS
    position = [n if n < TABLE_AT else n + share for n in range(tiles)]
    own = [[] for _ in range(CHAINS)]
    sib = [[] for _ in range(CHAINS)]

    def held(t, count=1):
        bufs = []
        for n in range(t, t + count):
            for k in range(CHAINS):
                bufs += own[k][n : n + chips] + sib[k][n : n + chips]
        return bufs

    known = solved = moved = None
    done = 0

    def update(many):
        nonlocal out, done, moved
        if moved is None:
            moved = fetch(seen, deliver(displaced) if later else displaced)
        bufs = []
        for n in range(done, done + many):
            bufs += held(position[n])
        uhl, brow = solved
        out = bulk(info, lists, chips, bufs, known[:2], m2, uhl, moved, brow, out, done, many)
        done += many
        return out

    def work(t):
        nonlocal known, solved, moved, displaced
        if later and t == DELIVER_AT:
            return list(displaced)
        if solved is None and t >= TABLE_AT + share + chips - 1:
            known = head(info, chips, held(TABLE_AT, share), inv)
            solved = solve(seen, owner, rank, gathered, *known[2:], inv)
            return [solved[1]]
        ready = [n for n in range(done, tiles) if position[n] + chips < t]
        if solved is not None and ready:
            return [update(min(AT_ONCE, len(ready)))]
        return []

    if out is not None:
        out = out.reshape(m2.shape)
    for t in range(length + chips - 1):
        fresh = work(t)
        if fresh:
            tied = lax.optimization_barrier(tuple(own[k][-1] for k in range(CHAINS)) + tuple(fresh))
            ends = tied[:CHAINS]
            if later and t == DELIVER_AT:
                moved = fetch(seen, deliver(tied[CHAINS:]))
        else:
            ends = [own[k][-1] if t else None for k in range(CHAINS)]
        for k in range(CHAINS):
            cur = items[t * CHAINS + k] if t < length else None
            if t > 0:
                came = came1[k] if t == 1 else send(ends[k], "pcol", hop)
                cur = came if cur is None else jnp.where(z == 0, cur, came)
            own[k].append(cur)
        if t == length + chips - 2 and solved is not None and done < tiles and position[done] + chips <= t:
            ready = sum(position[n] + chips <= t for n in range(done, tiles))
            fresh = update(min(AT_ONCE, ready))
            tied = lax.optimization_barrier(tuple(own[k][-1] for k in range(CHAINS)) + (fresh,))
            for k in range(CHAINS):
                own[k][-1] = tied[k]
            out = tied[-1]
        for k in range(CHAINS):
            sib[k].append(send(own[k][-1], "pcol", swap))
    while solved is None:
        work(length + chips)
    while done < tiles:
        update(min(AT_LAST, tiles - done))
    return out.reshape(rows, groups, LANES)


def shards(matrix, pivots, inverse_blocks):
    row_blocks, _, width, blocks, _, _ = matrix.shape
    procs = lax.axis_size("prow")
    me = lax.axis_index("prow").astype(jnp.int32)
    mc = lax.axis_index("pcol").astype(jnp.int32)
    info = jnp.stack([me, mc, mc // 2, mc % 2, me])
    m3 = matrix.reshape(row_blocks * width, -1, LANES)
    m4 = matrix.reshape(row_blocks * width, blocks, -1, LANES)
    first = panel(m4, 0, CHAINS, row_blocks * width // CHUNKS)
    pivots, first = lax.optimization_barrier((pivots, first))
    flat = [piece.reshape(-1, LANES) for piece in first]
    hop = [(q, q + 2) for q in range(lax.axis_size("pcol") - 2)]
    came = tuple(lax.ppermute(piece, "pcol", hop) for piece in flat)
    so, sl, sr, do, dl, dr, src_most, dest_most = plan(pivots, width, procs, me)
    mean = 2 * width // procs
    cap = min(2 * width, (mean + mean // 4 + 7) // 8 * 8)
    fmean = width // procs
    fcap = min(width, (fmean + fmean // 2 + 7) // 8 * 8)
    again = (src_most > cap) | (dest_most > fcap)
    args = (m3, inverse_blocks, info, tuple(first), came, (so, sl, sr), (do, dl, dr))
    out = factor(cap, fcap, *args)

    out = lax.cond(
        again,
        lambda done, *rest: factor(None, None, *rest, done),
        lambda done, *rest: done,
        out,
        *args,
    )
    return out.reshape(matrix.shape)


def solution(mesh):
    return jax.shard_map(
        shards,
        mesh=mesh,
        in_specs=(P(None, "prow", None, None, "pcol", None), P(), P()),
        out_specs=P(None, "prow", None, None, "pcol", None),
        check_vma=False,
    )
```

```python
import functools

import jax
import jax.numpy as jnp
from jax import lax
from jax.experimental import pallas as pl
from jax.experimental.pallas import tpu as pltpu
from jax.sharding import PartitionSpec as P

LANES = 128
CHUNKS = 16
CHAINS = 2
TABLE_AT = 2
TILE = 256
DELIVER_AT = 5
SOLVE_AFTER = 3
AT_ONCE = 4
AT_LAST = 4
F32 = jnp.float32
BF16 = jnp.bfloat16
ANY = pl.BlockSpec(memory_space=pl.ANY)
VMEM = pl.BlockSpec(memory_space=pltpu.VMEM)
SMEM = pl.BlockSpec(memory_space=pltpu.SMEM)
PARAMS = pltpu.CompilerParams(vmem_limit_bytes=56 << 20)


def cost(nbytes):
    return pl.CostEstimate(flops=0, bytes_accessed=int(nbytes), transcendentals=0)


def split(x):
    high = x.astype(BF16)
    return high, (x - high.astype(F32)).astype(BF16)


def dot3(left, right):
    out = jnp.dot(left[0], right[0], preferred_element_type=F32)
    out += jnp.dot(left[0], right[1], preferred_element_type=F32)
    return out + jnp.dot(left[1], right[0], preferred_element_type=F32)


def upper(packed):
    row = lax.broadcasted_iota(jnp.int32, packed.shape, 0)
    col = lax.broadcasted_iota(jnp.int32, packed.shape, 1)
    return jnp.where(col >= row, packed, 0.0)


def unit_lower(packed):
    row = lax.broadcasted_iota(jnp.int32, packed.shape, 0)
    col = lax.broadcasted_iota(jnp.int32, packed.shape, 1)
    return jnp.where(col < row, packed, jnp.where(col == row, 1.0, 0.0))


def get_block(ref, start, count, groups, block, per):
    parts = [
        ref[pl.ds(start * groups + block * per + h, count, stride=groups), :] for h in range(per)
    ]
    return jnp.concatenate(parts, axis=1)


def put_block(ref, start, count, groups, block, per, value):
    for h in range(per):
        ref[pl.ds(start * groups + block * per + h, count, stride=groups), :] = value[
            :, h * LANES : (h + 1) * LANES
        ]


def panel_copies(info_ref, chips, bufs, c0_ref, c1_ref, sem, act):
    rows = bufs[0].shape[0]
    for h in range(chips):
        for core in range(2):

            @pl.when((info_ref[2] == h) & (info_ref[3] == core))
            def _():
                for n in range(len(bufs) // (2 * chips)):
                    own, sib = bufs[2 * n * chips + h], bufs[(2 * n + 1) * chips + h]
                    first, second = (own, sib) if core == 0 else (sib, own)
                    spot = pl.ds(n * rows, rows)
                    act(pltpu.make_async_copy(first, c0_ref.at[spot], sem.at[2 * n]))
                    act(pltpu.make_async_copy(second, c1_ref.at[spot], sem.at[2 * n + 1]))


def start(copy):
    copy.start()


def wait(copy):
    copy.wait()


def panel(m4, first, count, rows):
    shape = (rows,) + m4.shape[2:]

    def kernel(m_ref, *rest):
        outs, sem = rest[:count], rest[count]
        copies = [
            pltpu.make_async_copy(m_ref.at[pl.ds((first + k) * rows, rows), 0], outs[k], sem.at[k])
            for k in range(count)
        ]
        for copy in copies:
            copy.start()
        for copy in copies:
            copy.wait()

    return pl.pallas_call(
        kernel,
        in_specs=[ANY],
        out_specs=[VMEM] * count,
        out_shape=[jax.ShapeDtypeStruct(shape, F32)] * count,
        scratch_shapes=[pltpu.SemaphoreType.DMA((count,))],
        compiler_params=PARAMS,
        cost_estimate=cost(1 << 18),
        name="panel",
    )(m4)


def collect_kernel(procs, per, info_ref, list_ref, out_list_ref, m_ref, *rest):
    row_ref = rest[0]
    out_refs, head_refs = rest[1 : 1 + procs], rest[1 + procs : 1 + 2 * procs]
    top_ref, sem = rest[1 + 2 * procs :]
    cap = row_ref.shape[0]
    width = top_ref.shape[0]
    fcap = out_refs[0].shape[0]
    top = pltpu.make_async_copy(m_ref.at[pl.ds(0, width)], top_ref, sem.at[0])
    top.start()

    def fetch(k, carry):
        pltpu.make_async_copy(m_ref.at[list_ref[k]], row_ref.at[k], sem.at[1]).start()
        return carry

    lax.fori_loop(0, cap, fetch, 0)
    top.wait()

    @pl.when(info_ref[0] < 2)
    def _():
        for x in range(procs):

            def give(k, carry):
                row = top_ref[out_list_ref[x, k]]
                out_refs[x][k] = row
                head_refs[x][cap + k] = row[0:per]
                return carry

            lax.fori_loop(0, fcap, give, 0, unroll=4)

    pltpu.make_async_copy(row_ref, row_ref, sem.at[1]).wait()

    def keep(k, carry):
        row = row_ref[k, 0:per, :]
        for x in range(procs):
            head_refs[x][k] = row
        return carry

    lax.fori_loop(0, cap, keep, 0, unroll=4)


def collect(info, row_list, out_list, m3, per, width):
    cap = row_list.shape[0]
    procs, fcap = out_list.shape
    groups = m3.shape[1]
    out = jax.ShapeDtypeStruct((fcap, groups, LANES), F32)
    head = jax.ShapeDtypeStruct((cap + fcap, per, LANES), F32)
    outs = pl.pallas_call(
        functools.partial(collect_kernel, procs, per),
        in_specs=[SMEM, SMEM, SMEM, ANY],
        out_specs=[VMEM] * (1 + 2 * procs),
        out_shape=[jax.ShapeDtypeStruct((cap, groups, LANES), F32)] + [out] * procs + [head] * procs,
        scratch_shapes=[
            pltpu.VMEM((width, groups, LANES), F32),
            pltpu.SemaphoreType.DMA((2,)),
        ],
        compiler_params=PARAMS,
        cost_estimate=cost(1 << 18),
        name="collect",
    )(info, row_list, out_list, m3)
    return outs[0], outs[1 : 1 + procs], outs[1 + procs :]


def tables_kernel(procs, cap, width, info_ref, owner_ref, rank_ref, *rest):
    ins = rest[:procs]
    o_ref, buf_ref, sem = rest[procs:]
    fcap = buf_ref.shape[1] - cap
    copies = [
        pltpu.make_async_copy(ins[x], buf_ref.at[info_ref[0] ^ x], sem.at[x]) for x in range(procs)
    ]
    for copy in copies:
        copy.start()
    for copy in copies:
        copy.wait()
    base = jnp.where(info_ref[3] == 0, width, 0)

    def pivot(k, carry):
        o_ref[k] = buf_ref[owner_ref[base + k], rank_ref[base + k]]
        return carry

    lax.fori_loop(0, width, pivot, 0, unroll=4)
    for source in range(2):

        def other(k, carry):
            o_ref[width + source * fcap + k] = buf_ref[source, cap + k]
            return carry

        lax.fori_loop(0, fcap, other, 0, unroll=4)


def tables(info, owner, rank, heads, cap, width, rows):
    procs = len(heads)
    both, per, _ = heads[0].shape
    return pl.pallas_call(
        functools.partial(tables_kernel, procs, cap, width),
        in_specs=[SMEM, SMEM, SMEM] + [ANY] * procs,
        out_specs=VMEM,
        out_shape=jax.ShapeDtypeStruct((rows, per, LANES), F32),
        scratch_shapes=[
            pltpu.VMEM((procs, both, per, LANES), F32),
            pltpu.SemaphoreType.DMA((procs,)),
        ],
        compiler_params=PARAMS,
        cost_estimate=cost(1 << 18),
        name="tables",
    )(info, owner, rank, *heads)


def head_kernel(chips, info_ref, *rest):
    (*bufs, inv_ref, c0_ref, c1_ref, l01_ref, own_ref, w_ref, left_ref, sem) = rest
    width = inv_ref.shape[1]
    per = width // LANES
    me, mc = info_ref[0], info_ref[1]
    panel_copies(info_ref, chips, bufs, c0_ref, c1_ref, sem, start)
    panel_copies(info_ref, chips, bufs, c0_ref, c1_ref, sem, wait)
    z1c0 = get_block(c0_ref, 0, width, per, 0, per)
    g0c1 = get_block(c1_ref, 0, width, per, 0, per)
    one0, one1 = unit_lower(inv_ref[0]), unit_lower(inv_ref[1])
    up0, up1 = upper(inv_ref[0]), upper(inv_ref[1])
    low0, low1, v0, v1 = split(one0), split(one1), split(up0), split(up1)
    l01 = dot3(split(z1c0), v0)
    l01_ref[...] = l01
    u01 = dot3(low0, split(g0c1))
    back = dot3(low1, split(dot3(split(l01), low0)))
    cross = dot3(v0, split(u01))
    crosses = split(cross)
    parts = (
        split(dot3(v0, low0)),
        split(dot3(v1, split(back))),
        split(dot3(v1, low1)),
        crosses,
    )
    for n, part in enumerate(parts):
        for k in range(2):
            w_ref[(2 * n + k) * width : (2 * n + k + 1) * width] = part[k]
    mine = (split(jnp.where(me == 0, one0, -back)), split(jnp.where(me == 0, 0.0, one1)))
    for n, part in enumerate(mine):
        for k in range(2):
            own_ref[(2 * n + k) * width : (2 * n + k + 1) * width] = part[k]
    left_ref[:width] = jnp.where(mc == 0, -up0, dot3(crosses, v1))
    left_ref[width:] = jnp.where(mc == 0, 0.0, -up1)


def head(info, chips, bufs, inv):
    width = inv.shape[1]
    count = len(bufs) // (2 * chips)
    tab = jax.ShapeDtypeStruct((count * bufs[0].shape[0], LANES), F32)
    return pl.pallas_call(
        functools.partial(head_kernel, chips),
        in_specs=[SMEM] + [ANY] * len(bufs) + [VMEM],
        out_specs=[VMEM] * 6,
        out_shape=[
            tab,
            tab,
            jax.ShapeDtypeStruct((width, width), F32),
            jax.ShapeDtypeStruct((4 * width, width), BF16),
            jax.ShapeDtypeStruct((8 * width, width), BF16),
            jax.ShapeDtypeStruct((2 * width, width), F32),
        ],
        scratch_shapes=[pltpu.SemaphoreType.DMA((2 * count,))],
        compiler_params=PARAMS,
        cost_estimate=cost(1 << 20),
        name="head",
    )(info, *bufs, inv)


def solve_kernel(groups, info_ref, owner_ref, rank_ref, *rest):
    g_ref, l01_ref, own_ref, w_ref, left_ref, inv_ref, u_ref, brow_ref, s_ref = rest
    width = l01_ref.shape[0]
    per = width // LANES
    mc, me = info_ref[1], info_ref[4]
    def line_up(k, carry):
        spot = pl.ds(pl.multiple_of(k * groups, groups), groups)
        s_ref[spot, :] = g_ref[owner_ref[k], rank_ref[k]]
        return carry

    lax.fori_loop(0, 2 * width, line_up, 0, unroll=8)

    def pair(ref, n):
        return ref[2 * n * width : (2 * n + 1) * width], ref[(2 * n + 1) * width : (2 * n + 2) * width]

    def keep(block, value, first):
        for n, part in enumerate(split(value)):
            at = 2 * n * width + first
            u_ref[at : at + width, block * width : (block + 1) * width] = part

    for block in range(groups // per):
        g0 = split(get_block(s_ref, 0, width, groups, block, per))
        z1 = split(get_block(s_ref, width, width, groups, block, per))
        w1 = dot3(pair(w_ref, 2), z1) - dot3(pair(w_ref, 1), g0)
        w0 = dot3(pair(w_ref, 0), g0) - dot3(pair(w_ref, 3), split(w1))
        if block == 0:
            w0 = jnp.where(mc < 2, left_ref[:width], w0)
            w1 = jnp.where(mc < 2, left_ref[width:], w1)
        keep(block, w0, 0)
        keep(block, w1, width)

    for holder in range(2):

        @pl.when(me == holder)
        def _():
            def step(block, carry):
                u = dot3(pair(own_ref, 0), split(get_block(s_ref, 0, width, groups, block, per)))
                if holder == 1:
                    z1 = split(get_block(s_ref, width, width, groups, block, per))
                    u += dot3(pair(own_ref, 1), z1)
                put_block(brow_ref, 0, width, groups, block, per, u)
                return carry

            lax.fori_loop(0, groups // per, step, 0)

    @pl.when((mc == 0) & (me == 0))
    def _():
        put_block(brow_ref, 0, width, groups, 0, per, get_block(s_ref, 0, width, groups, 0, per))

    @pl.when((mc == 0) & (me == 1))
    def _():
        put_block(brow_ref, 0, width, groups, 0, per, l01_ref[...])

    @pl.when((mc == 1) & (me == 1))
    def _():
        g0 = split(get_block(s_ref, 0, width, groups, 0, per))
        z1 = get_block(s_ref, width, width, groups, 0, per)
        u0 = split(dot3(split(unit_lower(inv_ref[0])), g0))
        put_block(brow_ref, 0, width, groups, 0, per, z1 - dot3(split(l01_ref[...]), u0))


def solve(info, owner, rank, gathered, l01, own, w, left, inv):
    groups = gathered.shape[2]
    width = l01.shape[0]
    cols = groups * LANES
    return pl.pallas_call(
        functools.partial(solve_kernel, groups),
        in_specs=[SMEM, SMEM, SMEM] + [VMEM] * 6,
        out_specs=[VMEM, VMEM],
        out_shape=[
            jax.ShapeDtypeStruct((4 * width, cols), BF16),
            jax.ShapeDtypeStruct((width * groups, LANES), F32),
        ],
        scratch_shapes=[pltpu.VMEM((2 * width * groups, LANES), F32)],
        compiler_params=PARAMS,
        cost_estimate=cost(50 << 20),
        name="solve",
    )(info, owner, rank, gathered, l01, own, w, left, inv)


def make_bulk(chips, first, tiles, number, groups, width):
    def kernel(info_ref, order_ref, spot_ref, first_ref, *rest):
        bufs = rest[:number]
        m_ref, uhl_ref, f_ref, brow_ref, t0_ref, t1_ref = rest[number : number + 6]
        o_ref, u_ref, moved_ref, row_ref, c0_ref, c1_ref, left_ref = rest[-11:-4]
        c_sem, in_sem, out_sem, sem = rest[-4:]
        each = number // tiles
        count = left_ref.shape[0]
        per = width // LANES
        mc = info_ref[1]
        parts = row_ref.shape[1]
        half = count // parts
        u_copy = pltpu.make_async_copy(uhl_ref, u_ref, sem.at[0])
        f_copy = pltpu.make_async_copy(f_ref, moved_ref, sem.at[1])

        def span(n, part):
            return pl.ds(((first + n) * count + part * half) * groups, half * groups)

        def panels(n, act):
            slot = n % 2
            panel_copies(
                info_ref, chips, bufs[n * each : (n + 1) * each], c0_ref.at[slot], c1_ref.at[slot],
                c_sem.at[slot], act,
            )

        def rows_in(n, part):
            slot = n % 2
            return pltpu.make_async_copy(
                m_ref.at[span(n, part)], row_ref.at[slot, part], in_sem.at[slot, part]
            )

        def store(n, part):
            slot = n % 2
            return pltpu.make_async_copy(
                row_ref.at[slot, part], o_ref.at[span(n, part)], out_sem.at[slot, part]
            )

        panels(0, start)
        f_copy.start()
        u_copy.start()
        for part in range(parts):
            rows_in(0, part).start()
        for n in range(tiles):
            slot = n % 2
            c0, c1 = c0_ref.at[slot], c1_ref.at[slot]
            panels(n, wait)
            if n + 1 < tiles:
                panels(n + 1, start)

            def replace(e, carry):
                k = order_ref[e]
                here = pl.ds((spot_ref[k] - (first + n) * count) * per, per)
                there = pl.ds((width + k) * per, per)
                c0[here, :] = t0_ref[there, :]
                c1[here, :] = t1_ref[there, :]
                return carry

            lax.fori_loop(first_ref[first + n], first_ref[first + n + 1], replace, 0)
            for k, c in enumerate((c0, c1)):
                for part, value in enumerate(split(get_block(c, 0, count, per, 0, per))):
                    left_ref[:, (2 * part + k) * width : (2 * part + k + 1) * width] = value
            if n == 0:
                f_copy.wait()
                u_copy.wait()
            for part in range(parts):
                rows_in(n, part).wait()
                if n + 1 < tiles:
                    if n > 0:
                        store(n - 1, part).wait()
                    rows_in(n + 1, part).start()
                rows = row_ref.at[slot, part]
                base = (first + n) * count + part * half

                def replace_row(e, carry):
                    k = order_ref[e]
                    here = spot_ref[k] - base

                    @pl.when((here >= 0) & (here < half))
                    def _():
                        spot = pl.ds(pl.multiple_of(here * groups, groups), groups)
                        rows[spot, :] = moved_ref[k]

                    return carry

                lax.fori_loop(first_ref[first + n], first_ref[first + n + 1], replace_row, 0)
                high = left_ref[part * half : (part + 1) * half, : 2 * width]
                low = left_ref[part * half : (part + 1) * half, 2 * width :]
                for block in range(groups // per):
                    cols = slice(block * width, (block + 1) * width)
                    acc = dot3((high, low), (u_ref[: 2 * width, cols], u_ref[2 * width :, cols]))
                    old = get_block(rows, 0, half, groups, block, per)
                    if block == 0:
                        old = jnp.where(mc < 2, 0.0, old)
                    put_block(rows, 0, half, groups, block, per, old - acc)
                if base < width:

                    @pl.when(info_ref[0] < 2)
                    def _():
                        many = min(half, width - base) * groups
                        copy = pltpu.make_async_copy(
                            brow_ref.at[pl.ds(base * groups, many)],
                            rows.at[pl.ds(0, many)],
                            sem.at[0],
                        )
                        copy.start()
                        copy.wait()

                store(n, part).start()
        for n in range(max(0, tiles - 2), tiles):
            for part in range(parts):
                store(n, part).wait()

    return kernel


def bulk(info, lists, chips, bufs, tabs, m2, uhl, moved, brow, out, first, tiles):
    groups = moved.shape[1]
    width = uhl.shape[0] // 4
    per = width // LANES
    pieces = len(bufs) // (2 * chips * tiles)
    count = pieces * bufs[0].shape[0] // per
    parts = max(1, count // TILE)
    in_specs = [SMEM] * 4 + [ANY] * (len(bufs) + 4) + [VMEM] * 2
    args = [info, *lists, *bufs, m2, uhl, moved, brow, *tabs]
    aliases = {}
    if out is not None:
        in_specs.append(ANY)
        aliases = {len(args): 0}
        args.append(out)
    panels = pltpu.VMEM((2, count * per, LANES), F32)
    return pl.pallas_call(
        make_bulk(chips, first, tiles, len(bufs), groups, width),
        in_specs=in_specs,
        out_specs=ANY,
        out_shape=jax.ShapeDtypeStruct(m2.shape, F32),
        scratch_shapes=[
            pltpu.VMEM(uhl.shape, BF16),
            pltpu.VMEM(moved.shape, F32),
            pltpu.VMEM((2, parts, count // parts * groups, LANES), F32),
            panels,
            panels,
            pltpu.VMEM((count, 4 * width), BF16),
            pltpu.SemaphoreType.DMA((2, 2 * pieces)),
            pltpu.SemaphoreType.DMA((2, parts)),
            pltpu.SemaphoreType.DMA((2, parts)),
            pltpu.SemaphoreType.DMA((2,)),
        ],
        input_output_aliases=aliases,
        compiler_params=PARAMS,
        cost_estimate=cost(tiles * (20 << 20)),
        name="bulk",
    )(*args)


def fetch_kernel(procs, info_ref, *rest):
    ins = rest[:procs]
    o_ref, sem = rest[procs:]
    rows = o_ref.shape[0] // 2
    for act in (start, wait):
        for source in range(2):
            spot = pl.ds(source * rows, rows)
            for x in range(procs):

                @pl.when((info_ref[0] ^ source) == x)
                def _():
                    act(pltpu.make_async_copy(ins[x], o_ref.at[spot], sem.at[source]))


def fetch(info, displaced):
    rows, groups, _ = displaced[0].shape
    return pl.pallas_call(
        functools.partial(fetch_kernel, len(displaced)),
        in_specs=[SMEM] + [ANY] * len(displaced),
        out_specs=VMEM,
        out_shape=jax.ShapeDtypeStruct((2 * rows, groups, LANES), F32),
        scratch_shapes=[pltpu.SemaphoreType.DMA((2,))],
        compiler_params=PARAMS,
        cost_estimate=cost(1 << 20),
        name="fetch",
    )(info, *displaced)


def plan(pivots, width, procs, me):
    p0, p1 = pivots[0], pivots[1]
    count = jnp.arange(width, dtype=jnp.int32)
    hit = p0[:, None] == p1[None, :]
    back = p0[:, None] == width + count[None, :]
    src1 = jnp.where(hit.any(0), jnp.sum(jnp.where(hit, count[:, None], 0), 0), p1)
    dest0 = jnp.where(
        back.any(1),
        jnp.sum(jnp.where(back, p1[None, :], 0), 1),
        jnp.where(hit.any(1), -1, p0),
    )
    dest1 = jnp.where(back.any(0), -1, p1)
    src = jnp.concatenate([p0, src1])
    dest = jnp.concatenate([dest0, dest1])
    src_owner = src // width % procs
    src_local = src // width // procs * width + src % width
    dest_owner = jnp.where(dest >= 0, dest // width % procs, -1)
    dest_local = dest // width // procs * width + dest % width
    order = jnp.arange(2 * width, dtype=jnp.int32)
    earlier = order[None, :] < order[:, None]
    same_half = (order[None, :] // width) == (order[:, None] // width)
    src_rank = jnp.sum(
        (earlier & (src_owner[None, :] == src_owner[:, None])).astype(jnp.int32), 1
    )
    dest_rank = jnp.sum(
        (earlier & same_half & (dest_owner[None, :] == dest_owner[:, None])).astype(jnp.int32), 1
    )
    src_most = jnp.max(src_rank) + 1
    dest_most = jnp.max(jnp.where(dest >= 0, dest_rank, -1)) + 1
    return src_owner, src_local, src_rank, dest_owner, dest_local, dest_rank, src_most, dest_most


def flip(procs, x):
    return [(s, s ^ x) for s in range(procs)]


def send(value, axis, pairs):
    flat = value.reshape(-1, LANES)
    return lax.ppermute(flat, axis, pairs).reshape(value.shape)


def exchange(cap, fcap, m3, width, info, came1, src, dest):
    per = width // LANES
    procs = lax.axis_size("prow")
    me = info[0]
    src_owner, src_local, src_rank = src
    dest_owner, dest_local, dest_rank = dest

    src_rank = jnp.minimum(src_rank, cap - 1)
    slots = jnp.arange(cap, dtype=jnp.int32)
    mine = (src_owner == me)[None, :] & (src_rank[None, :] == slots[:, None])
    row_list = jnp.max(jnp.where(mine, src_local[None, :], 0), 1)

    fslots = jnp.arange(fcap, dtype=jnp.int32)
    owner2 = dest_owner.reshape(2, width)
    rank2 = dest_rank.reshape(2, width)
    local2 = dest_local.reshape(2, width)
    to = me ^ jnp.arange(procs, dtype=jnp.int32)
    out_owner = jnp.where(me == 0, owner2[0], owner2[1])
    out_rank = jnp.where(me == 0, rank2[0], rank2[1])
    chosen = (out_owner[None, None, :] == to[:, None, None]) & (
        out_rank[None, None, :] == fslots[None, :, None]
    )
    out_list = jnp.sum(jnp.where(chosen, jnp.arange(width, dtype=jnp.int32), 0), 2)
    landing = (owner2[:, None, :] == me) & (rank2[:, None, :] == fslots[None, :, None])
    spots = (jnp.sum(jnp.where(landing, local2[:, None, :] + 1, 0), 2) - 1).reshape(2 * fcap)

    sent, outgoing, heads = collect(info, row_list, out_list, m3, per, width)
    heads = [heads[0]] + [send(heads[x], "prow", flip(procs, x)) for x in range(1, procs)]
    sent, *came1 = lax.optimization_barrier((sent, *came1))
    gathered = lax.all_gather(sent.reshape(-1, LANES), "prow", axis=0, tiled=True)
    gathered = gathered.reshape((procs,) + sent.shape)
    return info, src_owner, src_rank, heads, gathered, outgoing, spots, came1


def deliver(outgoing):
    procs = lax.axis_size("prow")
    return [outgoing[0]] + [
        send(outgoing[x], "prow", [(s, s ^ x) for s in range(2)]) for x in range(1, procs)
    ]


def exchange_any(m3, width, info, src, dest):
    per = width // LANES
    me = info[0]
    src_owner, src_local, _ = src
    dest_owner, dest_local, _ = dest
    rows = jnp.where((src_owner == me)[:, None, None], m3[src_local], 0.0)
    rows = lax.psum(rows.reshape(-1, LANES), "prow").reshape(rows.shape)
    displaced = []
    for source in range(2):
        top = jnp.where(me == source, m3[:width], 0.0)
        displaced.append(lax.psum(top.reshape(-1, LANES), "prow").reshape(top.shape))
    heads = [jnp.concatenate([rows[:, :per], top[:, :per]]) for top in displaced]
    spots = jnp.where(dest_owner == me, dest_local, -1)
    order = jnp.arange(2 * width, dtype=jnp.int32)
    first = jnp.concatenate([jnp.zeros((1,), jnp.int32), info[1:]])
    gathered = rows[None]
    return first, jnp.zeros_like(order), order, heads, gathered, displaced, spots


def factor(cap, fcap, m3, inv, info, first, came1, src, dest, out=None):
    rows, groups, _ = m3.shape
    width = inv.shape[1]
    chips = lax.axis_size("pcol") // 2
    per = width // LANES
    z = info[2]
    m2 = m3.reshape(rows * groups, LANES)
    m4 = m3.reshape(rows, groups // per, per, LANES)
    chunk = rows // CHUNKS
    hop = [(q, q + 2) for q in range(2 * chips - 2)]
    swap = [(q, q ^ 1) for q in range(2 * chips)]
    pieces = list(first) + list(panel(m4, CHAINS, CHUNKS - CHAINS, chunk))

    later = cap is not None
    if cap is None:
        cap, fcap = 2 * width, width
        moves = exchange_any(m3, width, info, src, dest) + (came1,)
    else:
        moves = exchange(cap, fcap, m3, width, info, came1, src, dest)
    seen, owner, rank, heads, gathered, displaced, spots, came1 = moves
    share = -(-(width + 2 * fcap) // (chunk * CHAINS))
    table = tables(seen, owner, rank, heads, cap, width, share * CHAINS * chunk)

    tiles = CHUNKS // CHAINS
    tile_of = jnp.where(spots < 0, tiles, spots // (CHAINS * chunk))
    place = jnp.arange(spots.shape[0], dtype=jnp.int32)
    before = (tile_of[None, :] < tile_of[:, None]) | (
        (tile_of[None, :] == tile_of[:, None]) & (place[None, :] < place[:, None])
    )
    at = jnp.sum(before.astype(jnp.int32), 1)
    order = jnp.sum(jnp.where(at[None, :] == place[:, None], place[None, :], 0), 1)
    starts = jnp.sum(
        (tile_of[None, :] < jnp.arange(tiles + 1, dtype=jnp.int32)[:, None]).astype(jnp.int32), 1
    )
    lists = (order, spots, starts)

    items = [piece.reshape(chunk * per, LANES) for piece in pieces]
    table = table.reshape(share * CHAINS, chunk * per, LANES)
    at = TABLE_AT * CHAINS
    items[at:at] = [table[n] for n in range(share * CHAINS)]
    length = len(items) // CHAINS
    position = [n if n < TABLE_AT else n + share for n in range(tiles)]
    own = [[] for _ in range(CHAINS)]
    sib = [[] for _ in range(CHAINS)]

    def held(t, count=1):
        bufs = []
        for n in range(t, t + count):
            for k in range(CHAINS):
                bufs += own[k][n : n + chips] + sib[k][n : n + chips]
        return bufs

    known = solved = moved = None
    done = 0

    def update(many):
        nonlocal out, done, moved
        if moved is None:
            moved = fetch(seen, deliver(displaced) if later else displaced)
        bufs = []
        for n in range(done, done + many):
            bufs += held(position[n])
        uhl, brow = solved
        out = bulk(info, lists, chips, bufs, known[:2], m2, uhl, moved, brow, out, done, many)
        done += many
        return out

    def work(t):
        nonlocal known, solved, moved, displaced
        if later and t == DELIVER_AT:
            return list(displaced)
        if known is None and t >= TABLE_AT + share + chips - 1:
            known = head(info, chips, held(TABLE_AT, share), inv)
            return [known[0]]
        if known is not None and solved is None and t >= TABLE_AT + share + chips - 1 + SOLVE_AFTER:
            solved = solve(seen, owner, rank, gathered, *known[2:], inv)
            return [solved[1]]
        return []

    if out is not None:
        out = out.reshape(m2.shape)
    for t in range(length + chips - 1):
        fresh = work(t)
        if fresh:
            tied = lax.optimization_barrier(tuple(own[k][-1] for k in range(CHAINS)) + tuple(fresh))
            ends = tied[:CHAINS]
            if later and t == DELIVER_AT:
                moved = fetch(seen, deliver(tied[CHAINS:]))
        else:
            ends = [own[k][-1] if t else None for k in range(CHAINS)]
        for k in range(CHAINS):
            cur = items[t * CHAINS + k] if t < length else None
            if t > 0:
                came = came1[k] if t == 1 else send(ends[k], "pcol", hop)
                cur = came if cur is None else jnp.where(z == 0, cur, came)
            own[k].append(cur)
        if t == length + chips - 2 and solved is not None and done < tiles and position[done] + chips <= t:
            ready = sum(position[n] + chips <= t for n in range(done, tiles))
            fresh = update(min(AT_ONCE, ready))
            tied = lax.optimization_barrier(tuple(own[k][-1] for k in range(CHAINS)) + (fresh,))
            for k in range(CHAINS):
                own[k][-1] = tied[k]
            out = tied[-1]
        for k in range(CHAINS):
            sib[k].append(send(own[k][-1], "pcol", swap))
    while solved is None:
        work(2 * (length + chips))
    while done < tiles:
        update(min(AT_LAST, tiles - done))
    return out.reshape(rows, groups, LANES)


def shards(matrix, pivots, inverse_blocks):
    row_blocks, _, width, blocks, _, _ = matrix.shape
    procs = lax.axis_size("prow")
    me = lax.axis_index("prow").astype(jnp.int32)
    mc = lax.axis_index("pcol").astype(jnp.int32)
    info = jnp.stack([me, mc, mc // 2, mc % 2, me])
    m3 = matrix.reshape(row_blocks * width, -1, LANES)
    m4 = matrix.reshape(row_blocks * width, blocks, -1, LANES)
    first = panel(m4, 0, CHAINS, row_blocks * width // CHUNKS)
    pivots, first = lax.optimization_barrier((pivots, first))
    flat = [piece.reshape(-1, LANES) for piece in first]
    hop = [(q, q + 2) for q in range(lax.axis_size("pcol") - 2)]
    came = tuple(lax.ppermute(piece, "pcol", hop) for piece in flat)
    so, sl, sr, do, dl, dr, src_most, dest_most = plan(pivots, width, procs, me)
    mean = 2 * width // procs
    cap = min(2 * width, (mean + mean // 4 + 7) // 8 * 8)
    fmean = width // procs
    fcap = min(width, (fmean + fmean // 2 + 7) // 8 * 8)
    again = (src_most > cap) | (dest_most > fcap)
    args = (m3, inverse_blocks, info, tuple(first), came, (so, sl, sr), (do, dl, dr))
    out = factor(cap, fcap, *args)

    out = lax.cond(
        again,
        lambda done, *rest: factor(None, None, *rest, done),
        lambda done, *rest: done,
        out,
        *args,
    )
    return out.reshape(matrix.shape)


def solution(mesh):
    return jax.shard_map(
        shards,
        mesh=mesh,
        in_specs=(P(None, "prow", None, None, "pcol", None), P(), P()),
        out_specs=P(None, "prow", None, None, "pcol", None),
        check_vma=False,
    )
```

```python
import functools

import jax
import jax.numpy as jnp
from jax import lax
from jax.experimental import pallas as pl
from jax.experimental.pallas import tpu as pltpu
from jax.sharding import PartitionSpec as P

LANES = 128
CHUNKS = 16
CHAINS = 2
TABLE_AT = 5
TILE = 256
DELIVER_AT = 6
AT_ONCE = 4
AT_LAST = 4
F32 = jnp.float32
BF16 = jnp.bfloat16
ANY = pl.BlockSpec(memory_space=pl.ANY)
VMEM = pl.BlockSpec(memory_space=pltpu.VMEM)
SMEM = pl.BlockSpec(memory_space=pltpu.SMEM)
PARAMS = pltpu.CompilerParams(vmem_limit_bytes=56 << 20)


def cost(nbytes):
    return pl.CostEstimate(flops=0, bytes_accessed=int(nbytes), transcendentals=0)


def split(x):
    high = x.astype(BF16)
    return high, (x - high.astype(F32)).astype(BF16)


def dot3(left, right):
    out = jnp.dot(left[0], right[0], preferred_element_type=F32)
    out += jnp.dot(left[0], right[1], preferred_element_type=F32)
    return out + jnp.dot(left[1], right[0], preferred_element_type=F32)


def upper(packed):
    row = lax.broadcasted_iota(jnp.int32, packed.shape, 0)
    col = lax.broadcasted_iota(jnp.int32, packed.shape, 1)
    return jnp.where(col >= row, packed, 0.0)


def unit_lower(packed):
    row = lax.broadcasted_iota(jnp.int32, packed.shape, 0)
    col = lax.broadcasted_iota(jnp.int32, packed.shape, 1)
    return jnp.where(col < row, packed, jnp.where(col == row, 1.0, 0.0))


def get_block(ref, start, count, groups, block, per):
    parts = [
        ref[pl.ds(start * groups + block * per + h, count, stride=groups), :] for h in range(per)
    ]
    return jnp.concatenate(parts, axis=1)


def put_block(ref, start, count, groups, block, per, value):
    for h in range(per):
        ref[pl.ds(start * groups + block * per + h, count, stride=groups), :] = value[
            :, h * LANES : (h + 1) * LANES
        ]


def panel_copies(info_ref, chips, bufs, c0_ref, c1_ref, sem, act):
    rows = bufs[0].shape[0]
    for h in range(chips):
        for core in range(2):

            @pl.when((info_ref[2] == h) & (info_ref[3] == core))
            def _():
                for n in range(len(bufs) // (2 * chips)):
                    own, sib = bufs[2 * n * chips + h], bufs[(2 * n + 1) * chips + h]
                    first, second = (own, sib) if core == 0 else (sib, own)
                    spot = pl.ds(n * rows, rows)
                    act(pltpu.make_async_copy(first, c0_ref.at[spot], sem.at[2 * n]))
                    act(pltpu.make_async_copy(second, c1_ref.at[spot], sem.at[2 * n + 1]))


def start(copy):
    copy.start()


def wait(copy):
    copy.wait()


def panel(m4, first, count, rows):
    shape = (rows,) + m4.shape[2:]

    def kernel(m_ref, *rest):
        outs, sem = rest[:count], rest[count]
        copies = [
            pltpu.make_async_copy(m_ref.at[pl.ds((first + k) * rows, rows), 0], outs[k], sem.at[k])
            for k in range(count)
        ]
        for copy in copies:
            copy.start()
        for copy in copies:
            copy.wait()

    return pl.pallas_call(
        kernel,
        in_specs=[ANY],
        out_specs=[VMEM] * count,
        out_shape=[jax.ShapeDtypeStruct(shape, F32)] * count,
        scratch_shapes=[pltpu.SemaphoreType.DMA((count,))],
        compiler_params=PARAMS,
        cost_estimate=cost(1 << 18),
        name="panel",
    )(m4)


def collect_kernel(procs, per, info_ref, list_ref, out_list_ref, m_ref, *rest):
    row_ref = rest[0]
    out_refs, head_refs = rest[1 : 1 + procs], rest[1 + procs : 1 + 2 * procs]
    top_ref, sem = rest[1 + 2 * procs :]
    cap = row_ref.shape[0]
    width = top_ref.shape[0]
    fcap = out_refs[0].shape[0]
    top = pltpu.make_async_copy(m_ref.at[pl.ds(0, width)], top_ref, sem.at[0])
    top.start()

    def fetch(k, carry):
        pltpu.make_async_copy(m_ref.at[list_ref[k]], row_ref.at[k], sem.at[1]).start()
        return carry

    lax.fori_loop(0, cap, fetch, 0)
    top.wait()

    @pl.when(info_ref[0] < 2)
    def _():
        for x in range(procs):

            def give(k, carry):
                row = top_ref[out_list_ref[x, k]]
                out_refs[x][k] = row
                head_refs[x][cap + k] = row[0:per]
                return carry

            lax.fori_loop(0, fcap, give, 0, unroll=4)

    pltpu.make_async_copy(row_ref, row_ref, sem.at[1]).wait()

    def keep(k, carry):
        row = row_ref[k, 0:per, :]
        for x in range(procs):
            head_refs[x][k] = row
        return carry

    lax.fori_loop(0, cap, keep, 0, unroll=4)


def collect(info, row_list, out_list, m3, per, width):
    cap = row_list.shape[0]
    procs, fcap = out_list.shape
    groups = m3.shape[1]
    out = jax.ShapeDtypeStruct((fcap, groups, LANES), F32)
    head = jax.ShapeDtypeStruct((cap + fcap, per, LANES), F32)
    outs = pl.pallas_call(
        functools.partial(collect_kernel, procs, per),
        in_specs=[SMEM, SMEM, SMEM, ANY],
        out_specs=[VMEM] * (1 + 2 * procs),
        out_shape=[jax.ShapeDtypeStruct((cap, groups, LANES), F32)] + [out] * procs + [head] * procs,
        scratch_shapes=[
            pltpu.VMEM((width, groups, LANES), F32),
            pltpu.SemaphoreType.DMA((2,)),
        ],
        compiler_params=PARAMS,
        cost_estimate=cost(1 << 18),
        name="collect",
    )(info, row_list, out_list, m3)
    return outs[0], outs[1 : 1 + procs], outs[1 + procs :]


def tables_kernel(procs, cap, width, info_ref, owner_ref, rank_ref, *rest):
    ins = rest[:procs]
    o_ref, buf_ref, sem = rest[procs:]
    fcap = buf_ref.shape[1] - cap
    copies = [
        pltpu.make_async_copy(ins[x], buf_ref.at[info_ref[0] ^ x], sem.at[x]) for x in range(procs)
    ]
    for copy in copies:
        copy.start()
    for copy in copies:
        copy.wait()
    base = jnp.where(info_ref[3] == 0, width, 0)

    def pivot(k, carry):
        o_ref[k] = buf_ref[owner_ref[base + k], rank_ref[base + k]]
        return carry

    lax.fori_loop(0, width, pivot, 0, unroll=4)
    for source in range(2):

        def other(k, carry):
            o_ref[width + source * fcap + k] = buf_ref[source, cap + k]
            return carry

        lax.fori_loop(0, fcap, other, 0, unroll=4)


def tables(info, owner, rank, heads, cap, width, rows):
    procs = len(heads)
    both, per, _ = heads[0].shape
    return pl.pallas_call(
        functools.partial(tables_kernel, procs, cap, width),
        in_specs=[SMEM, SMEM, SMEM] + [ANY] * procs,
        out_specs=VMEM,
        out_shape=jax.ShapeDtypeStruct((rows, per, LANES), F32),
        scratch_shapes=[
            pltpu.VMEM((procs, both, per, LANES), F32),
            pltpu.SemaphoreType.DMA((procs,)),
        ],
        compiler_params=PARAMS,
        cost_estimate=cost(1 << 18),
        name="tables",
    )(info, owner, rank, *heads)


def head_kernel(chips, info_ref, *rest):
    (*bufs, inv_ref, c0_ref, c1_ref, l01_ref, own_ref, w_ref, left_ref, sem) = rest
    width = inv_ref.shape[1]
    per = width // LANES
    me, mc = info_ref[0], info_ref[1]
    panel_copies(info_ref, chips, bufs, c0_ref, c1_ref, sem, start)
    panel_copies(info_ref, chips, bufs, c0_ref, c1_ref, sem, wait)
    z1c0 = get_block(c0_ref, 0, width, per, 0, per)
    g0c1 = get_block(c1_ref, 0, width, per, 0, per)
    one0, one1 = unit_lower(inv_ref[0]), unit_lower(inv_ref[1])
    up0, up1 = upper(inv_ref[0]), upper(inv_ref[1])
    low0, low1, v0, v1 = split(one0), split(one1), split(up0), split(up1)
    l01 = dot3(split(z1c0), v0)
    l01_ref[...] = l01
    u01 = dot3(low0, split(g0c1))
    back = dot3(low1, split(dot3(split(l01), low0)))
    cross = dot3(v0, split(u01))
    crosses = split(cross)
    parts = (
        split(dot3(v0, low0)),
        split(dot3(v1, split(back))),
        split(dot3(v1, low1)),
        crosses,
    )
    for n, part in enumerate(parts):
        for k in range(2):
            w_ref[(2 * n + k) * width : (2 * n + k + 1) * width] = part[k]
    mine = (split(jnp.where(me == 0, one0, -back)), split(jnp.where(me == 0, 0.0, one1)))
    for n, part in enumerate(mine):
        for k in range(2):
            own_ref[(2 * n + k) * width : (2 * n + k + 1) * width] = part[k]
    left_ref[:width] = jnp.where(mc == 0, -up0, dot3(crosses, v1))
    left_ref[width:] = jnp.where(mc == 0, 0.0, -up1)


def head(info, chips, bufs, inv):
    width = inv.shape[1]
    count = len(bufs) // (2 * chips)
    tab = jax.ShapeDtypeStruct((count * bufs[0].shape[0], LANES), F32)
    return pl.pallas_call(
        functools.partial(head_kernel, chips),
        in_specs=[SMEM] + [ANY] * len(bufs) + [VMEM],
        out_specs=[VMEM] * 6,
        out_shape=[
            tab,
            tab,
            jax.ShapeDtypeStruct((width, width), F32),
            jax.ShapeDtypeStruct((4 * width, width), BF16),
            jax.ShapeDtypeStruct((8 * width, width), BF16),
            jax.ShapeDtypeStruct((2 * width, width), F32),
        ],
        scratch_shapes=[pltpu.SemaphoreType.DMA((2 * count,))],
        compiler_params=PARAMS,
        cost_estimate=cost(1 << 20),
        name="head",
    )(info, *bufs, inv)


def solve_kernel(groups, info_ref, owner_ref, rank_ref, *rest):
    g_ref, l01_ref, own_ref, w_ref, left_ref, inv_ref, u_ref, brow_ref, s_ref = rest
    width = l01_ref.shape[0]
    per = width // LANES
    mc, me = info_ref[1], info_ref[4]
    def line_up(k, carry):
        spot = pl.ds(pl.multiple_of(k * groups, groups), groups)
        s_ref[spot, :] = g_ref[owner_ref[k], rank_ref[k]]
        return carry

    lax.fori_loop(0, 2 * width, line_up, 0, unroll=8)

    def pair(ref, n):
        return ref[2 * n * width : (2 * n + 1) * width], ref[(2 * n + 1) * width : (2 * n + 2) * width]

    def keep(block, value, first):
        for n, part in enumerate(split(value)):
            at = 2 * n * width + first
            u_ref[at : at + width, block * width : (block + 1) * width] = part

    for block in range(groups // per):
        g0 = split(get_block(s_ref, 0, width, groups, block, per))
        z1 = split(get_block(s_ref, width, width, groups, block, per))
        w1 = dot3(pair(w_ref, 2), z1) - dot3(pair(w_ref, 1), g0)
        w0 = dot3(pair(w_ref, 0), g0) - dot3(pair(w_ref, 3), split(w1))
        if block == 0:
            w0 = jnp.where(mc < 2, left_ref[:width], w0)
            w1 = jnp.where(mc < 2, left_ref[width:], w1)
        keep(block, w0, 0)
        keep(block, w1, width)

    for holder in range(2):

        @pl.when(me == holder)
        def _():
            def step(block, carry):
                u = dot3(pair(own_ref, 0), split(get_block(s_ref, 0, width, groups, block, per)))
                if holder == 1:
                    z1 = split(get_block(s_ref, width, width, groups, block, per))
                    u += dot3(pair(own_ref, 1), z1)
                put_block(brow_ref, 0, width, groups, block, per, u)
                return carry

            lax.fori_loop(0, groups // per, step, 0)

    @pl.when((mc == 0) & (me == 0))
    def _():
        put_block(brow_ref, 0, width, groups, 0, per, get_block(s_ref, 0, width, groups, 0, per))

    @pl.when((mc == 0) & (me == 1))
    def _():
        put_block(brow_ref, 0, width, groups, 0, per, l01_ref[...])

    @pl.when((mc == 1) & (me == 1))
    def _():
        g0 = split(get_block(s_ref, 0, width, groups, 0, per))
        z1 = get_block(s_ref, width, width, groups, 0, per)
        u0 = split(dot3(split(unit_lower(inv_ref[0])), g0))
        put_block(brow_ref, 0, width, groups, 0, per, z1 - dot3(split(l01_ref[...]), u0))


def solve(info, owner, rank, gathered, l01, own, w, left, inv):
    groups = gathered.shape[2]
    width = l01.shape[0]
    cols = groups * LANES
    return pl.pallas_call(
        functools.partial(solve_kernel, groups),
        in_specs=[SMEM, SMEM, SMEM] + [VMEM] * 6,
        out_specs=[VMEM, VMEM],
        out_shape=[
            jax.ShapeDtypeStruct((4 * width, cols), BF16),
            jax.ShapeDtypeStruct((width * groups, LANES), F32),
        ],
        scratch_shapes=[pltpu.VMEM((2 * width * groups, LANES), F32)],
        compiler_params=PARAMS,
        cost_estimate=cost(50 << 20),
        name="solve",
    )(info, owner, rank, gathered, l01, own, w, left, inv)


def make_bulk(chips, first, tiles, number, groups, width):
    def kernel(info_ref, order_ref, spot_ref, first_ref, *rest):
        bufs = rest[:number]
        m_ref, uhl_ref, f_ref, brow_ref, t0_ref, t1_ref = rest[number : number + 6]
        o_ref, u_ref, moved_ref, row_ref, c0_ref, c1_ref, left_ref = rest[-11:-4]
        c_sem, in_sem, out_sem, sem = rest[-4:]
        each = number // tiles
        count = left_ref.shape[0]
        per = width // LANES
        mc = info_ref[1]
        parts = row_ref.shape[1]
        half = count // parts
        u_copy = pltpu.make_async_copy(uhl_ref, u_ref, sem.at[0])
        f_copy = pltpu.make_async_copy(f_ref, moved_ref, sem.at[1])

        def span(n, part):
            return pl.ds(((first + n) * count + part * half) * groups, half * groups)

        def panels(n, act):
            slot = n % 2
            panel_copies(
                info_ref, chips, bufs[n * each : (n + 1) * each], c0_ref.at[slot], c1_ref.at[slot],
                c_sem.at[slot], act,
            )

        def rows_in(n, part):
            slot = n % 2
            return pltpu.make_async_copy(
                m_ref.at[span(n, part)], row_ref.at[slot, part], in_sem.at[slot, part]
            )

        def store(n, part):
            slot = n % 2
            return pltpu.make_async_copy(
                row_ref.at[slot, part], o_ref.at[span(n, part)], out_sem.at[slot, part]
            )

        panels(0, start)
        f_copy.start()
        u_copy.start()
        for part in range(parts):
            rows_in(0, part).start()
        for n in range(tiles):
            slot = n % 2
            c0, c1 = c0_ref.at[slot], c1_ref.at[slot]
            panels(n, wait)
            if n + 1 < tiles:
                panels(n + 1, start)

            def replace(e, carry):
                k = order_ref[e]
                here = pl.ds((spot_ref[k] - (first + n) * count) * per, per)
                there = pl.ds((width + k) * per, per)
                c0[here, :] = t0_ref[there, :]
                c1[here, :] = t1_ref[there, :]
                return carry

            lax.fori_loop(first_ref[first + n], first_ref[first + n + 1], replace, 0)
            for k, c in enumerate((c0, c1)):
                for part, value in enumerate(split(get_block(c, 0, count, per, 0, per))):
                    left_ref[:, (2 * part + k) * width : (2 * part + k + 1) * width] = value
            if n == 0:
                f_copy.wait()
                u_copy.wait()
            for part in range(parts):
                rows_in(n, part).wait()
                if n + 1 < tiles:
                    if n > 0:
                        store(n - 1, part).wait()
                    rows_in(n + 1, part).start()
                rows = row_ref.at[slot, part]
                base = (first + n) * count + part * half

                def replace_row(e, carry):
                    k = order_ref[e]
                    here = spot_ref[k] - base

                    @pl.when((here >= 0) & (here < half))
                    def _():
                        spot = pl.ds(pl.multiple_of(here * groups, groups), groups)
                        rows[spot, :] = moved_ref[k]

                    return carry

                lax.fori_loop(first_ref[first + n], first_ref[first + n + 1], replace_row, 0)
                high = left_ref[part * half : (part + 1) * half, : 2 * width]
                low = left_ref[part * half : (part + 1) * half, 2 * width :]
                for block in range(groups // per):
                    cols = slice(block * width, (block + 1) * width)
                    acc = dot3((high, low), (u_ref[: 2 * width, cols], u_ref[2 * width :, cols]))
                    old = get_block(rows, 0, half, groups, block, per)
                    if block == 0:
                        old = jnp.where(mc < 2, 0.0, old)
                    put_block(rows, 0, half, groups, block, per, old - acc)
                if base < width:

                    @pl.when(info_ref[0] < 2)
                    def _():
                        many = min(half, width - base) * groups
                        copy = pltpu.make_async_copy(
                            brow_ref.at[pl.ds(base * groups, many)],
                            rows.at[pl.ds(0, many)],
                            sem.at[0],
                        )
                        copy.start()
                        copy.wait()

                store(n, part).start()
        for n in range(max(0, tiles - 2), tiles):
            for part in range(parts):
                store(n, part).wait()

    return kernel


def bulk(info, lists, chips, bufs, tabs, m2, uhl, moved, brow, out, first, tiles):
    groups = moved.shape[1]
    width = uhl.shape[0] // 4
    per = width // LANES
    pieces = len(bufs) // (2 * chips * tiles)
    count = pieces * bufs[0].shape[0] // per
    parts = max(1, count // TILE)
    in_specs = [SMEM] * 4 + [ANY] * (len(bufs) + 4) + [VMEM] * 2
    args = [info, *lists, *bufs, m2, uhl, moved, brow, *tabs]
    aliases = {}
    if out is not None:
        in_specs.append(ANY)
        aliases = {len(args): 0}
        args.append(out)
    panels = pltpu.VMEM((2, count * per, LANES), F32)
    return pl.pallas_call(
        make_bulk(chips, first, tiles, len(bufs), groups, width),
        in_specs=in_specs,
        out_specs=ANY,
        out_shape=jax.ShapeDtypeStruct(m2.shape, F32),
        scratch_shapes=[
            pltpu.VMEM(uhl.shape, BF16),
            pltpu.VMEM(moved.shape, F32),
            pltpu.VMEM((2, parts, count // parts * groups, LANES), F32),
            panels,
            panels,
            pltpu.VMEM((count, 4 * width), BF16),
            pltpu.SemaphoreType.DMA((2, 2 * pieces)),
            pltpu.SemaphoreType.DMA((2, parts)),
            pltpu.SemaphoreType.DMA((2, parts)),
            pltpu.SemaphoreType.DMA((2,)),
        ],
        input_output_aliases=aliases,
        compiler_params=PARAMS,
        cost_estimate=cost(tiles * (20 << 20)),
        name="bulk",
    )(*args)


def fetch_kernel(procs, info_ref, *rest):
    ins = rest[:procs]
    o_ref, sem = rest[procs:]
    rows = o_ref.shape[0] // 2
    for act in (start, wait):
        for source in range(2):
            spot = pl.ds(source * rows, rows)
            for x in range(procs):

                @pl.when((info_ref[0] ^ source) == x)
                def _():
                    act(pltpu.make_async_copy(ins[x], o_ref.at[spot], sem.at[source]))


def fetch(info, displaced):
    rows, groups, _ = displaced[0].shape
    return pl.pallas_call(
        functools.partial(fetch_kernel, len(displaced)),
        in_specs=[SMEM] + [ANY] * len(displaced),
        out_specs=VMEM,
        out_shape=jax.ShapeDtypeStruct((2 * rows, groups, LANES), F32),
        scratch_shapes=[pltpu.SemaphoreType.DMA((2,))],
        compiler_params=PARAMS,
        cost_estimate=cost(1 << 20),
        name="fetch",
    )(info, *displaced)


def plan(pivots, width, procs, me):
    p0, p1 = pivots[0], pivots[1]
    count = jnp.arange(width, dtype=jnp.int32)
    hit = p0[:, None] == p1[None, :]
    back = p0[:, None] == width + count[None, :]
    src1 = jnp.where(hit.any(0), jnp.sum(jnp.where(hit, count[:, None], 0), 0), p1)
    dest0 = jnp.where(
        back.any(1),
        jnp.sum(jnp.where(back, p1[None, :], 0), 1),
        jnp.where(hit.any(1), -1, p0),
    )
    dest1 = jnp.where(back.any(0), -1, p1)
    src = jnp.concatenate([p0, src1])
    dest = jnp.concatenate([dest0, dest1])
    src_owner = src // width % procs
    src_local = src // width // procs * width + src % width
    dest_owner = jnp.where(dest >= 0, dest // width % procs, -1)
    dest_local = dest // width // procs * width + dest % width
    order = jnp.arange(2 * width, dtype=jnp.int32)
    earlier = order[None, :] < order[:, None]
    same_half = (order[None, :] // width) == (order[:, None] // width)
    src_rank = jnp.sum(
        (earlier & (src_owner[None, :] == src_owner[:, None])).astype(jnp.int32), 1
    )
    dest_rank = jnp.sum(
        (earlier & same_half & (dest_owner[None, :] == dest_owner[:, None])).astype(jnp.int32), 1
    )
    src_most = jnp.max(src_rank) + 1
    dest_most = jnp.max(jnp.where(dest >= 0, dest_rank, -1)) + 1
    return src_owner, src_local, src_rank, dest_owner, dest_local, dest_rank, src_most, dest_most


def flip(procs, x):
    return [(s, s ^ x) for s in range(procs)]


def send(value, axis, pairs):
    flat = value.reshape(-1, LANES)
    return lax.ppermute(flat, axis, pairs).reshape(value.shape)


def exchange(cap, fcap, m3, width, info, came1, src, dest):
    per = width // LANES
    procs = lax.axis_size("prow")
    me = info[0]
    src_owner, src_local, src_rank = src
    dest_owner, dest_local, dest_rank = dest

    src_rank = jnp.minimum(src_rank, cap - 1)
    slots = jnp.arange(cap, dtype=jnp.int32)
    mine = (src_owner == me)[None, :] & (src_rank[None, :] == slots[:, None])
    row_list = jnp.max(jnp.where(mine, src_local[None, :], 0), 1)

    fslots = jnp.arange(fcap, dtype=jnp.int32)
    owner2 = dest_owner.reshape(2, width)
    rank2 = dest_rank.reshape(2, width)
    local2 = dest_local.reshape(2, width)
    to = me ^ jnp.arange(procs, dtype=jnp.int32)
    out_owner = jnp.where(me == 0, owner2[0], owner2[1])
    out_rank = jnp.where(me == 0, rank2[0], rank2[1])
    chosen = (out_owner[None, None, :] == to[:, None, None]) & (
        out_rank[None, None, :] == fslots[None, :, None]
    )
    out_list = jnp.sum(jnp.where(chosen, jnp.arange(width, dtype=jnp.int32), 0), 2)
    landing = (owner2[:, None, :] == me) & (rank2[:, None, :] == fslots[None, :, None])
    spots = (jnp.sum(jnp.where(landing, local2[:, None, :] + 1, 0), 2) - 1).reshape(2 * fcap)

    row_list, *came1 = lax.optimization_barrier((row_list, *came1))
    sent, outgoing, heads = collect(info, row_list, out_list, m3, per, width)
    heads = [heads[0]] + [send(heads[x], "prow", flip(procs, x)) for x in range(1, procs)]
    gathered = lax.all_gather(sent.reshape(-1, LANES), "prow", axis=0, tiled=True)
    gathered = gathered.reshape((procs,) + sent.shape)
    return info, src_owner, src_rank, heads, gathered, outgoing, spots, came1


def deliver(outgoing):
    procs = lax.axis_size("prow")
    return [outgoing[0]] + [
        send(outgoing[x], "prow", [(s, s ^ x) for s in range(2)]) for x in range(1, procs)
    ]


def exchange_any(m3, width, info, src, dest):
    per = width // LANES
    me = info[0]
    src_owner, src_local, _ = src
    dest_owner, dest_local, _ = dest
    rows = jnp.where((src_owner == me)[:, None, None], m3[src_local], 0.0)
    rows = lax.psum(rows.reshape(-1, LANES), "prow").reshape(rows.shape)
    displaced = []
    for source in range(2):
        top = jnp.where(me == source, m3[:width], 0.0)
        displaced.append(lax.psum(top.reshape(-1, LANES), "prow").reshape(top.shape))
    heads = [jnp.concatenate([rows[:, :per], top[:, :per]]) for top in displaced]
    spots = jnp.where(dest_owner == me, dest_local, -1)
    order = jnp.arange(2 * width, dtype=jnp.int32)
    first = jnp.concatenate([jnp.zeros((1,), jnp.int32), info[1:]])
    gathered = rows[None]
    return first, jnp.zeros_like(order), order, heads, gathered, displaced, spots


def factor(cap, fcap, m3, inv, info, first, came1, src, dest, out=None):
    rows, groups, _ = m3.shape
    width = inv.shape[1]
    chips = lax.axis_size("pcol") // 2
    per = width // LANES
    z = info[2]
    m2 = m3.reshape(rows * groups, LANES)
    m4 = m3.reshape(rows, groups // per, per, LANES)
    chunk = rows // CHUNKS
    hop = [(q, q + 2) for q in range(2 * chips - 2)]
    swap = [(q, q ^ 1) for q in range(2 * chips)]
    pieces = list(first) + list(panel(m4, 2 * CHAINS, CHUNKS - 2 * CHAINS, chunk))

    later = cap is not None
    if cap is None:
        cap, fcap = 2 * width, width
        moves = exchange_any(m3, width, info, src, dest) + (came1,)
    else:
        moves = exchange(cap, fcap, m3, width, info, came1, src, dest)
    seen, owner, rank, heads, gathered, displaced, spots, came1 = moves
    share = -(-(width + 2 * fcap) // (chunk * CHAINS))
    table = tables(seen, owner, rank, heads, cap, width, share * CHAINS * chunk)

    tiles = CHUNKS // CHAINS
    tile_of = jnp.where(spots < 0, tiles, spots // (CHAINS * chunk))
    place = jnp.arange(spots.shape[0], dtype=jnp.int32)
    before = (tile_of[None, :] < tile_of[:, None]) | (
        (tile_of[None, :] == tile_of[:, None]) & (place[None, :] < place[:, None])
    )
    at = jnp.sum(before.astype(jnp.int32), 1)
    order = jnp.sum(jnp.where(at[None, :] == place[:, None], place[None, :], 0), 1)
    starts = jnp.sum(
        (tile_of[None, :] < jnp.arange(tiles + 1, dtype=jnp.int32)[:, None]).astype(jnp.int32), 1
    )
    lists = (order, spots, starts)

    items = [piece.reshape(chunk * per, LANES) for piece in pieces]
    table = table.reshape(share * CHAINS, chunk * per, LANES)
    at = TABLE_AT * CHAINS
    items[at:at] = [table[n] for n in range(share * CHAINS)]
    length = len(items) // CHAINS
    position = [n if n < TABLE_AT else n + share for n in range(tiles)]
    own = [[] for _ in range(CHAINS)]
    sib = [[] for _ in range(CHAINS)]

    def held(t, count=1):
        bufs = []
        for n in range(t, t + count):
            for k in range(CHAINS):
                bufs += own[k][n : n + chips] + sib[k][n : n + chips]
        return bufs

    known = solved = moved = None
    done = 0

    def update(many):
        nonlocal out, done, moved
        if moved is None:
            moved = fetch(seen, deliver(displaced) if later else displaced)
        bufs = []
        for n in range(done, done + many):
            bufs += held(position[n])
        uhl, brow = solved
        out = bulk(info, lists, chips, bufs, known[:2], m2, uhl, moved, brow, out, done, many)
        done += many
        return out

    def work(t):
        nonlocal known
        if later and t == DELIVER_AT:
            return list(displaced)
        if known is None and t >= TABLE_AT + share + chips - 1:
            known = head(info, chips, held(TABLE_AT, share), inv)
            return [known[0]]
        return []

    if out is not None:
        out = out.reshape(m2.shape)
    for t in range(length + chips - 1):
        fresh = work(t)
        if fresh:
            tied = lax.optimization_barrier(tuple(own[k][-1] for k in range(CHAINS)) + tuple(fresh))
            ends = tied[:CHAINS]
            if later and t == DELIVER_AT:
                moved = fetch(seen, deliver(tied[CHAINS:]))
        else:
            ends = [own[k][-1] if t else None for k in range(CHAINS)]
        for k in range(CHAINS):
            cur = items[t * CHAINS + k] if t < length else None
            if t > 0:
                if t == 1:
                    cur = came1[k]
                else:
                    came = send(ends[k], "pcol", hop)
                    cur = came if cur is None else jnp.where(z == 0, cur, came)
            own[k].append(cur)
        if t == length + chips - 2 and known is not None:
            solved = solve(seen, owner, rank, gathered, *known[2:], inv)
            ready = sum(position[n] + chips <= t for n in range(done, tiles))
            fresh = update(min(AT_ONCE, ready))
            tied = lax.optimization_barrier(tuple(own[k][-1] for k in range(CHAINS)) + (fresh,))
            for k in range(CHAINS):
                own[k][-1] = tied[k]
            out = tied[-1]
        for k in range(CHAINS):
            sib[k].append(send(own[k][-1], "pcol", swap))
    if known is None:
        known = head(info, chips, held(TABLE_AT, share), inv)
    if solved is None:
        solved = solve(seen, owner, rank, gathered, *known[2:], inv)
    while done < tiles:
        update(min(AT_LAST, tiles - done))
    return out.reshape(rows, groups, LANES)


def shards(matrix, pivots, inverse_blocks):
    row_blocks, _, width, blocks, _, _ = matrix.shape
    procs = lax.axis_size("prow")
    me = lax.axis_index("prow").astype(jnp.int32)
    mc = lax.axis_index("pcol").astype(jnp.int32)
    info = jnp.stack([me, mc, mc // 2, mc % 2, me])
    m3 = matrix.reshape(row_blocks * width, -1, LANES)
    m4 = matrix.reshape(row_blocks * width, blocks, -1, LANES)
    first = panel(m4, 0, 2 * CHAINS, row_blocks * width // CHUNKS)
    pivots, first = lax.optimization_barrier((pivots, first))
    flat = [piece.reshape(-1, LANES) for piece in first]
    hop = [(q, q + 2) for q in range(lax.axis_size("pcol") - 2)]
    came = []
    for k in range(CHAINS):
        arrived = lax.ppermute(flat[k], "pcol", hop)
        came.append(jnp.where(mc < 2, flat[CHAINS + k], arrived))
    came = tuple(came)
    so, sl, sr, do, dl, dr, src_most, dest_most = plan(pivots, width, procs, me)
    mean = 2 * width // procs
    cap = min(2 * width, (mean + mean // 4 + 7) // 8 * 8)
    fmean = width // procs
    fcap = min(width, (fmean + fmean // 2 + 7) // 8 * 8)
    again = (src_most > cap) | (dest_most > fcap)
    args = (m3, inverse_blocks, info, tuple(first), came, (so, sl, sr), (do, dl, dr))
    out = factor(cap, fcap, *args)

    out = lax.cond(
        again,
        lambda done, *rest: factor(None, None, *rest, done),
        lambda done, *rest: done,
        out,
        *args,
    )
    return out.reshape(matrix.shape)


def solution(mesh):
    return jax.shard_map(
        shards,
        mesh=mesh,
        in_specs=(P(None, "prow", None, None, "pcol", None), P(), P()),
        out_specs=P(None, "prow", None, None, "pcol", None),
        check_vma=False,
    )
```
